32 devices in a mesh: groups: 2 (over y), section: 4 (over x, core), tp: 4 (over z).
Axes of the slice: x: 2, y: 2, z: 4, core: 2. Of those that a mesh axis runs over, the one named last changes fastest.
Arguments:
- step_token_states: bfloat16 [4, 64, 8192], P(None, ('groups', 'section')), parts along dimension 1, may hold values from -6 to 6
- input_norm_gain: bfloat16 [8192], replicated, may hold values from 0.099609375 to 1.8984375
- wq: bfloat16 [8192, 8192], P(None, 'tp'), may hold values from -0.0625 to 0.0625
- wkv: bfloat16 [8192, 2048], P(None, 'tp'), may hold values from -0.25 to 0.25
- wo: bfloat16 [8192, 8192], P('tp'), may hold values from -0.0625 to 0.0625
- adapter_down: bfloat16 [32, 8192, 128], P(('groups', 'section'), 'tp'), parts along dimension 0, may hold values from -0.0625 to 0.0625
- adapter_up: bfloat16 [32, 128, 8192], P(('groups', 'section'), None, 'tp'), parts along dimension 0, may hold values from -0.375 to 0.375
- prompt_cache_pool: bfloat16 [64, 2, 2048, 1024], P('groups', None, 'section', 'tp'), parts along dimension 0, may hold values from -1100 to 1100
- prompt_slot: int32 [64], P('groups'), parts along dimension 0, may hold values from 0 to 31, each once
- prompt_cache_length: int32 [64], P('groups'), parts along dimension 0, may hold values from 512 to 2044, as said below
- slot_adapter: int32 [64], P('groups'), parts along dimension 0, may hold values from 0 to 15
- adapter_ranks: int32 [32], P('groups'), parts along dimension 0, may hold values from 8 to 128, as said below
Outputs:
- block_output: bfloat16 [4, 64, 8192], P(None, ('groups', 'section')), parts along dimension 1
The draws below stay inside these ranges and needn't reach their ends.
There are 2 independent parts, one for each index of `groups`. The reference program is written for one: setup_inputs(seed, part) draws one part's arguments, and reference() takes and returns one part's arrays. A program takes and returns all parts, laid end to end along the dimension named above; an argument that names none is the same for every part. Nothing has to cross between parts.
Inputs may be any that keep to these rules, and one draw needn't show every extreme that they name: `prompt_cache_length`: some prompt has 2044 cached tokens. `adapter_ranks`: some adapter has rank 128 and some rank 8.
All inputs are finite; a program needn't handle non-finite values.
Results may differ from the reference program's by a relative error of at most 0.013.
The reference program's roundings to bfloat16 on the way count: a program that leaves them out, or rounds other values in their place, can miss the bound.
Values may be sent and summed in bfloat16 or wider, within the bound.
No kernel may reach another device: no remote copies, remote signals or barrier semaphores. Data moves between devices by JAX's collectives and lax.ppermute only.
A program may use at most 320 MiB of HBM per device.

```python
import math
import jax
import jax.numpy as jnp
from jax import lax

MODEL_DIM = 8192
QUERY_HEADS = 64
KVH = 8
HEAD_DIM = 128
PADDED_RANK = 128
STEPS = 4
L = 2048
REPLICA_ADAPTERS = 16
QUERY_DIM = 8192
REQS = 32


def draw_prompt_cache_pool(key, part):
    key = jax.random.fold_in(key, 11)
    shape = (REQS, 2, L, KVH * HEAD_DIM)
    scales = jnp.array([2.0, 1.0], jnp.float32)[None, :, None, None]
    draws_f32 = jnp.clip(jax.random.normal(jax.random.fold_in(key, 1), shape, jnp.float32), -6.0, 6.0) * scales
    return draws_f32.astype(jnp.bfloat16)


def draw_prompt_cache_length(key, part):
    key = jax.random.fold_in(key, 5)
    lengths = jax.random.randint(jax.random.fold_in(key, 1), (REQS,), L // 4, L - STEPS + 1)
    longest = jax.random.randint(jax.random.fold_in(key, 2), (), 0, REQS)
    return jnp.where(jnp.arange(REQS) == longest, L - STEPS, lengths).astype(jnp.int32)


def draw_adapter_ranks(key, part):
    key = jax.random.fold_in(key, 7)
    rank_entries = jax.random.randint(jax.random.fold_in(key, 1), (REPLICA_ADAPTERS,), 8, PADDED_RANK + 1)
    widest = jax.random.randint(jax.random.fold_in(key, 2), (), 0, REPLICA_ADAPTERS)
    narrow = (widest + jax.random.randint(jax.random.fold_in(key, 3), (), 1, REPLICA_ADAPTERS)) % REPLICA_ADAPTERS
    indices = jnp.arange(REPLICA_ADAPTERS)
    rank_entries = jnp.where(indices == widest, PADDED_RANK, jnp.where(indices == narrow, 8, rank_entries))
    return rank_entries.astype(jnp.int32)


def with_ends(values, own_key, low, high):
    extent = values.shape
    spot = [jax.random.randint(jax.random.fold_in(own_key, axis), (), 0, extent[axis]) for axis in range(len(extent))]
    values = values.at[tuple(spot)].set(low)
    longest = extent.index(max(extent))
    spot[longest] = (spot[longest] + 1) % extent[longest]
    return values.at[tuple(spot)].set(high)


def steps_of(key, shape, cuts, least, largest):
    level, own = 1.0, jax.random.fold_in(key, 6)
    for dim, blocks in cuts:
        draws = jnp.exp(jax.random.uniform(jax.random.fold_in(own, dim), (blocks,), jnp.float32, least / len(cuts), largest / len(cuts)))
        level = level * jnp.repeat(draws, shape[dim] // blocks).reshape([-1 if axis == dim else 1 for axis in range(len(shape))])
    return level


def centred(rng, shape, width, most, cuts=(), held_as=jnp.bfloat16):
    level = steps_of(rng, shape, cuts, -0.22, 0.18) if cuts else 1.0
    values = jax.random.normal(rng, shape, jnp.float32) * width * level
    return jnp.minimum(jnp.maximum(values, -most), most).astype(held_as)


def setup_inputs(seed: int = 0, part: int = 0) -> dict:
    key_list = jax.random.split(jax.random.key(seed), 13)
    own_keys = jax.random.split(jax.random.fold_in(key_list[12], part), 13)
    step_token_states = centred(own_keys[0], (STEPS, REQS, MODEL_DIM), 1.0, 6.0, ((1, 4),))
    input_norm_gain = jnp.clip(1.0 + 0.18 * jax.random.normal(key_list[1], (MODEL_DIM,), jnp.float32), 0.099609375, 1.8984375).astype(jnp.bfloat16)
    wq = centred(key_list[2], (MODEL_DIM, QUERY_DIM), MODEL_DIM ** -0.5, 0.0625, ((1, 4),))
    wkv = centred(key_list[3], (MODEL_DIM, 2 * KVH * HEAD_DIM), (MODEL_DIM // 16) ** -0.5, 0.25, ((1, 4),))
    wo = centred(key_list[4], (QUERY_DIM, MODEL_DIM), QUERY_DIM ** -0.5, 0.0625, ((0, 4),))
    adapter_down = centred(own_keys[5], (REPLICA_ADAPTERS, MODEL_DIM, PADDED_RANK), MODEL_DIM ** -0.5, 0.0625, ((0, 4), (1, 4)))
    adapter_up = centred(own_keys[6], (REPLICA_ADAPTERS, PADDED_RANK, QUERY_DIM), 256 ** -0.5, 0.375, ((0, 4), (2, 4)))
    prompt_cache_pool = draw_prompt_cache_pool(jax.random.fold_in(jax.random.fold_in(key_list[12], part), 71), part)
    prompt_slot = jax.random.permutation(own_keys[8], REQS).astype(jnp.int32)
    prompt_cache_length = draw_prompt_cache_length(jax.random.fold_in(jax.random.fold_in(key_list[12], part), 71), part)
    slot_adapter = with_ends(jax.random.randint(own_keys[10], (REQS,), 0, REPLICA_ADAPTERS), jax.random.fold_in(own_keys[10], 1), 0, REPLICA_ADAPTERS - 1).astype(jnp.int32)
    adapter_ranks = draw_adapter_ranks(jax.random.fold_in(jax.random.fold_in(key_list[12], part), 71), part)
    return {"step_token_states": step_token_states, "input_norm_gain": input_norm_gain, "wq": wq, "wkv": wkv, "wo": wo, "adapter_down": adapter_down, "adapter_up": adapter_up, "prompt_cache_pool": prompt_cache_pool, "prompt_slot": prompt_slot, "prompt_cache_length": prompt_cache_length, "slot_adapter": slot_adapter, "adapter_ranks": adapter_ranks}


EPSILON = 1e-05
ROPE_BASE = 500000.0
ADAPTER_ALPHA = 16.0
NEGATIVE = -1e+30

def apply_rotary(vectors, positions):
    half_dim = vectors.shape[-1] // 2
    exponents = jnp.arange(half_dim, dtype=jnp.float32) * (2.0 / vectors.shape[-1])
    frequency = ROPE_BASE ** (-exponents)
    angles = positions.astype(jnp.float32)[:, None] * frequency[None, :]
    cosine = jnp.cos(angles)[:, None, :]
    sine = jnp.sin(angles)[:, None, :]
    first_half = vectors[..., :half_dim]
    second_half = vectors[..., half_dim:]
    return jnp.concatenate([first_half * cosine - second_half * sine, second_half * cosine + first_half * sine], axis=-1)

def reference(step_token_states, input_norm_gain, wq, wkv, wo, adapter_down, adapter_up, prompt_cache_pool, prompt_slot, prompt_cache_length, slot_adapter, adapter_ranks):
    request_list = prompt_slot.shape[0]
    owners = jnp.zeros((request_list,), jnp.int32).at[prompt_slot].set(jnp.arange(request_list, dtype=jnp.int32))
    lengths = prompt_cache_length[owners]
    ordered = prompt_cache_pool[owners]
    cache_keys = ordered[:, 0].reshape(request_list, L, KVH, HEAD_DIM).astype(jnp.float32)
    cache_values = ordered[:, 1].reshape(request_list, L, KVH, HEAD_DIM).astype(jnp.float32)
    rank_entries = adapter_ranks[slot_adapter]
    valid_rank_mask = jnp.arange(PADDED_RANK)[None, :] < rank_entries[:, None]
    adapter_scale = ADAPTER_ALPHA / rank_entries.astype(jnp.float32)
    chosen_down = adapter_down[slot_adapter].astype(jnp.float32)
    chosen_up = adapter_up[slot_adapter].astype(jnp.float32)
    is_valid = (jnp.arange(L)[None, :] < lengths[:, None])[:, None, None, :]
    root_dim = math.sqrt(HEAD_DIM)
    kv_cols = KVH * HEAD_DIM
    fresh_keys = []
    fresh_values = []
    results = []
    for step_index in range(STEPS):
        values_f32 = step_token_states[step_index].astype(jnp.float32)
        inverse = lax.rsqrt(lax.optimization_barrier(jnp.mean(values_f32 * values_f32, axis=-1, keepdims=True)) + EPSILON)
        normed = lax.optimization_barrier((values_f32 * inverse * input_norm_gain.astype(jnp.float32)).astype(jnp.bfloat16))
        plain_query = jnp.dot(normed, wq, preferred_element_type=jnp.float32)
        rank_products_sum = jnp.einsum('rd,rdk->rk', normed.astype(jnp.float32), chosen_down)
        reduced_rank_state = lax.optimization_barrier(jnp.where(valid_rank_mask, rank_products_sum * adapter_scale[:, None], 0.0).astype(jnp.bfloat16))
        adapter_change = jnp.einsum('vf,vfs->vs', reduced_rank_state.astype(jnp.float32), chosen_up)
        current_position = lengths + step_index
        query_rows = apply_rotary((plain_query + adapter_change).reshape(request_list, QUERY_HEADS, HEAD_DIM), current_position).astype(jnp.bfloat16)
        kv_new = jnp.dot(normed, wkv, preferred_element_type=jnp.float32)
        new_key = apply_rotary(kv_new[:, :kv_cols].reshape(request_list, KVH, HEAD_DIM), current_position).astype(jnp.bfloat16)
        new_value = kv_new[:, kv_cols:].reshape(request_list, KVH, HEAD_DIM).astype(jnp.bfloat16)
        fresh_keys.append(new_key)
        fresh_values.append(new_value)
        stacked_keys = jnp.stack(fresh_keys).astype(jnp.float32)
        stacked_values = jnp.stack(fresh_values).astype(jnp.float32)
        grouped = query_rows.astype(jnp.float32).reshape(request_list, KVH, QUERY_HEADS // KVH, HEAD_DIM)
        old_scores = jnp.einsum('rkgd,rtkd->rkgt', grouped, cache_keys) / root_dim
        new_scores = jnp.einsum('rkgd,srkd->rkgs', grouped, stacked_keys) / root_dim
        row_top = jnp.maximum(lax.optimization_barrier(jnp.max(jnp.where(is_valid, old_scores, NEGATIVE), axis=-1)), lax.optimization_barrier(jnp.max(new_scores, axis=-1)))
        old_weights = jnp.where(is_valid, jnp.exp(old_scores - row_top[..., None]), 0.0)
        new_weights = jnp.exp(new_scores - row_top[..., None])
        row_total = lax.optimization_barrier(jnp.sum(old_weights, axis=-1)) + lax.optimization_barrier(jnp.sum(new_weights, axis=-1))
        old_round = lax.optimization_barrier(old_weights.astype(jnp.bfloat16)).astype(jnp.float32)
        new_round = lax.optimization_barrier(new_weights.astype(jnp.bfloat16)).astype(jnp.float32)
        weighted = jnp.einsum('rkgt,rtkd->rkgd', old_round, cache_values) + jnp.einsum('rkgs,srkd->rkgd', new_round, stacked_values)
        attended = (weighted / row_total[..., None]).reshape(request_list, QUERY_HEADS * HEAD_DIM).astype(jnp.bfloat16)
        results.append(jnp.dot(attended, wo, preferred_element_type=jnp.float32).astype(jnp.bfloat16))
    return jnp.stack(results)
```

```python
import functools
import math

import jax
import jax.numpy as jnp
from jax import lax
from jax.experimental import pallas as pl
from jax.experimental.pallas import tpu as pltpu
from jax.sharding import PartitionSpec as P

QUERY_HEADS = 64
KVH = 8
HEAD_DIM = 128
PER_KV = QUERY_HEADS // KVH

EPSILON = 1e-05
ROPE_BASE = 500000.0
ADAPTER_ALPHA = 16.0
NEGATIVE = -1e30
STAT_ROWS = 8
FRESH_ROWS = 16
F32 = jnp.float32
BF16 = jnp.bfloat16
VMEM = pl.BlockSpec(memory_space=pltpu.VMEM)
SMEM = pl.BlockSpec(memory_space=pltpu.SMEM)
ANYWHERE = pl.BlockSpec(memory_space=pl.ANY)


def params(mebibytes):
    return pltpu.CompilerParams(vmem_limit_bytes=mebibytes * 1024 * 1024)


def swap(value, axis, bit):
    size = lax.axis_size(axis)
    pairs = [(i, i ^ bit) for i in range(size)]
    return jax.tree.map(lambda a: lax.ppermute(a, axis, pairs), value)


def normalize(hidden_rows, input_norm_gain):
    values_f32 = hidden_rows.astype(F32)
    inverse = lax.rsqrt(jnp.mean(values_f32 * values_f32, axis=-1, keepdims=True) + EPSILON)
    return (values_f32 * inverse * input_norm_gain.astype(F32)).astype(BF16)


def rotary_tables(positions):
    half_dim = HEAD_DIM // 2
    exponents = jnp.arange(half_dim, dtype=F32) * (2.0 / HEAD_DIM)
    frequency = ROPE_BASE ** (-exponents)
    angles = positions.astype(F32)[:, None] * frequency[None, :]
    cosine, sine = jnp.cos(angles), jnp.sin(angles)
    return jnp.concatenate([cosine, cosine], -1), jnp.concatenate([-sine, sine], -1)


def down_kernel(own, across, beside, beside_across, pick, down, out):
    rows = own.shape[0]
    for position, ref in enumerate((own, beside, across, beside_across)):
        block = slice(position * rows, (position + 1) * rows)
        total = jnp.zeros((rows, down.shape[2]), F32)
        for a in range(down.shape[0]):
            product = jnp.dot(ref[...], down[a], preferred_element_type=F32)
            total = jnp.where(pick[block, a : a + 1] > 0, product, total)
        out[block, :] = total


def query_kernel(parts, scale, pick, up, own, across, beside, beside_across, cosine, sine, out):
    rank_sum = parts[0]
    for i in range(1, parts.shape[0]):
        rank_sum = rank_sum + parts[i]
    low_rank = jnp.where(scale[...] > 0, rank_sum * scale[...], 0.0)
    adapters = up.shape[0]
    wide = jnp.concatenate(
        [jnp.where(pick[:, a : a + 1] > 0, low_rank, 0.0) for a in range(adapters)], axis=1
    ).astype(BF16)
    up_rows = up.reshape(adapters * up.shape[1], up.shape[2])
    rows = own.shape[0]
    here = jnp.sum(pick[...], axis=1, keepdims=True) > 0
    for head in range(up.shape[2] // HEAD_DIM):
        cols = slice(head * HEAD_DIM, (head + 1) * HEAD_DIM)
        change = jnp.dot(wide, up_rows[:, cols], preferred_element_type=F32)
        plain = jnp.concatenate([ref[:, cols] for ref in (own, beside, across, beside_across)], 0)
        query = plain + change
        turned = query * cosine[...] + pltpu.roll(query, HEAD_DIM // 2, 1) * sine[...]
        out[:, cols] = jnp.where(here, turned, 0.0).astype(BF16)


def attend_kernel(fresh, steps, slots, kvl, owners, limits, qa, qb, nk, nv, cache, out, kv, qf, qs, sems):
    count = 2 * slots
    heads = qa.shape[1] // HEAD_DIM
    per_kv = heads // kvl
    rows = heads * steps
    tokens = cache.shape[2]
    root = 1.0 / math.sqrt(HEAD_DIM)

    def copy(i):
        return pltpu.make_async_copy(cache.at[owners[i]], kv.at[i], sems.at[i])

    for i in range(count):
        copy(i).start()
    qs[...] = jnp.zeros_like(qs)
    eye = lax.broadcasted_iota(jnp.int32, (rows, rows), 0) == lax.broadcasted_iota(
        jnp.int32, (rows, rows), 1
    )
    token = lax.broadcasted_iota(jnp.int32, (rows, tokens), 1)
    step_of_row = lax.broadcasted_iota(jnp.int32, (rows, FRESH_ROWS), 0) % steps
    fresh_valid = lax.broadcasted_iota(jnp.int32, (rows, FRESH_ROWS), 1) <= step_of_row
    for i in range(count):
        part, slot = divmod(i, slots)
        if slot == 0:
            for h in range(heads):
                qf[h] = (qa, qb)[part][:, h * HEAD_DIM : (h + 1) * HEAD_DIM].astype(F32)
        buf = i % 2
        for h in range(heads):
            k = h // per_kv
            qs[buf, h * steps : (h + 1) * steps, k * HEAD_DIM : (k + 1) * HEAD_DIM] = qf[
                h, pl.ds(slot, steps, stride=slots), :
            ]
        query = qs[buf].astype(BF16)
        copy(i).wait()
        nt = (((1,), (1,)), ((), ()))
        scores = lax.dot_general(query, kv[i, 0], nt, preferred_element_type=F32) * root
        valid = token < limits[i]
        scores = jnp.where(valid, scores, NEGATIVE)
        top = jnp.max(scores, axis=1, keepdims=True)
        with_fresh = fresh and part == 0
        if with_fresh:
            new_scores = lax.dot_general(query, nk[slot], nt, preferred_element_type=F32) * root
            new_scores = jnp.where(fresh_valid, new_scores, NEGATIVE)
            top = jnp.maximum(top, jnp.max(new_scores, axis=1, keepdims=True))
        weights = jnp.where(valid, jnp.exp(scores - top), 0.0)
        total = jnp.sum(weights, axis=1, keepdims=True)
        value = jnp.dot(weights.astype(BF16), kv[i, 1], preferred_element_type=F32)
        if with_fresh:
            new_weights = jnp.where(fresh_valid, jnp.exp(new_scores - top), 0.0)
            total = total + jnp.sum(new_weights, axis=1, keepdims=True)
            value = value + jnp.dot(new_weights.astype(BF16), nv[slot], preferred_element_type=F32)
        for k in range(kvl):
            block = slice(k * per_kv * steps, (k + 1) * per_kv * steps)
            out[i, block, :] = value[block, k * HEAD_DIM : (k + 1) * HEAD_DIM]
        out[i, rows : rows + 1, :rows] = jnp.sum(jnp.where(eye, top, 0.0), axis=0, keepdims=True)
        out[i, rows + 1 : rows + 2, :rows] = jnp.sum(jnp.where(eye, total, 0.0), axis=0, keepdims=True)


def merge_stats(a, b, i, rows):
    top_a, total_a = a[i, rows : rows + 1, :rows], a[i, rows + 1 : rows + 2, :rows]
    top_b, total_b = b[i, rows : rows + 1, :rows], b[i, rows + 1 : rows + 2, :rows]
    top = jnp.maximum(top_a, top_b)
    scale_a, scale_b = jnp.exp(top_a - top), jnp.exp(top_b - top)
    return top, total_a * scale_a + total_b * scale_b, scale_a, scale_b


def as_column(row, eye):
    return jnp.sum(jnp.where(eye, row, 0.0), axis=1, keepdims=True)


def merge_kernel(a, b, out):
    rows = a.shape[1] - STAT_ROWS
    eye = lax.broadcasted_iota(jnp.int32, (rows, rows), 0) == lax.broadcasted_iota(
        jnp.int32, (rows, rows), 1
    )
    for i in range(a.shape[0]):
        top, total, scale_a, scale_b = merge_stats(a, b, i, rows)
        out[i, :rows, :] = a[i, :rows, :] * as_column(scale_a, eye) + b[i, :rows, :] * as_column(scale_b, eye)
        out[i, rows : rows + 1, :rows] = top
        out[i, rows + 1 : rows + 2, :rows] = total


def finish_kernel(steps, a, b, out, wide):
    rows = a.shape[1] - STAT_ROWS
    slots = a.shape[0]
    eye = lax.broadcasted_iota(jnp.int32, (rows, rows), 0) == lax.broadcasted_iota(
        jnp.int32, (rows, rows), 1
    )
    for i in range(slots):
        _, total, scale_a, scale_b = merge_stats(a, b, i, rows)
        weighted = a[i, :rows, :] * as_column(scale_a, eye) + b[i, :rows, :] * as_column(scale_b, eye)
        weighted = weighted / as_column(total, eye)
        for h in range(rows // steps):
            wide[h, pl.ds(i, steps, stride=slots), :] = weighted[h * steps : (h + 1) * steps, :]
    for h in range(rows // steps):
        out[:, h * HEAD_DIM : (h + 1) * HEAD_DIM] = wide[h].astype(BF16)


def attend(fresh, steps, slots, kvl, owners, limits, queries, new_keys, new_values, cache):
    rows = queries[0].shape[1] // HEAD_DIM * steps
    count = 2 * slots
    tokens, columns = cache.shape[2:]
    return pl.pallas_call(
        functools.partial(attend_kernel, fresh, steps, slots, kvl),
        out_shape=jax.ShapeDtypeStruct((count, rows + STAT_ROWS, HEAD_DIM), F32),
        in_specs=[SMEM, SMEM, VMEM, VMEM, VMEM, VMEM, ANYWHERE],
        out_specs=VMEM,
        scratch_shapes=[
            pltpu.VMEM((count, 2, tokens, columns), BF16),
            pltpu.VMEM((rows // steps, queries[0].shape[0], HEAD_DIM), F32),
            pltpu.VMEM((2, rows, columns), F32),
            pltpu.SemaphoreType.DMA((count,)),
        ],
        compiler_params=params(32),
        cost_estimate=pl.CostEstimate(
            flops=count * 4 * rows * tokens * columns,
            bytes_accessed=count * 4 * tokens * columns,
            transcendentals=count * rows * tokens,
        ),
        name="attend",
    )(owners, limits, *queries, new_keys, new_values, cache)


def merge(a, b):
    return pl.pallas_call(
        merge_kernel,
        out_shape=jax.ShapeDtypeStruct(a.shape, F32),
        in_specs=[VMEM] * 2,
        out_specs=VMEM,
        name="merge",
    )(a, b)


def per_device(
    step_token_states,
    input_norm_gain,
    wq,
    wkv,
    wo,
    adapter_down,
    adapter_up,
    prompt_cache_pool,
    prompt_slot,
    prompt_cache_length,
    slot_adapter,
    adapter_ranks,
):
    sections = lax.axis_size("section")
    tp_width = lax.axis_size("tp")
    section_id = lax.axis_index("section")
    tp_id = lax.axis_index("tp")
    steps, slots, model_width = step_token_states.shape
    requests = prompt_slot.shape[0]
    section_tokens = prompt_cache_pool.shape[2]
    cols_dev = prompt_cache_pool.shape[3]
    adapters = adapter_down.shape[0]
    rank = adapter_down.shape[2]
    local_heads = QUERY_HEADS // tp_width
    kvl = max(1, local_heads // PER_KV)
    kv_start = tp_id * local_heads // PER_KV * HEAD_DIM
    rows = steps * slots
    slice_cols = model_width // tp_width
    assert sections == 4

    position_section = section_id ^ jnp.arange(sections, dtype=jnp.int32)
    slot_ids = (position_section[:, None] * slots + jnp.arange(slots, dtype=jnp.int32)).reshape(-1)
    owns = prompt_slot[None, :] == slot_ids[:, None]
    owners = jnp.sum(jnp.where(owns, jnp.arange(requests, dtype=jnp.int32), 0), axis=1)
    lengths = jnp.sum(jnp.where(owns, prompt_cache_length, 0), axis=1)
    slot_here = jnp.arange(requests, dtype=jnp.int32)[None, :] == slot_ids[:, None]
    adapter_of = jnp.sum(jnp.where(slot_here, slot_adapter, 0), axis=1)
    rank_is = jnp.arange(adapter_ranks.shape[0], dtype=jnp.int32)[None, :] == adapter_of[:, None]
    ranks = jnp.sum(jnp.where(rank_is, adapter_ranks, 0), axis=1)
    limits = jnp.clip(lengths - section_id * section_tokens, 0, section_tokens)

    def by_row(per_slot):
        wide = jnp.broadcast_to(
            per_slot.reshape((sections, 1, slots) + per_slot.shape[1:]),
            (sections, steps, slots) + per_slot.shape[1:],
        )
        return wide.reshape((sections * rows,) + per_slot.shape[1:])

    local = adapter_of - section_id * adapters
    pick = by_row((local[:, None] == jnp.arange(adapters, dtype=jnp.int32)).astype(F32))
    scale = jnp.where(
        jnp.arange(rank)[None, :] < ranks[:, None], ADAPTER_ALPHA / ranks.astype(F32)[:, None], 0.0
    )
    scale = by_row(scale)
    step_of = jnp.broadcast_to(
        jnp.arange(steps, dtype=jnp.int32)[None, :, None], (sections, steps, slots)
    ).reshape(-1)
    cosine, sine = rotary_tables(by_row(lengths) + step_of)

    normed = normalize(step_token_states, input_norm_gain).reshape(rows, model_width)
    piece = lax.dynamic_slice_in_dim(normed, tp_id * slice_cols, slice_cols, 1)
    piece_across = swap(piece, "section", 2)
    piece_beside, piece_beside_across = swap((piece, piece_across), "section", 1)

    plain = jnp.dot(normed, wq, preferred_element_type=F32)
    plain_across = swap(plain, "section", 2)
    plain_beside, plain_beside_across = swap((plain, plain_across), "section", 1)
    kv_part = jnp.dot(normed, wkv, preferred_element_type=F32)

    rank_part = pl.pallas_call(
        down_kernel,
        out_shape=jax.ShapeDtypeStruct((sections * rows, rank), F32),
        in_specs=[VMEM] * 6,
        out_specs=VMEM,
        name="down",
    )(piece, piece_across, piece_beside, piece_beside_across, pick, adapter_down)
    if tp_width <= 4:
        parts = jnp.stack([rank_part] + [swap(rank_part, "tp", bit) for bit in range(1, tp_width)])
    else:
        parts = lax.psum(rank_part, "tp")[None]

    masked = pl.pallas_call(
        query_kernel,
        out_shape=jax.ShapeDtypeStruct((sections * rows, plain.shape[1]), BF16),
        in_specs=[VMEM] * 10,
        out_specs=VMEM,
        name="queries",
    )(
        parts,
        scale,
        pick,
        adapter_up,
        plain,
        plain_across,
        plain_beside,
        plain_beside_across,
        cosine,
        sine,
    ).reshape(sections, rows, plain.shape[1])
    other = swap(masked, "section", 1)
    own_pair, across_pair = masked[0] + other[1], masked[2] + other[3]
    own_far, across_far = swap((across_pair, own_pair), "section", 2)
    query_own, query_across = own_pair + own_far, across_pair + across_far
    query_beside, query_beside_across = swap((query_own, query_across), "section", 1)

    kv_full = lax.all_gather(kv_part, "tp", axis=1, tiled=True)
    kv_cols = KVH * HEAD_DIM
    key_rows = lax.dynamic_slice_in_dim(kv_full, kv_start, kvl * HEAD_DIM, 1)
    value_rows = lax.dynamic_slice_in_dim(kv_full, kv_cols + kv_start, kvl * HEAD_DIM, 1)

    def by_slot(array):
        array = array.astype(BF16).reshape(steps, slots, kvl * HEAD_DIM).transpose(1, 0, 2)
        return jnp.pad(array, ((0, 0), (0, FRESH_ROWS - steps), (0, 0)))

    turned = [
        key_rows[:, k * HEAD_DIM : (k + 1) * HEAD_DIM] * cosine[:rows]
        + jnp.roll(key_rows[:, k * HEAD_DIM : (k + 1) * HEAD_DIM], HEAD_DIM // 2, 1) * sine[:rows]
        for k in range(kvl)
    ]
    new_keys, new_values = by_slot(jnp.concatenate(turned, 1)), by_slot(value_rows)

    cache = prompt_cache_pool
    if cols_dev < HEAD_DIM:
        share = HEAD_DIM // cols_dev
        groups = [list(range(g, g + share)) for g in range(0, tp_width, share)]
        cache = lax.all_gather(cache, "tp", axis=3, tiled=True, axis_index_groups=groups)

    owners, limits = owners.reshape(sections, slots), limits.reshape(sections, slots)

    def attend_two(positions, fresh, queries):
        chosen = jnp.asarray(positions)
        return attend(
            fresh, steps, slots, kvl, jnp.concatenate([owners[j] for j in positions]),
            jnp.concatenate([limits[j] for j in positions]), queries, new_keys, new_values, cache,
        )

    sent = attend_two((3, 1), False, (query_beside_across, query_beside))
    kept = attend_two((0, 2), True, (query_own, query_across))
    received = swap(sent, "section", 1)
    across = merge(kept[slots:], received[:slots])
    own = merge(kept[:slots], received[slots:])
    far = swap(across, "section", 2)
    attended = pl.pallas_call(
        functools.partial(finish_kernel, steps),
        out_shape=jax.ShapeDtypeStruct((rows, plain.shape[1]), BF16),
        in_specs=[VMEM] * 2,
        out_specs=VMEM,
        scratch_shapes=[pltpu.VMEM((local_heads, rows, HEAD_DIM), F32)],
        name="finish",
    )(own, far)

    partial_out = jnp.dot(attended, wo, preferred_element_type=F32).astype(BF16)
    if tp_width <= 4:
        quarter = model_width // tp_width

        def part_of(bit):
            return lax.dynamic_slice_in_dim(partial_out, (tp_id ^ bit) * quarter, quarter, 1)

        total = part_of(0).astype(F32)
        for bit in range(1, tp_width):
            total = total + swap(part_of(bit), "tp", bit).astype(F32)
        total = total.astype(BF16)
        result = jnp.zeros((rows, model_width), BF16)
        for bit in range(tp_width):
            chunk = swap(total, "tp", bit) if bit else total
            result = lax.dynamic_update_slice_in_dim(result, chunk, (tp_id ^ bit) * quarter, 1)
    else:
        result = lax.psum(partial_out, "tp")
    return result.reshape(steps, slots, model_width)


def solution(mesh):
    return jax.shard_map(
        per_device,
        mesh=mesh,
        in_specs=(
            P(None, ("groups", "section"), None),
            P(),
            P(None, "tp"),
            P(None, "tp"),
            P("tp", None),
            P(("groups", "section"), "tp", None),
            P(("groups", "section"), None, "tp"),
            P("groups", None, "section", "tp"),
            P("groups"),
            P("groups"),
            P("groups"),
            P("groups"),
        ),
        out_specs=P(None, ("groups", "section"), None),
        check_vma=False,
    )
```

```python
import functools
import math

import jax
import jax.numpy as jnp
from jax import lax
from jax.experimental import pallas as pl
from jax.experimental.pallas import tpu as pltpu
from jax.sharding import PartitionSpec as P

QUERY_HEADS = 64
KVH = 8
HEAD_DIM = 128
PER_KV = QUERY_HEADS // KVH

EPSILON = 1e-05
ROPE_BASE = 500000.0
ADAPTER_ALPHA = 16.0
NEGATIVE = -1e30
STAT_ROWS = 8
FRESH_ROWS = 16
GROUP = 4
F32 = jnp.float32
BF16 = jnp.bfloat16
VMEM = pl.BlockSpec(memory_space=pltpu.VMEM)
SMEM = pl.BlockSpec(memory_space=pltpu.SMEM)
IN_HBM = pl.BlockSpec(memory_space=pltpu.HBM)
QUICK = pl.CostEstimate(flops=1, bytes_accessed=1, transcendentals=0)


def in_hbm(value):
    return pltpu.with_memory_space_constraint(value, pltpu.HBM)


def in_vmem(*values):
    return [pltpu.with_memory_space_constraint(value, pltpu.VMEM) for value in values]


def params(mebibytes):
    return pltpu.CompilerParams(vmem_limit_bytes=mebibytes * 1024 * 1024)


def swap(value, axis, bit):
    size = lax.axis_size(axis)
    pairs = [(i, i ^ bit) for i in range(size)]
    return jax.tree.map(lambda a: lax.ppermute(a, axis, pairs), value)


def tables_kernel(slots, section_tokens, adapters, here, prompt_slot, prompt_length, slot_adapter, ranks, frequency, *outs):
    owners, limits, pick, scale, cosine, sine = outs
    section = here[0]
    requests = owners.shape[0]
    shape = pick.shape
    row = lax.broadcasted_iota(jnp.int32, shape, 0)
    lane = lax.broadcasted_iota(jnp.int32, shape, 1)

    def place(slot):
        return (lax.div(slot, slots) ^ section) * slots + lax.rem(slot, slots)

    lengths = jnp.zeros(shape, jnp.int32)
    adapter = jnp.zeros(shape, jnp.int32)
    rank = jnp.zeros(shape, jnp.int32)
    for i in range(requests):
        at, length = place(prompt_slot[i]), prompt_length[i]
        owners[at] = i
        limits[at] = jnp.clip(length - section * section_tokens, 0, section_tokens)
        lengths = jnp.where(row == at, length, lengths)
        at, chosen = place(i), slot_adapter[i]
        adapter = jnp.where(row == at, chosen, adapter)
        rank = jnp.where(row == at, ranks[chosen], rank)
    held = jnp.where(lane < adapters, section * adapters + lane, (section ^ 1) * adapters + lane - adapters)
    pick[...] = jnp.where((lane < 2 * adapters) & (adapter == held), 1.0, 0.0)
    rank_f32 = rank.astype(F32)
    scale[...] = jnp.where(lane < rank, ADAPTER_ALPHA / rank_f32, 0.0)
    steps = cosine.shape[0] // requests
    positions = by_row(lengths, steps, slots).astype(F32)
    step = lax.rem(lax.div(lax.broadcasted_iota(jnp.int32, cosine.shape, 0), slots), steps)
    angles = (positions + step.astype(F32)) * frequency[...]
    cosine[...] = jnp.cos(angles)
    low = lax.broadcasted_iota(jnp.int32, cosine.shape, 1) < HEAD_DIM // 2
    sine[...] = jnp.where(low, -jnp.sin(angles), jnp.sin(angles))


def norm_kernel(here, states, gain, normed, piece, wide, gains):
    steps, slots, width = states.shape
    gains[...] = gain[...].astype(F32)
    for t in range(steps):
        values = states[t].astype(F32)
        inverse = lax.rsqrt(jnp.mean(values * values, axis=-1, keepdims=True) + EPSILON)
        for c in range(width // 128):
            cols = slice(c * 128, (c + 1) * 128)
            wide[t * slots : (t + 1) * slots, cols] = values[:, cols] * inverse * gains[c : c + 1, :]
    normed[...] = wide[...].astype(BF16)
    cols = piece.shape[1]
    piece[...] = wide[:, pl.ds(pl.multiple_of(here[1] * cols, 128), cols)].astype(BF16)


def product_kernel(chunk, count_left, starts, here, *refs):
    lefts, right, refs = refs[:count_left], refs[count_left], refs[count_left + 1 :]
    *refs, held, sems, carry_sems = refs
    half = (len(refs) - len(starts)) // 2
    sources, outs, targets = refs[:half], refs[half : half + len(starts)], refs[half + len(starts) :]
    carries = [
        pltpu.make_async_copy(source, target, carry_sems.at[i])
        for i, (source, target) in enumerate(zip(sources, targets))
    ]
    slots, cols = held.shape[0], held.shape[2]
    chunks = right.shape[0] // chunk
    count = chunks * len(outs)

    def copy(n):
        block, i = divmod(n, chunks)
        first = pl.multiple_of(starts[block](here) * 128, 128)
        source = right.at[pl.ds(i * chunk, chunk), pl.ds(first, cols)]
        return pltpu.make_async_copy(source, held.at[n % slots], sems.at[n % slots])

    for n in range(min(slots, count)):
        copy(n).start()
    for carry in carries:
        carry.start()
    for n in range(count):
        block, i = divmod(n, chunks)
        copy(n).wait()
        left = jnp.concatenate([ref[:, i * chunk : (i + 1) * chunk] for ref in lefts], axis=0)
        part = jnp.dot(left, held[n % slots], preferred_element_type=F32)
        total = part if i == 0 else total + part
        if n + slots < count:
            copy(n + slots).start()
        if i + 1 == chunks:
            outs[block][...] = total.astype(outs[block].dtype)
    for carry in carries:
        carry.wait()


def product(name, here, lefts, right, starts, cols, types, chunk, carried=()):
    rows = sum(left.shape[0] for left in lefts)
    slots = min(8, right.shape[0] // chunk * len(starts))
    return pl.pallas_call(
        functools.partial(product_kernel, chunk, len(lefts), starts),
        out_shape=tuple(pltpu.VMEM((rows, cols), dtype) for dtype in types)
        + tuple(pltpu.VMEM(c.shape, c.dtype) for c in carried),
        in_specs=[SMEM] + [VMEM] * len(lefts) + [IN_HBM] * (1 + len(carried)),
        out_specs=(VMEM,) * (len(types) + len(carried)),
        scratch_shapes=[
            pltpu.VMEM((slots, chunk, cols), BF16),
            pltpu.SemaphoreType.DMA((slots,)),
            pltpu.SemaphoreType.DMA((max(1, len(carried)),)),
        ],
        compiler_params=params(14),
        cost_estimate=QUICK,
        name=name,
    )(here, *in_vmem(*lefts), in_hbm(right), *[in_hbm(c) for c in carried])


def add_kernel(*refs):
    *terms, out = refs
    total = terms[0][...].astype(F32)
    for term in terms[1:]:
        total = total + term[...].astype(F32)
    out[...] = total.astype(out.dtype)


def add(*terms):
    return pl.pallas_call(
        add_kernel,
        out_shape=pltpu.VMEM(terms[0].shape, BF16),
        in_specs=[VMEM] * len(terms),
        out_specs=VMEM,
        compiler_params=params(8),
        cost_estimate=QUICK,
        name="add",
    )(*in_vmem(*terms))


def by_row(table, steps, slots):
    blocks = [table[i : i + slots] for i in range(0, table.shape[0], slots)]
    return jnp.concatenate([block for block in blocks for _ in range(steps)], axis=0)


def down_kernel(steps, slots, own, beside, across, beside_across, pick, down, down_beside, out):
    states = jnp.concatenate([ref[...] for ref in (own, beside, across, beside_across)], axis=0)
    picks = by_row(pick[...], steps, slots)
    adapters = down.shape[0]
    total = jnp.zeros(out.shape, F32)
    for a in range(2 * adapters):
        part = jnp.dot(states, (down, down_beside)[a // adapters][a % adapters], preferred_element_type=F32)
        total = jnp.where(picks[:, a : a + 1] > 0, part, total)
    out[...] = total


def query_kernel(steps, slots, count, here, *refs):
    parts, refs = refs[:count], refs[count:]
    scale, pick, up, up_beside, cosine, sine, plain_near, plain_far, near, far = refs
    rank_sum = parts[0][...]
    for part in parts[1:]:
        rank_sum = rank_sum + part[...]
    scales = by_row(scale[...], steps, slots)
    picks = by_row(pick[...], steps, slots)
    low_rank = jnp.where(scales > 0, rank_sum * scales, 0.0)
    adapters, rank, width = up.shape
    wide = jnp.concatenate(
        [jnp.where(picks[:, a : a + 1] > 0, low_rank, 0.0) for a in range(2 * adapters)], axis=1
    ).astype(BF16)
    depth = adapters * rank
    ups = [ref.reshape(depth, width) for ref in (up, up_beside)]
    half = plain_near.shape[1]
    rows = steps * slots
    shown = jnp.sum(picks, axis=1, keepdims=True) > 0
    first = (here[0] & 1) * half
    step = min(2 * HEAD_DIM, half)
    for c in range(0, half, step):
        block = pl.ds(pl.multiple_of(first + c, 128), step)
        changes = jnp.dot(wide[:, :depth], ups[0][:, block], preferred_element_type=F32)
        changes = changes + jnp.dot(wide[:, depth:], ups[1][:, block], preferred_element_type=F32)
        for h in range(0, step, HEAD_DIM):
            cols = slice(c + h, c + h + HEAD_DIM)
            plain = jnp.concatenate([plain_near[:, cols], plain_far[:, cols]], axis=0)
            query = plain + changes[:, h : h + HEAD_DIM]
            turned = query * cosine[...] + pltpu.roll(query, HEAD_DIM // 2, 1) * sine[...]
            turned = jnp.where(shown, turned, 0.0).astype(BF16)
            for position in range(4):
                target = (near, far)[position // 2]
                target[position % 2, :, cols] = turned[position * rows : (position + 1) * rows]


def fetch_kernel(owners, cache, up, *refs):
    *outs, up_out, done, held, key_sems, value_sems, up_sem = refs
    sections = len(outs) // 2
    slots, ring = outs[0].shape[0], held.shape[0]
    count = sections * slots
    order = [(p, i) for p in (3, 2, 1, 0) for i in range(slots)]

    def key_copy(n):
        position, i = order[n]
        source = cache.at[owners[position * slots + i], 0]
        return pltpu.make_async_copy(source, held.at[n % ring], key_sems.at[n % ring])

    def value_copy(n):
        position, i = order[n]
        source = cache.at[owners[position * slots + i], 1]
        return pltpu.make_async_copy(source, outs[sections + position].at[i], value_sems.at[n])

    up_copy = pltpu.make_async_copy(up, up_out, up_sem.at[0])
    for n in range(ring):
        key_copy(n).start()
        value_copy(n).start()
    up_copy.start()
    for n in range(count):
        position, i = order[n]
        key_copy(n).wait()
        outs[position][i] = held[n % ring].T
        if n + ring < count:
            key_copy(n + ring).start()
            value_copy(n + ring).start()
    done[...] = jnp.zeros_like(done)
    up_copy.wait()
    for n in range(count):
        value_copy(n).wait()


def hold_kernel(starts, here, source, *refs):
    *outs, done, sems = refs
    cols = outs[0].shape[1]
    copies = []
    for i, out in enumerate(outs):
        first = pl.multiple_of(starts[i](here) * 128, 128)
        copies.append(pltpu.make_async_copy(source.at[:, pl.ds(first, cols)], out, sems.at[i]))
    for copy in copies:
        copy.start()
    done[...] = jnp.zeros_like(done)
    for copy in copies:
        copy.wait()


def place_kernel(starts, here, *refs):
    *blocks, out, sems = refs
    copies = []
    for i, block in enumerate(blocks):
        cols = block.shape[1]
        first = pl.multiple_of(starts[i](here) * 128, 128)
        copies.append(pltpu.make_async_copy(block, out.at[:, pl.ds(first, cols)], sems.at[i]))
    for copy in copies:
        copy.start()
    for copy in copies:
        copy.wait()


def held_output_kernel(left, *refs):
    half = len(refs) // 2
    for right, out in zip(refs[:half], refs[half:]):
        out[...] = jnp.dot(left[...], right[...], preferred_element_type=F32).astype(out.dtype)


def attend_kernel(position, steps, slots, kvl, here, limits, own, other, keys, values, *refs):
    fresh = position == 0
    if fresh:
        first, second, cosine, sine, out, qf, qs, turned, nk, nv = refs
    else:
        out, qf, qs = refs
    half = own.shape[2] // HEAD_DIM
    heads = 2 * half
    per_kv = heads // kvl
    rows = heads * steps
    tokens = values.shape[1]
    root = 1.0 / math.sqrt(HEAD_DIM)
    qs[...] = jnp.zeros_like(qs)
    lower = here[0] & 1 == 0
    for h in range(half):
        cols = slice(h * HEAD_DIM, (h + 1) * HEAD_DIM)
        mine = own[position % 2, :, cols].astype(F32)
        theirs = other[1 - position % 2, :, cols].astype(F32)
        qf[h] = jnp.where(lower, mine, theirs)
        qf[half + h] = jnp.where(lower, theirs, mine)
    for i in range(slots):
        for h in range(heads):
            k = h // per_kv
            qs[i, h * steps : (h + 1) * steps, k * HEAD_DIM : (k + 1) * HEAD_DIM] = qf[
                h, pl.ds(i, steps, stride=slots), :
            ]
    if fresh:
        step_of_row = lax.broadcasted_iota(jnp.int32, (rows, FRESH_ROWS), 0) % steps
        fresh_valid = lax.broadcasted_iota(jnp.int32, (rows, FRESH_ROWS), 1) <= step_of_row
        rows_here = steps * slots
        nk[...] = jnp.zeros_like(nk)
        nv[...] = jnp.zeros_like(nv)
        for k in range(kvl):
            cols = slice(k * HEAD_DIM, (k + 1) * HEAD_DIM)
            swapped = here[1] & 1 == 1
            key = jnp.where(swapped, second[:, cols], first[:, cols])
            turned[0, k] = key * cosine[:rows_here, :] + pltpu.roll(key, HEAD_DIM // 2, 1) * sine[:rows_here, :]
            turned[1, k] = jnp.where(swapped, first[:, cols], second[:, cols])
            for i in range(slots):
                nk[i, :steps, cols] = turned[0, k, pl.ds(i, steps, stride=slots), :]
                nv[i, :steps, cols] = turned[1, k, pl.ds(i, steps, stride=slots), :]
    eye = diagonal(rows)
    token = lax.broadcasted_iota(jnp.int32, (rows, tokens), 1)
    for i in range(slots):
        limit = limits[position * slots + i]
        queries = qs[i].astype(BF16)
        scores = jnp.dot(queries, keys[i], preferred_element_type=F32) * root
        valid = token < limit
        scores = jnp.where(valid, scores, NEGATIVE)
        top = jnp.max(scores, axis=1, keepdims=True)
        if fresh:
            new_scores = lax.dot_general(
                queries, nk[i].astype(BF16), (((1,), (1,)), ((), ())), preferred_element_type=F32
            )
            new_scores = jnp.where(fresh_valid, new_scores * root, NEGATIVE)
            top = jnp.maximum(top, jnp.max(new_scores, axis=1, keepdims=True))
        weights = jnp.where(valid, jnp.exp(scores - top), 0.0)
        total = jnp.sum(weights, axis=1, keepdims=True)
        value = jnp.dot(weights.astype(BF16), values[i], preferred_element_type=F32)
        if fresh:
            new_weights = jnp.where(fresh_valid, jnp.exp(new_scores - top), 0.0)
            total = total + jnp.sum(new_weights, axis=1, keepdims=True)
            value = value + jnp.dot(
                new_weights.astype(BF16), nv[i].astype(BF16), preferred_element_type=F32
            )
        for k in range(kvl):
            block = slice(k * per_kv * steps, (k + 1) * per_kv * steps)
            out[i, block, :] = value[block, k * HEAD_DIM : (k + 1) * HEAD_DIM]
        out[i, rows : rows + 1, :rows] = jnp.sum(jnp.where(eye, top, 0.0), axis=0, keepdims=True)
        out[i, rows + 1 : rows + 2, :rows] = jnp.sum(jnp.where(eye, total, 0.0), axis=0, keepdims=True)


def joined(refs, i, rows, eye):
    tops = [ref[i, rows : rows + 1, :rows] for ref in refs]
    top = functools.reduce(jnp.maximum, tops)
    total, weighted = 0.0, 0.0
    for ref, part_top in zip(refs, tops):
        scale = jnp.exp(part_top - top)
        total = total + ref[i, rows + 1 : rows + 2, :rows] * scale
        column = jnp.sum(jnp.where(eye, scale, 0.0), axis=1, keepdims=True)
        weighted = weighted + ref[i, :rows, :] * column
    return weighted, top, total


def diagonal(rows):
    return lax.broadcasted_iota(jnp.int32, (rows, rows), 0) == lax.broadcasted_iota(
        jnp.int32, (rows, rows), 1
    )


def merge_kernel(a, b, out):
    rows = a.shape[1] - STAT_ROWS
    eye = diagonal(rows)
    for i in range(a.shape[0]):
        weighted, top, total = joined((a, b), i, rows, eye)
        out[i, :rows, :] = weighted
        out[i, rows : rows + 1, :rows] = top
        out[i, rows + 1 : rows + 2, :rows] = total


def finish_kernel(steps, a, b, c, out, wide):
    rows = a.shape[1] - STAT_ROWS
    slots = a.shape[0]
    eye = diagonal(rows)
    for i in range(slots):
        weighted, _, total = joined((a, b, c), i, rows, eye)
        weighted = weighted / jnp.sum(jnp.where(eye, total, 0.0), axis=1, keepdims=True)
        for h in range(rows // steps):
            wide[h, pl.ds(i, steps, stride=slots), :] = weighted[h * steps : (h + 1) * steps, :]
    for h in range(rows // steps):
        out[:, h * HEAD_DIM : (h + 1) * HEAD_DIM] = wide[h].astype(BF16)


def attend(position, steps, slots, kvl, here, limits, own, other, keys, values, *new):
    heads = 2 * own.shape[2] // HEAD_DIM
    rows, columns = heads * steps, values.shape[2]
    scratch = [
        pltpu.VMEM((heads, steps * slots, HEAD_DIM), F32),
        pltpu.VMEM((slots, rows, columns), F32),
    ]
    if new:
        scratch += [
            pltpu.VMEM((2, kvl, steps * slots, HEAD_DIM), F32),
            pltpu.VMEM((slots, FRESH_ROWS, columns), F32),
            pltpu.VMEM((slots, FRESH_ROWS, columns), F32),
        ]
    return pl.pallas_call(
        functools.partial(attend_kernel, position, steps, slots, kvl),
        out_shape=pltpu.VMEM((slots, rows + STAT_ROWS, HEAD_DIM), F32),
        in_specs=[SMEM] * 2 + [VMEM] * (4 + len(new)),
        out_specs=VMEM,
        scratch_shapes=scratch,
        compiler_params=params(8),
        cost_estimate=QUICK,
        name="attend",
    )(here, limits, *in_vmem(own, other, keys, values, *new))


def merge(a, b):
    return pl.pallas_call(
        merge_kernel,
        out_shape=pltpu.VMEM(a.shape, F32),
        in_specs=[VMEM] * 2,
        out_specs=VMEM,
        compiler_params=params(8),
        cost_estimate=QUICK,
        name="merge",
    )(*in_vmem(a, b))


def per_device(
    step_token_states,
    input_norm_gain,
    wq,
    wkv,
    wo,
    adapter_down,
    adapter_up,
    prompt_cache_pool,
    prompt_slot,
    prompt_cache_length,
    slot_adapter,
    adapter_ranks,
):
    sections = lax.axis_size("section")
    tp_width = lax.axis_size("tp")
    here = jnp.stack([lax.axis_index("section"), lax.axis_index("tp")]).astype(jnp.int32)
    steps, slots, model_width = step_token_states.shape
    requests = prompt_slot.shape[0]
    section_tokens = prompt_cache_pool.shape[2]
    cols_dev = prompt_cache_pool.shape[3]
    adapters, slice_cols, rank = adapter_down.shape
    local_heads = QUERY_HEADS // tp_width
    half_cols = local_heads // 2 * HEAD_DIM
    kvl = max(1, local_heads // PER_KV)
    width = kvl * HEAD_DIM
    rows = steps * slots
    assert sections == 4

    exponents = jnp.arange(HEAD_DIM // 2, dtype=F32) * (2.0 / HEAD_DIM)
    frequency = ROPE_BASE ** (-exponents)
    frequency = jnp.concatenate([frequency, frequency])[None]
    ints = jax.ShapeDtypeStruct((requests,), jnp.int32)
    owners, limits, pick, scale, cosine, sine = pl.pallas_call(
        functools.partial(tables_kernel, slots, section_tokens, adapters),
        out_shape=(ints, ints)
        + (pltpu.VMEM((requests, rank), F32),) * 2
        + (pltpu.VMEM((sections * rows, HEAD_DIM), F32),) * 2,
        in_specs=[SMEM] * 5 + [VMEM],
        out_specs=(SMEM, SMEM) + (VMEM,) * 4,
        compiler_params=params(8),
        cost_estimate=QUICK,
        name="tables",
    )(here, prompt_slot, prompt_cache_length, slot_adapter, adapter_ranks, frequency)

    normed, piece = pl.pallas_call(
        norm_kernel,
        out_shape=(pltpu.VMEM((rows, model_width), BF16), pltpu.VMEM((rows, slice_cols), BF16)),
        in_specs=[SMEM, VMEM, VMEM],
        out_specs=(VMEM, VMEM),
        scratch_shapes=[
            pltpu.VMEM((rows, model_width), F32),
            pltpu.VMEM((model_width // 128, 128), F32),
        ],
        compiler_params=params(8),
        cost_estimate=QUICK,
        name="norm",
    )(here, step_token_states, input_norm_gain.reshape(model_width // 128, 128))
    normed_beside = swap(normed, "section", 1)
    piece_across = swap(piece, "section", 2)
    piece_beside = swap(piece, "section", 1)
    late_down, late_up, _ = lax.optimization_barrier((adapter_down, adapter_up, normed_beside))
    down_beside = swap(late_down, "section", 1)
    up_beside = swap(late_up, "section", 1)

    chunk = min(256, model_width // 2)
    plain_near, held_down = product(
        "query", here, (normed, normed_beside), wq,
        [lambda at: (at[0] & 1) * (half_cols // 128)], half_cols, [F32], chunk, (adapter_down,),
    )
    plain_far = swap(plain_near, "section", 2)
    piece_beside_across = swap(piece_across, "section", 1)
    rank_part = pl.pallas_call(
        functools.partial(down_kernel, steps, slots),
        out_shape=pltpu.VMEM((sections * rows, rank), F32),
        in_specs=[VMEM] * 7,
        out_specs=VMEM,
        compiler_params=params(8),
        cost_estimate=QUICK,
        name="down",
    )(*in_vmem(piece, piece_beside, piece_across, piece_beside_across, pick, held_down, down_beside))
    if tp_width <= 4:
        parts = [rank_part] + [swap(rank_part, "tp", bit) for bit in range(tp_width - 1, 0, -1)]
    else:
        parts = [lax.psum(rank_part, "tp")]

    cache = prompt_cache_pool
    if cols_dev < HEAD_DIM:
        share = HEAD_DIM // cols_dev
        groups = [list(range(g, g + share)) for g in range(0, tp_width, share)]
        cache = lax.all_gather(cache, "tp", axis=3, tiled=True, axis_index_groups=groups)
    cache_ring = min(8, requests)
    *fetched, held_up, fetch_done = pl.pallas_call(
        fetch_kernel,
        out_shape=(pltpu.VMEM((slots, width, section_tokens), BF16),) * sections
        + (pltpu.VMEM((slots, section_tokens, width), BF16),) * sections
        + (pltpu.VMEM(adapter_up.shape, BF16), pltpu.VMEM((8, 128), F32)),
        in_specs=[SMEM, IN_HBM, IN_HBM],
        out_specs=(VMEM,) * (2 * sections + 2),
        scratch_shapes=[
            pltpu.VMEM((cache_ring, section_tokens, width), BF16),
            pltpu.SemaphoreType.DMA((cache_ring,)),
            pltpu.SemaphoreType.DMA((requests,)),
            pltpu.SemaphoreType.DMA((1,)),
        ],
        compiler_params=params(12),
        cost_estimate=QUICK,
        name="fetch",
    )(lax.optimization_barrier((owners, rank_part))[0], in_hbm(cache), in_hbm(adapter_up))
    scale = lax.optimization_barrier((scale, fetch_done))[0]

    pair = pltpu.VMEM((2, rows, half_cols), BF16)
    masked_near, masked_far = pl.pallas_call(
        functools.partial(query_kernel, steps, slots, len(parts)),
        out_shape=(pair, pair),
        in_specs=[SMEM] + [VMEM] * (len(parts) + 8),
        out_specs=(VMEM, VMEM),
        compiler_params=params(8),
        cost_estimate=QUICK,
        name="queries",
    )(here, *in_vmem(*parts, scale, pick, held_up, up_beside, cosine, sine, plain_near, plain_far))
    query_far = add(masked_far, swap(masked_near, "section", 2))
    query_near = add(masked_near, swap(masked_far, "section", 2))
    beside_far = swap(query_far, "section", 1)
    beside_near = swap(query_near, "section", 1)

    late_normed = lax.optimization_barrier((normed, masked_near))[0]
    if tp_width == 4:
        starts = [
            lambda at: jnp.where(at[1] >= 2, width // 128, 0),
            lambda at: jnp.where(at[1] >= 2, 0, width // 128),
        ]
        first, second = product("new_kv", here, (late_normed,), wkv, starts, width, [F32, F32], 1024)
        first = lax.ppermute(first, "tp", [(0, 0), (1, 2), (2, 1), (3, 3)])
        second = lax.ppermute(second, "tp", [(0, 1), (1, 3), (2, 0), (3, 2)])
    else:
        kv_part = jnp.dot(late_normed, wkv, preferred_element_type=F32)
        kv_full = lax.all_gather(kv_part, "tp", axis=1, tiled=True)
        kv_start = here[1] * local_heads // PER_KV * HEAD_DIM
        first = lax.dynamic_slice_in_dim(kv_full, kv_start, width, 1)
        second = lax.dynamic_slice_in_dim(kv_full, KVH * HEAD_DIM + kv_start, width, 1)
        odd = here[1] % 2 == 1
        first, second = jnp.where(odd, second, first), jnp.where(odd, first, second)

    def attend_to(position, own, other, *new):
        return attend(
            position, steps, slots, kvl, here, limits, own, other, fetched[position],
            fetched[sections + position], *new,
        )

    part_beside_across = attend_to(3, query_far, beside_far)
    part_across = attend_to(2, query_far, beside_far)
    across = merge(part_across, swap(part_beside_across, "section", 1))
    far = swap(across, "section", 2)
    late_near, late_beside, _ = lax.optimization_barrier((query_near, beside_near, across))
    part_beside = attend_to(1, late_near, late_beside)
    part_own = attend_to(0, late_near, late_beside, first, second, cosine, sine)
    final = (part_own, swap(part_beside, "section", 1), far)
    if tp_width <= 4:
        quarter = model_width // tp_width
        columns = [
            functools.partial(lambda bit, at: (at[1] ^ bit) * (quarter // 128), bit)
            for bit in range(tp_width)
        ]
        far_columns = columns[: tp_width // 2 - 1 : -1]
        near_columns = columns[tp_width // 2 - 1 :: -1]
        *held_wo, hold_done = pl.pallas_call(
            functools.partial(hold_kernel, far_columns),
            out_shape=(pltpu.VMEM((wo.shape[0], quarter), BF16),) * len(far_columns)
            + (pltpu.VMEM((8, 128), F32),),
            in_specs=[SMEM, IN_HBM],
            out_specs=(VMEM,) * (len(far_columns) + 1),
            scratch_shapes=[pltpu.SemaphoreType.DMA((len(far_columns),))],
            compiler_params=params(8),
            cost_estimate=QUICK,
            name="hold",
        )(lax.optimization_barrier((here, part_own, part_beside))[0], in_hbm(wo))
        final = lax.optimization_barrier((*final, hold_done))[:3]
    attended = pl.pallas_call(
        functools.partial(finish_kernel, steps),
        out_shape=pltpu.VMEM((rows, local_heads * HEAD_DIM), BF16),
        in_specs=[VMEM] * 3,
        out_specs=VMEM,
        scratch_shapes=[pltpu.VMEM((local_heads, rows, HEAD_DIM), F32)],
        compiler_params=params(8),
        cost_estimate=QUICK,
        name="finish",
    )(*in_vmem(*final))

    if tp_width <= 4:
        sent = pl.pallas_call(
            held_output_kernel,
            out_shape=(pltpu.VMEM((rows, quarter), BF16),) * len(held_wo),
            in_specs=[VMEM] * (1 + len(held_wo)),
            out_specs=(VMEM,) * len(held_wo),
            compiler_params=params(8),
            cost_estimate=QUICK,
            name="far_output",
        )(*in_vmem(attended, *held_wo))
        late = lax.optimization_barrier((attended, sent[0]))[0]
        types = [BF16] * (len(near_columns) - 1) + [F32]
        *more, total = product("near_output", here, (late,), wo, near_columns, quarter, types, wo.shape[0] // 8)
        sent = [*sent, *more]
        total = add(total, *[swap(sent[tp_width - 1 - bit], "tp", bit) for bit in range(1, tp_width)])
        blocks = [total] + [swap(total, "tp", bit) for bit in range(1, tp_width)]
        result = pl.pallas_call(
            functools.partial(place_kernel, columns),
            out_shape=jax.ShapeDtypeStruct((rows, model_width), BF16),
            in_specs=[SMEM] + [VMEM] * tp_width,
            out_specs=IN_HBM,
            scratch_shapes=[pltpu.SemaphoreType.DMA((tp_width,))],
            compiler_params=params(8),
            cost_estimate=QUICK,
            name="place",
        )(here, *in_vmem(*blocks))
    else:
        partial_out = jnp.dot(attended, wo, preferred_element_type=F32).astype(BF16)
        result = lax.psum(partial_out, "tp")
    return result.reshape(steps, slots, model_width)


def solution(mesh):
    return jax.shard_map(
        per_device,
        mesh=mesh,
        in_specs=(
            P(None, ("groups", "section"), None),
            P(),
            P(None, "tp"),
            P(None, "tp"),
            P("tp", None),
            P(("groups", "section"), "tp", None),
            P(("groups", "section"), None, "tp"),
            P("groups", None, "section", "tp"),
            P("groups"),
            P("groups"),
            P("groups"),
            P("groups"),
        ),
        out_specs=P(None, ("groups", "section"), None),
        check_vma=False,
    )
```

```python
import functools
import math

import jax
import jax.numpy as jnp
from jax import lax
from jax.experimental import pallas as pl
from jax.experimental.pallas import tpu as pltpu
from jax.sharding import PartitionSpec as P

QUERY_HEADS = 64
KVH = 8
HEAD_DIM = 128
PER_KV = QUERY_HEADS // KVH

EPSILON = 1e-05
ROPE_BASE = 500000.0
ADAPTER_ALPHA = 16.0
NEGATIVE = -1e30
STAT_ROWS = 8
FRESH_ROWS = 16
AHEAD = 6
CUTS = 4
F32 = jnp.float32
BF16 = jnp.bfloat16
VMEM = pl.BlockSpec(memory_space=pltpu.VMEM)
SMEM = pl.BlockSpec(memory_space=pltpu.SMEM)
IN_HBM = pl.BlockSpec(memory_space=pltpu.HBM)
ANYWHERE = pl.BlockSpec(memory_space=pl.ANY)
QUICK = pl.CostEstimate(flops=1, bytes_accessed=1, transcendentals=0)


def in_hbm(value):
    return pltpu.with_memory_space_constraint(value, pltpu.HBM)


def in_vmem(*values):
    return [pltpu.with_memory_space_constraint(value, pltpu.VMEM) for value in values]


def params(mebibytes):
    return pltpu.CompilerParams(vmem_limit_bytes=mebibytes * 1024 * 1024)


def swap(value, axis, bit):
    size = lax.axis_size(axis)
    pairs = [(i, i ^ bit) for i in range(size)]
    return jax.tree.map(lambda a: lax.ppermute(a, axis, pairs), value)


def tables(slots, section_tokens, adapters, here, prompt_slot, prompt_length, slot_adapter, ranks, frequency, *outs):
    owners, limits, pick, scale, cosine, sine = outs
    section = here[0]
    requests = owners.shape[0]
    shape = pick.shape
    row = lax.broadcasted_iota(jnp.int32, shape, 0)
    lane = lax.broadcasted_iota(jnp.int32, shape, 1)

    def place(slot):
        return (lax.div(slot, slots) ^ section) * slots + lax.rem(slot, slots)

    lengths = jnp.zeros(shape, jnp.int32)
    adapter = jnp.zeros(shape, jnp.int32)
    rank = jnp.zeros(shape, jnp.int32)
    for i in range(requests):
        at, length = place(prompt_slot[i]), prompt_length[i]
        owners[at] = i
        limits[at] = jnp.clip(length - section * section_tokens, 0, section_tokens)
        lengths = jnp.where(row == at, length, lengths)
        at, chosen = place(i), slot_adapter[i]
        adapter = jnp.where(row == at, chosen, adapter)
        rank = jnp.where(row == at, ranks[chosen], rank)
    held = jnp.where(lane < adapters, section * adapters + lane, (section ^ 1) * adapters + lane - adapters)
    pick[...] = jnp.where((lane < 2 * adapters) & (adapter == held), 1.0, 0.0)
    rank_f32 = rank.astype(F32)
    scale[...] = jnp.where(lane < rank, ADAPTER_ALPHA / rank_f32, 0.0)
    steps = cosine.shape[0] // requests
    positions = by_row(lengths, steps, slots).astype(F32)
    step = lax.rem(lax.div(lax.broadcasted_iota(jnp.int32, cosine.shape, 0), slots), steps)
    angles = (positions + step.astype(F32)) * frequency[...]
    cosine[...] = jnp.cos(angles)
    low = lax.broadcasted_iota(jnp.int32, cosine.shape, 1) < HEAD_DIM // 2
    sine[...] = jnp.where(low, -jnp.sin(angles), jnp.sin(angles))


def start_kernel(section_tokens, adapters, here, *refs):
    slot_arrays, frequency, refs = refs[:4], refs[4], refs[5:]
    states, gain, normed, piece, *outs, wide, gains, states_in, gain_in, sems = refs[:-4]
    slot_refs = refs[-4:]
    steps, slots, width = states.shape
    copies = [
        pltpu.make_async_copy(gain, gain_in, sems.at[0]),
        pltpu.make_async_copy(states, states_in, sems.at[1]),
    ]
    small = [
        pltpu.make_async_copy(source, target, sems.at[2 + i])
        for i, (source, target) in enumerate(zip(slot_arrays, slot_refs))
    ]
    for copy in small + copies:
        copy.start()
    for copy in small:
        copy.wait()
    tables(slots, section_tokens, adapters, here, *slot_refs, frequency, *outs)
    for copy in copies:
        copy.wait()
    gains[...] = gain_in[...].astype(F32)
    for t in range(steps):
        values = states_in[t].astype(F32)
        inverse = lax.rsqrt(jnp.mean(values * values, axis=-1, keepdims=True) + EPSILON)
        for c in range(width // 128):
            cols = slice(c * 128, (c + 1) * 128)
            wide[t * slots : (t + 1) * slots, cols] = values[:, cols] * inverse * gains[c : c + 1, :]
    normed[...] = wide[...].astype(BF16)
    cols = piece.shape[1]
    piece[...] = wide[:, pl.ds(pl.multiple_of(here[1] * cols, 128), cols)].astype(BF16)


class Stream:
    def __init__(self, here, rights, jobs, held, sems):
        self.items = [
            (j, i) for j, job in enumerate(jobs) for i in range(rights[job[0]].shape[0] // job[3])
        ]
        self.here, self.rights, self.jobs, self.held, self.sems = here, rights, jobs, held, sems
        for n in range(min(AHEAD, len(self.items))):
            self.copy(n).start()

    def copy(self, n):
        j, i = self.items[n]
        which, start, cols, chunk = self.jobs[j]
        first = pl.multiple_of(start(self.here) * 128, 128)
        source = self.rights[which].at[pl.ds(i * chunk, chunk), pl.ds(first, cols)]
        held = self.held[j]
        return pltpu.make_async_copy(source, held.at[i % held.shape[0]], self.sems.at[n])

    def multiply(self, left_rows, outs):
        for n, (j, i) in enumerate(self.items):
            chunk, held = self.jobs[j][3], self.held[j]
            self.copy(n).wait()
            part = jnp.dot(
                left_rows(i * chunk, chunk), held[i % held.shape[0]], preferred_element_type=F32
            )
            total = part if i == 0 else total + part
            if n + AHEAD < len(self.items):
                self.copy(n + AHEAD).start()
            if (i + 1) * chunk == self.rights[self.jobs[j][0]].shape[0]:
                outs[j][...] = total.astype(outs[j].dtype)


def stream_scratch(rights, jobs):
    counts = [rights[which].shape[0] // chunk for which, _, _, chunk in jobs]
    return [
        pltpu.VMEM((min(AHEAD, count), chunk, cols), BF16)
        for count, (_, _, cols, chunk) in zip(counts, jobs)
    ] + [pltpu.SemaphoreType.DMA((sum(counts),))]


def product_kernel(sizes, jobs, here, *refs):
    refs = list(refs)

    def take(count):
        taken = refs[:count]
        del refs[:count]
        return taken

    lefts, rights, sources, _ = [take(size) for size in sizes]
    outs, targets = take(len(jobs)), take(len(sources))
    held, (sems, carry_sems) = take(len(jobs)), refs
    stream = Stream(here, rights, jobs, held, sems)
    carries = [
        pltpu.make_async_copy(source, target, carry_sems.at[i])
        for i, (source, target) in enumerate(zip(sources, targets))
    ]
    for carry in carries:
        carry.start()
    stream.multiply(
        lambda first, count: jnp.concatenate([ref[:, first : first + count] for ref in lefts], axis=0), outs
    )
    for carry in carries:
        carry.wait()


def product(name, here, lefts, rights, jobs, types, carried=(), after=()):
    rows = sum(left.shape[0] for left in lefts)
    sizes = (len(lefts), len(rights), len(carried), len(after))
    return pl.pallas_call(
        functools.partial(product_kernel, sizes, jobs),
        out_shape=tuple(pltpu.VMEM((rows, job[2]), dtype) for job, dtype in zip(jobs, types))
        + tuple(pltpu.VMEM(c.shape, c.dtype) for c in carried),
        in_specs=[SMEM] + [VMEM] * len(lefts) + [IN_HBM] * (len(rights) + len(carried)) + [ANYWHERE] * len(after),
        out_specs=(VMEM,) * (len(types) + len(carried)),
        scratch_shapes=stream_scratch(rights, jobs) + [pltpu.SemaphoreType.DMA((max(1, len(carried)),))],
        compiler_params=params(20),
        cost_estimate=QUICK,
        name=name,
    )(here, *in_vmem(*lefts), *[in_hbm(c) for c in (*rights, *carried)], *after)


def cross_add_kernel(own, across, after, out):
    for p in range(own.shape[0]):
        out[p] = (own[p].astype(F32) + across[p ^ 2].astype(F32)).astype(out.dtype)


def add_kernel(*refs):
    *terms, out = refs
    total = terms[0][...].astype(F32)
    for term in terms[1:]:
        total = total + term[...].astype(F32)
    out[...] = total.astype(out.dtype)


def add(*terms):
    return pl.pallas_call(
        add_kernel,
        out_shape=pltpu.VMEM(terms[0].shape, BF16),
        in_specs=[VMEM] * len(terms),
        out_specs=VMEM,
        compiler_params=params(8),
        cost_estimate=QUICK,
        name="add",
    )(*in_vmem(*terms))


def by_row(table, steps, slots):
    blocks = [table[i : i + slots] for i in range(0, table.shape[0], slots)]
    return jnp.concatenate([block for block in blocks for _ in range(steps)], axis=0)


def down_kernel(steps, slots, here, own, beside, across, beside_across, pick, down, down_beside, kv, *outs):
    states = jnp.concatenate([ref[...] for ref in (own, beside, across, beside_across)], axis=0)
    picks = by_row(pick[...], steps, slots)
    adapters = down.shape[0]
    rows, rank = states.shape[0], down.shape[2]
    total = jnp.zeros((rows, rank), F32)
    for a in range(2 * adapters):
        part = jnp.dot(states, (down, down_beside)[a // adapters][a % adapters], preferred_element_type=F32)
        total = jnp.where(picks[:, a : a + 1] > 0, part, total)
    half = kv.shape[1] // 2
    new_rows = steps * slots
    for bit, out in enumerate(outs):
        out[:rows, :] = total
        if bit == 0:
            continue
        upper = here[1] == (0, 0, 1, 2)[bit]
        for k in range(half // HEAD_DIM):
            low = kv[:new_rows, k * HEAD_DIM : (k + 1) * HEAD_DIM]
            high = kv[:new_rows, half + k * HEAD_DIM : half + (k + 1) * HEAD_DIM]
            out[rows + k * new_rows : rows + (k + 1) * new_rows, :] = jnp.where(upper, high, low)


def query_kernel(steps, slots, count, here, after, *refs):
    parts, refs = refs[:count], refs[count:]
    scale, pick, up, up_beside, cosine, sine, plain_near, plain_far, out = refs
    all_rows = cosine.shape[0]
    rank_sum = parts[0][:all_rows, :]
    for part in parts[1:]:
        rank_sum = rank_sum + part[:all_rows, :]
    scales = by_row(scale[...], steps, slots)
    picks = by_row(pick[...], steps, slots)
    low_rank = jnp.where(scales > 0, rank_sum * scales, 0.0)
    adapters, rank, width = up.shape
    wide = jnp.concatenate(
        [jnp.where(picks[:, a : a + 1] > 0, low_rank, 0.0) for a in range(2 * adapters)], axis=1
    ).astype(BF16)
    depth = adapters * rank
    ups = [ref.reshape(depth, width) for ref in (up, up_beside)]
    half = plain_near.shape[1]
    rows = steps * slots
    shown = jnp.sum(picks, axis=1, keepdims=True) > 0
    first = (here[0] & 1) * half
    step = min(2 * HEAD_DIM, half)
    for c in range(0, half, step):
        block = pl.ds(pl.multiple_of(first + c, 128), step)
        changes = jnp.dot(wide[:, :depth], ups[0][:, block], preferred_element_type=F32)
        changes = changes + jnp.dot(wide[:, depth:], ups[1][:, block], preferred_element_type=F32)
        for h in range(0, step, HEAD_DIM):
            cols = slice(c + h, c + h + HEAD_DIM)
            plain = jnp.concatenate([plain_near[:, cols], plain_far[:, cols]], axis=0)
            query = plain + changes[:, h : h + HEAD_DIM]
            turned = query * cosine[...] + pltpu.roll(query, HEAD_DIM // 2, 1) * sine[...]
            turned = jnp.where(shown, turned, 0.0).astype(BF16)
            for position in range(4):
                out[position, :, cols] = turned[position * rows : (position + 1) * rows]


def fetch_kernel(places, slots, starts, here, owners, cache, after, *refs):
    sections = len(places)
    *refs, held, key_sems, value_sems, up_sem = refs
    carried = len(refs) // 2 - sections
    ups, outs, targets, done = refs[:carried], refs[carried:][: 2 * sections], refs[carried + 2 * sections : -1], refs[-1]
    ring = held.shape[0]
    count = sections * slots
    order = [(p, i) for p in range(sections) for i in range(slots)]

    def part(up, start, target):
        if start is None:
            return up
        return up.at[:, pl.ds(pl.multiple_of(start(here) * 128, 128), target.shape[1])]

    up_copies = [
        pltpu.make_async_copy(part(up, start, target), target, up_sem.at[0])
        for up, start, target in zip(ups, starts, targets)
    ]

    def key_copy(n):
        position, i = order[n]
        source = cache.at[owners[places[position] * slots + i], 0]
        return pltpu.make_async_copy(source, held.at[n % ring], key_sems.at[n % ring])

    def value_copy(n):
        position, i = order[n]
        source = cache.at[owners[places[position] * slots + i], 1]
        return pltpu.make_async_copy(source, outs[sections + position].at[i], value_sems.at[n])

    for n in range(ring):
        key_copy(n).start()
        value_copy(n).start()
    for copy in up_copies:
        copy.start()
    for n in range(count):
        position, i = order[n]
        key_copy(n).wait()
        outs[position][i] = held[n % ring].T
        if n + ring < count:
            key_copy(n + ring).start()
            value_copy(n + ring).start()
    done[...] = jnp.zeros_like(done)
    for copy in up_copies:
        copy.wait()
    for n in range(count):
        value_copy(n).wait()


def hold_kernel(starts, here, source, after, *refs):
    *outs, sems = refs
    cols = outs[0].shape[1]
    copies = []
    for i, out in enumerate(outs):
        first = pl.multiple_of(starts[i](here) * 128, 128)
        copies.append(pltpu.make_async_copy(source.at[:, pl.ds(first, cols)], out, sems.at[i]))
    for copy in copies:
        copy.start()
    for copy in copies:
        copy.wait()


def place_kernel(starts, here, *refs):
    *blocks, out, sems = refs
    copies = []
    for i, block in enumerate(blocks):
        cols = block.shape[1]
        first = pl.multiple_of(starts[i](here) * 128, 128)
        copies.append(pltpu.make_async_copy(block, out.at[:, pl.ds(first, cols)], sems.at[i]))
    for copy in copies:
        copy.start()
    for copy in copies:
        copy.wait()


def attend_kernel(position, steps, slots, kvl, here, limits, after, own, other, keys, values, *refs):
    fresh = position == 0
    if fresh:
        kv, *received, cosine, sine, out, qf, qs, turned, nk, nv = refs
    else:
        out, qf, qs = refs
    half = own.shape[2] // HEAD_DIM
    heads = 2 * half
    per_kv = heads // kvl
    rows = heads * steps
    tokens = values.shape[1]
    root = 1.0 / math.sqrt(HEAD_DIM)
    qs[...] = jnp.zeros_like(qs)
    lower = here[0] & 1 == 0
    for h in range(half):
        cols = slice(h * HEAD_DIM, (h + 1) * HEAD_DIM)
        mine = own[position, :, cols].astype(F32)
        theirs = other[position ^ 1, :, cols].astype(F32)
        qf[h] = jnp.where(lower, mine, theirs)
        qf[half + h] = jnp.where(lower, theirs, mine)
    for i in range(slots):
        for h in range(heads):
            k = h // per_kv
            qs[i, h * steps : (h + 1) * steps, k * HEAD_DIM : (k + 1) * HEAD_DIM] = qf[
                h, pl.ds(i, steps, stride=slots), :
            ]
    if fresh:
        step_of_row = lax.broadcasted_iota(jnp.int32, (rows, FRESH_ROWS), 0) % steps
        fresh_valid = lax.broadcasted_iota(jnp.int32, (rows, FRESH_ROWS), 1) <= step_of_row
        rows_here = steps * slots
        nk[...] = jnp.zeros_like(nk)
        nv[...] = jnp.zeros_like(nv)
        for k in range(kvl):
            cols = slice(k * HEAD_DIM, (k + 1) * HEAD_DIM)
            if received:
                tp, half_kv = here[1], kvl * HEAD_DIM
                first = cosine.shape[0] + k * rows_here
                one, two, three = [ref[first : first + rows_here, :] for ref in received]
                low, high = kv[:rows_here, cols], kv[:rows_here, half_kv + k * HEAD_DIM : half_kv + (k + 1) * HEAD_DIM]
                key = jnp.where(tp == 0, low, jnp.where(tp == 1, one, jnp.where(tp == 2, three, two)))
                value = jnp.where(tp == 0, two, jnp.where(tp == 1, three, jnp.where(tp == 2, one, high)))
            else:
                key, value = kv[:, cols], kv[:, (kvl + k) * HEAD_DIM : (kvl + k + 1) * HEAD_DIM]
            turned[0, k] = key * cosine[:rows_here, :] + pltpu.roll(key, HEAD_DIM // 2, 1) * sine[:rows_here, :]
            turned[1, k] = value
            for i in range(slots):
                nk[i, :steps, cols] = turned[0, k, pl.ds(i, steps, stride=slots), :]
                nv[i, :steps, cols] = turned[1, k, pl.ds(i, steps, stride=slots), :]
    eye = diagonal(rows)
    token = lax.broadcasted_iota(jnp.int32, (rows, tokens), 1)
    for i in range(slots):
        limit = limits[position * slots + i]
        queries = qs[i].astype(BF16)
        scores = jnp.dot(queries, keys[i], preferred_element_type=F32) * root
        valid = token < limit
        scores = jnp.where(valid, scores, NEGATIVE)
        top = jnp.max(scores, axis=1, keepdims=True)
        if fresh:
            new_scores = lax.dot_general(
                queries, nk[i].astype(BF16), (((1,), (1,)), ((), ())), preferred_element_type=F32
            )
            new_scores = jnp.where(fresh_valid, new_scores * root, NEGATIVE)
            top = jnp.maximum(top, jnp.max(new_scores, axis=1, keepdims=True))
        weights = jnp.where(valid, jnp.exp(scores - top), 0.0)
        total = jnp.sum(weights, axis=1, keepdims=True)
        value = jnp.dot(weights.astype(BF16), values[i], preferred_element_type=F32)
        if fresh:
            new_weights = jnp.where(fresh_valid, jnp.exp(new_scores - top), 0.0)
            total = total + jnp.sum(new_weights, axis=1, keepdims=True)
            value = value + jnp.dot(
                new_weights.astype(BF16), nv[i].astype(BF16), preferred_element_type=F32
            )
        for k in range(kvl):
            block = slice(k * per_kv * steps, (k + 1) * per_kv * steps)
            out[i, block, :] = value[block, k * HEAD_DIM : (k + 1) * HEAD_DIM]
        out[i, rows : rows + 1, :rows] = jnp.sum(jnp.where(eye, top, 0.0), axis=0, keepdims=True)
        out[i, rows + 1 : rows + 2, :rows] = jnp.sum(jnp.where(eye, total, 0.0), axis=0, keepdims=True)


def joined(refs, i, rows, eye):
    tops = [ref[i, rows : rows + 1, :rows] for ref in refs]
    top = functools.reduce(jnp.maximum, tops)
    total, weighted = 0.0, 0.0
    for ref, part_top in zip(refs, tops):
        scale = jnp.exp(part_top - top)
        total = total + ref[i, rows + 1 : rows + 2, :rows] * scale
        column = jnp.sum(jnp.where(eye, scale, 0.0), axis=1, keepdims=True)
        weighted = weighted + ref[i, :rows, :] * column
    return weighted, top, total


def diagonal(rows):
    return lax.broadcasted_iota(jnp.int32, (rows, rows), 0) == lax.broadcasted_iota(
        jnp.int32, (rows, rows), 1
    )


def merge_kernel(a, b, out):
    rows = a.shape[1] - STAT_ROWS
    eye = diagonal(rows)
    for i in range(a.shape[0]):
        weighted, top, total = joined((a, b), i, rows, eye)
        out[i, :rows, :] = weighted
        out[i, rows : rows + 1, :rows] = top
        out[i, rows + 1 : rows + 2, :rows] = total


def finish_kernel(steps, a, b, c, out, wide):
    rows = a.shape[1] - STAT_ROWS
    slots = a.shape[0]
    eye = diagonal(rows)
    for i in range(slots):
        weighted, _, total = joined((a, b, c), i, rows, eye)
        weighted = weighted / jnp.sum(jnp.where(eye, total, 0.0), axis=1, keepdims=True)
        for h in range(rows // steps):
            wide[h, pl.ds(i, steps, stride=slots), :] = weighted[h * steps : (h + 1) * steps, :]
    for h in range(rows // steps):
        out[:, h * HEAD_DIM : (h + 1) * HEAD_DIM] = wide[h].astype(BF16)


def far_kernel(jobs, here, left, held_right, right, held_out, *refs):
    count = len(jobs)
    outs, held, sems = refs[:count], refs[count:-1], refs[-1]
    stream = Stream(here, [right], jobs, held, sems)
    held_out[...] = jnp.dot(left[...], held_right[...], preferred_element_type=F32).astype(BF16)
    stream.multiply(lambda first, count: left[:, first : first + count], outs)


def finish_far_kernel(steps, a, b, c, held_right, attended, held_out, wide):
    finish_kernel(steps, a, b, c, attended, wide)
    held_out[...] = jnp.dot(attended[...], held_right[...], preferred_element_type=F32).astype(BF16)


def attend(position, steps, slots, kvl, here, limits, after, own, other, keys, values, *new):
    heads = 2 * own.shape[2] // HEAD_DIM
    rows, columns = heads * steps, values.shape[2]
    scratch = [
        pltpu.VMEM((heads, steps * slots, HEAD_DIM), F32),
        pltpu.VMEM((slots, rows, columns), F32),
    ]
    if new:
        scratch += [
            pltpu.VMEM((2, kvl, steps * slots, HEAD_DIM), F32),
            pltpu.VMEM((slots, FRESH_ROWS, columns), F32),
            pltpu.VMEM((slots, FRESH_ROWS, columns), F32),
        ]
    return pl.pallas_call(
        functools.partial(attend_kernel, position, steps, slots, kvl),
        out_shape=pltpu.VMEM((slots, rows + STAT_ROWS, HEAD_DIM), F32),
        in_specs=[SMEM] * 2 + [ANYWHERE] + [VMEM] * (4 + len(new)),
        out_specs=VMEM,
        scratch_shapes=scratch,
        compiler_params=params(8),
        cost_estimate=QUICK,
        name="attend",
    )(here, limits, after, *in_vmem(own, other, keys, values, *new))


def merge(a, b):
    return pl.pallas_call(
        merge_kernel,
        out_shape=pltpu.VMEM(a.shape, F32),
        in_specs=[VMEM] * 2,
        out_specs=VMEM,
        compiler_params=params(8),
        cost_estimate=QUICK,
        name="merge",
    )(*in_vmem(a, b))


def per_device(
    step_token_states,
    input_norm_gain,
    wq,
    wkv,
    wo,
    adapter_down,
    adapter_up,
    prompt_cache_pool,
    prompt_slot,
    prompt_cache_length,
    slot_adapter,
    adapter_ranks,
):
    sections = lax.axis_size("section")
    tp_width = lax.axis_size("tp")
    here = jnp.stack([lax.axis_index("section"), lax.axis_index("tp")]).astype(jnp.int32)
    steps, slots, model_width = step_token_states.shape
    requests = prompt_slot.shape[0]
    section_tokens = prompt_cache_pool.shape[2]
    cols_dev = prompt_cache_pool.shape[3]
    adapters, slice_cols, rank = adapter_down.shape
    local_heads = QUERY_HEADS // tp_width
    half_cols = local_heads // 2 * HEAD_DIM
    kvl = max(1, local_heads // PER_KV)
    width = kvl * HEAD_DIM
    rows = steps * slots
    assert sections == 4

    exponents = jnp.arange(HEAD_DIM // 2, dtype=F32) * (2.0 / HEAD_DIM)
    frequency = ROPE_BASE ** (-exponents)
    frequency = jnp.concatenate([frequency, frequency])[None]
    ints = jax.ShapeDtypeStruct((requests,), jnp.int32)
    normed, piece, owners, limits, pick, scale, cosine, sine = pl.pallas_call(
        functools.partial(start_kernel, section_tokens, adapters),
        out_shape=(pltpu.VMEM((rows, model_width), BF16), pltpu.VMEM((rows, slice_cols), BF16), ints, ints)
        + (pltpu.VMEM((requests, rank), F32),) * 2
        + (pltpu.VMEM((sections * rows, HEAD_DIM), F32),) * 2,
        in_specs=[SMEM] + [IN_HBM] * 4 + [VMEM] + [IN_HBM] * 2,
        out_specs=(VMEM, VMEM, SMEM, SMEM) + (VMEM,) * 4,
        scratch_shapes=[
            pltpu.VMEM((rows, model_width), F32),
            pltpu.VMEM((model_width // 128, 128), F32),
            pltpu.VMEM(step_token_states.shape, BF16),
            pltpu.VMEM((model_width // 128, 128), BF16),
            pltpu.SemaphoreType.DMA((6,)),
            *[
                pltpu.SMEM(array.shape, jnp.int32)
                for array in (prompt_slot, prompt_cache_length, slot_adapter, adapter_ranks)
            ],
        ],
        compiler_params=params(8),
        cost_estimate=QUICK,
        name="start",
    )(
        here,
        *[in_hbm(array) for array in (prompt_slot, prompt_cache_length, slot_adapter, adapter_ranks)],
        frequency,
        in_hbm(step_token_states), in_hbm(input_norm_gain.reshape(model_width // 128, 128)),
    )
    normed_beside = swap(normed, "section", 1)
    piece_across = swap(piece, "section", 2)
    piece_beside = swap(piece, "section", 1)
    late_down, late_up, _ = lax.optimization_barrier((adapter_down, adapter_up, normed_beside))
    down_beside = swap(late_down, "section", 1)
    up_beside = swap(late_up, "section", 1)

    packed = tp_width == 4
    chunk = min(512, model_width // 2)
    jobs = [(0, lambda at: (at[0] & 1) * (half_cols // 128), half_cols, chunk)]
    if packed:
        jobs += [(1, lambda at: 0, wkv.shape[1], 2 * chunk)]
    plain_near, *kv_part, held_down = product(
        "query", here, (normed, normed_beside), (wq, wkv), jobs, [F32] * len(jobs), (adapter_down,)
    )
    kv_part = kv_part[0] if packed else jnp.dot(normed, wkv, preferred_element_type=F32)
    plain_far = swap(plain_near, "section", 2)
    late_across = lax.optimization_barrier((piece_across, plain_near))[0]
    piece_beside_across = swap(late_across, "section", 1)
    payload = pltpu.VMEM((sections * rows + kvl * rows, rank), F32)
    own_part = pltpu.VMEM((sections * rows, rank), F32)
    rank_part, *payloads = pl.pallas_call(
        functools.partial(down_kernel, steps, slots),
        out_shape=(own_part,) + ((payload,) * 3 if packed else ()),
        in_specs=[SMEM] + [VMEM] * 8,
        out_specs=(VMEM,) * (4 if packed else 1),
        compiler_params=params(8),
        cost_estimate=QUICK,
        name="down",
    )(
        here,
        *in_vmem(
            piece, piece_beside, piece_across, piece_beside_across, pick, held_down, down_beside, kv_part
        ),
    )
    if packed:
        received = [swap(payloads[bit], "tp", bit + 1) for bit in (2, 1, 0)][::-1]
        parts = [rank_part, *received[::-1]]
        new = (kv_part, *received)
    else:
        parts = [lax.psum(rank_part, "tp")]
        kv_full = lax.all_gather(kv_part[:rows], "tp", axis=1, tiled=True)
        kv_start = here[1] * local_heads // PER_KV * HEAD_DIM
        new = (
            jnp.concatenate(
                [
                    lax.dynamic_slice_in_dim(kv_full, kv_start, width, 1),
                    lax.dynamic_slice_in_dim(kv_full, KVH * HEAD_DIM + kv_start, width, 1),
                ],
                axis=1,
            ),
        )

    cache = prompt_cache_pool
    if cols_dev < HEAD_DIM:
        share = HEAD_DIM // cols_dev
        groups = [list(range(g, g + share)) for g in range(0, tp_width, share)]
        cache = lax.all_gather(cache, "tp", axis=3, tiled=True, axis_index_groups=groups)
    ring = min(8, slots)

    def fetch(places, after, carried, start=None, shape=None):
        count = len(places)
        out = pl.pallas_call(
            functools.partial(fetch_kernel, places, slots, [start] * len(carried)),
            out_shape=(pltpu.VMEM((slots, width, section_tokens), BF16),) * count
            + (pltpu.VMEM((slots, section_tokens, width), BF16),) * count
            + tuple(pltpu.VMEM(shape or c.shape, c.dtype) for c in carried)
            + (pltpu.VMEM((8, 128), F32),),
            in_specs=[SMEM, SMEM, IN_HBM, ANYWHERE] + [IN_HBM] * len(carried),
            out_specs=(VMEM,) * (2 * count + len(carried) + 1),
            scratch_shapes=[
                pltpu.VMEM((ring, section_tokens, width), BF16),
                pltpu.SemaphoreType.DMA((ring,)),
                pltpu.SemaphoreType.DMA((count * slots,)),
                pltpu.SemaphoreType.DMA((1,)),
            ],
            compiler_params=params(12),
            cost_estimate=QUICK,
            name="fetch",
        )(here, owners, in_hbm(cache), after, *[in_hbm(c) for c in carried])
        return dict(zip(places, zip(out[:count], out[count : 2 * count]))), *out[2 * count :]

    caches, held_up, fetch_done = fetch((3, 2, 1), rank_part, (adapter_up,))

    masked = pl.pallas_call(
        functools.partial(query_kernel, steps, slots, len(parts)),
        out_shape=pltpu.VMEM((sections, rows, half_cols), BF16),
        in_specs=[SMEM, ANYWHERE] + [VMEM] * (len(parts) + 8),
        out_specs=VMEM,
        compiler_params=params(8),
        cost_estimate=QUICK,
        name="queries",
    )(here, fetch_done, *in_vmem(*parts, scale, pick, held_up, up_beside, cosine, sine, plain_near, plain_far))
    masked_across = swap(masked, "section", 2)
    quarter = model_width // tp_width
    depth = wo.shape[0]
    columns = [
        functools.partial(lambda bit, at: (at[1] ^ bit) * (quarter // 128), bit)
        for bit in range(tp_width)
    ]
    if packed:
        more, farthest_wo, fetch_done = fetch((0,), masked, (wo,), columns[-1], (depth, quarter))
    else:
        more, fetch_done = fetch((0,), masked, ())
    caches.update(more)

    query_own = pl.pallas_call(
        cross_add_kernel,
        out_shape=pltpu.VMEM(masked.shape, BF16),
        in_specs=[VMEM] * 2 + [ANYWHERE],
        out_specs=VMEM,
        compiler_params=params(8),
        cost_estimate=QUICK,
        name="sum_queries",
    )(*in_vmem(masked, masked_across), fetch_done)
    query_beside = swap(query_own, "section", 1)

    def attend_to(position, after, *new):
        return attend(
            position, steps, slots, kvl, here, limits, after, query_own, query_beside, *caches[position], *new
        )

    part_beside_across = attend_to(3, query_beside)
    part_across = attend_to(2, part_beside_across)
    across = merge(part_across, swap(part_beside_across, "section", 1))
    far = swap(across, "section", 2)
    part_beside = attend_to(1, across)
    part_own = attend_to(0, part_beside, *new, cosine, sine)
    final = in_vmem(part_own, swap(part_beside, "section", 1), far)
    attended_shape = pltpu.VMEM((rows, local_heads * HEAD_DIM), BF16)
    wide_scratch = pltpu.VMEM((local_heads, rows, HEAD_DIM), F32)
    if packed:
        held_wo = pl.pallas_call(
            functools.partial(hold_kernel, columns[-2:-1]),
            out_shape=(pltpu.VMEM((depth, quarter), BF16),),
            in_specs=[SMEM, IN_HBM, ANYWHERE],
            out_specs=(VMEM,),
            scratch_shapes=[pltpu.SemaphoreType.DMA((1,))],
            compiler_params=params(8),
            cost_estimate=QUICK,
            name="hold",
        )(here, in_hbm(wo), part_own)[0]
        block = pltpu.VMEM((rows, quarter), BF16)
        attended, farthest = pl.pallas_call(
            functools.partial(finish_far_kernel, steps),
            out_shape=(attended_shape, block),
            in_specs=[VMEM] * 4,
            out_specs=(VMEM,) * 2,
            scratch_shapes=[wide_scratch],
            compiler_params=params(8),
            cost_estimate=QUICK,
            name="finish",
        )(*final, *in_vmem(farthest_wo))
        farthest = swap(farthest, "tp", tp_width - 1)
        jobs = [(0, columns[1], quarter, depth // CUTS)]
        sent = pl.pallas_call(
            functools.partial(far_kernel, jobs),
            out_shape=(block, block),
            in_specs=[SMEM] + [VMEM] * 2 + [IN_HBM],
            out_specs=(VMEM,) * 2,
            scratch_shapes=stream_scratch([wo], jobs),
            compiler_params=params(16),
            cost_estimate=QUICK,
            name="far_output",
        )(here, *in_vmem(attended, held_wo), in_hbm(wo))
        received = [swap(block, "tp", bit) for block, bit in zip(sent, range(tp_width - 2, 0, -1))]
        jobs = [(0, columns[0], quarter, depth // CUTS)]
        (total,) = product(
            "own_output", here, (attended,), (wo,), jobs, [F32], after=(*sent[:1], farthest)
        )
        total = add(total, farthest, *received)
        blocks = [total] + [swap(total, "tp", bit) for bit in range(1, tp_width)]
        result = pl.pallas_call(
            functools.partial(place_kernel, columns),
            out_shape=jax.ShapeDtypeStruct((rows, model_width), BF16),
            in_specs=[SMEM] + [VMEM] * tp_width,
            out_specs=IN_HBM,
            scratch_shapes=[pltpu.SemaphoreType.DMA((tp_width,))],
            compiler_params=params(8),
            cost_estimate=QUICK,
            name="place",
        )(here, *in_vmem(*blocks))
    else:
        attended = pl.pallas_call(
            functools.partial(finish_kernel, steps),
            out_shape=attended_shape,
            in_specs=[VMEM] * 3,
            out_specs=VMEM,
            scratch_shapes=[wide_scratch],
            compiler_params=params(8),
            cost_estimate=QUICK,
            name="finish",
        )(*final)
        partial_out = jnp.dot(attended, wo, preferred_element_type=F32).astype(BF16)
        result = lax.psum(partial_out, "tp")
    return result.reshape(steps, slots, model_width)


def solution(mesh):
    return jax.shard_map(
        per_device,
        mesh=mesh,
        in_specs=(
            P(None, ("groups", "section"), None),
            P(),
            P(None, "tp"),
            P(None, "tp"),
            P("tp", None),
            P(("groups", "section"), "tp", None),
            P(("groups", "section"), None, "tp"),
            P("groups", None, "section", "tp"),
            P("groups"),
            P("groups"),
            P("groups"),
            P("groups"),
        ),
        out_specs=P(None, ("groups", "section"), None),
        check_vma=False,
    )
```

```python
import functools
import math

import jax
import jax.numpy as jnp
from jax import lax
from jax.experimental import pallas as pl
from jax.experimental.pallas import tpu as pltpu
from jax.sharding import PartitionSpec as P

QUERY_HEADS = 64
KVH = 8
HEAD_DIM = 128
PER_KV = QUERY_HEADS // KVH

EPSILON = 1e-05
ROPE_BASE = 500000.0
ADAPTER_ALPHA = 16.0
NEGATIVE = -1e30
STAT_ROWS = 8
FRESH_ROWS = 16
AHEAD = 6
CUTS = 4
F32 = jnp.float32
BF16 = jnp.bfloat16
VMEM = pl.BlockSpec(memory_space=pltpu.VMEM)
SMEM = pl.BlockSpec(memory_space=pltpu.SMEM)
IN_HBM = pl.BlockSpec(memory_space=pltpu.HBM)
ANYWHERE = pl.BlockSpec(memory_space=pl.ANY)
QUICK = pl.CostEstimate(flops=1, bytes_accessed=1, transcendentals=0)


def in_hbm(value):
    return pltpu.with_memory_space_constraint(value, pltpu.HBM)


def in_vmem(*values):
    return [pltpu.with_memory_space_constraint(value, pltpu.VMEM) for value in values]


def params(mebibytes):
    return pltpu.CompilerParams(vmem_limit_bytes=mebibytes * 1024 * 1024)


def swap(value, axis, bit):
    size = lax.axis_size(axis)
    pairs = [(i, i ^ bit) for i in range(size)]
    return jax.tree.map(lambda a: lax.ppermute(a, axis, pairs), value)


def tables(slots, section_tokens, adapters, here, prompt_slot, prompt_length, slot_adapter, ranks, frequency, *outs):
    owners, limits, pick, scale, cosine, sine = outs
    section = here[0]
    requests = owners.shape[0]
    shape = pick.shape
    row = lax.broadcasted_iota(jnp.int32, shape, 0)
    lane = lax.broadcasted_iota(jnp.int32, shape, 1)

    def place(slot):
        return (lax.div(slot, slots) ^ section) * slots + lax.rem(slot, slots)

    lengths = jnp.zeros(shape, jnp.int32)
    adapter = jnp.zeros(shape, jnp.int32)
    rank = jnp.zeros(shape, jnp.int32)
    for i in range(requests):
        at, length = place(prompt_slot[i]), prompt_length[i]
        owners[at] = i
        limits[at] = jnp.clip(length - section * section_tokens, 0, section_tokens)
        lengths = jnp.where(row == at, length, lengths)
        at, chosen = place(i), slot_adapter[i]
        adapter = jnp.where(row == at, chosen, adapter)
        rank = jnp.where(row == at, ranks[chosen], rank)
    held = jnp.where(lane < adapters, section * adapters + lane, (section ^ 1) * adapters + lane - adapters)
    pick[...] = jnp.where((lane < 2 * adapters) & (adapter == held), 1.0, 0.0)
    rank_f32 = rank.astype(F32)
    scale[...] = jnp.where(lane < rank, ADAPTER_ALPHA / rank_f32, 0.0)
    steps = cosine.shape[0] // requests
    positions = by_row(lengths, steps, slots).astype(F32)
    step = lax.rem(lax.div(lax.broadcasted_iota(jnp.int32, cosine.shape, 0), slots), steps)
    angles = (positions + step.astype(F32)) * frequency[...]
    cosine[...] = jnp.cos(angles)
    low = lax.broadcasted_iota(jnp.int32, cosine.shape, 1) < HEAD_DIM // 2
    sine[...] = jnp.where(low, -jnp.sin(angles), jnp.sin(angles))


def start_kernel(section_tokens, adapters, here, *refs):
    slot_arrays, frequency, refs = refs[:4], refs[4], refs[5:]
    states, gain, normed, piece, *outs, wide, gains, states_in, gain_in, sems = refs[:-4]
    slot_refs = refs[-4:]
    steps, slots, width = states.shape
    copies = [
        pltpu.make_async_copy(gain, gain_in, sems.at[0]),
        pltpu.make_async_copy(states, states_in, sems.at[1]),
    ]
    small = [
        pltpu.make_async_copy(source, target, sems.at[2 + i])
        for i, (source, target) in enumerate(zip(slot_arrays, slot_refs))
    ]
    for copy in small + copies:
        copy.start()
    for copy in small:
        copy.wait()
    tables(slots, section_tokens, adapters, here, *slot_refs, frequency, *outs)
    for copy in copies:
        copy.wait()
    gains[...] = gain_in[...].astype(F32)
    for t in range(steps):
        values = states_in[t].astype(F32)
        inverse = lax.rsqrt(jnp.mean(values * values, axis=-1, keepdims=True) + EPSILON)
        for c in range(width // 128):
            cols = slice(c * 128, (c + 1) * 128)
            wide[t * slots : (t + 1) * slots, cols] = values[:, cols] * inverse * gains[c : c + 1, :]
    normed[...] = wide[...].astype(BF16)
    cols = piece.shape[1]
    piece[...] = wide[:, pl.ds(pl.multiple_of(here[1] * cols, 128), cols)].astype(BF16)


class Stream:
    def __init__(self, here, rights, jobs, held, sems):
        self.items = [
            (j, i) for j, job in enumerate(jobs) for i in range(rights[job[0]].shape[0] // job[3])
        ]
        self.here, self.rights, self.jobs, self.held, self.sems = here, rights, jobs, held, sems
        for n in range(min(AHEAD, len(self.items))):
            self.copy(n).start()

    def copy(self, n):
        j, i = self.items[n]
        which, start, cols, chunk = self.jobs[j]
        first = pl.multiple_of(start(self.here) * 128, 128)
        source = self.rights[which].at[pl.ds(i * chunk, chunk), pl.ds(first, cols)]
        held = self.held[j]
        return pltpu.make_async_copy(source, held.at[i % held.shape[0]], self.sems.at[n])

    def multiply(self, left_rows, outs):
        for n, (j, i) in enumerate(self.items):
            chunk, held = self.jobs[j][3], self.held[j]
            self.copy(n).wait()
            part = jnp.dot(
                left_rows(i * chunk, chunk), held[i % held.shape[0]], preferred_element_type=F32
            )
            total = part if i == 0 else total + part
            if n + AHEAD < len(self.items):
                self.copy(n + AHEAD).start()
            if (i + 1) * chunk == self.rights[self.jobs[j][0]].shape[0]:
                outs[j][...] = total.astype(outs[j].dtype)


def stream_scratch(rights, jobs):
    counts = [rights[which].shape[0] // chunk for which, _, _, chunk in jobs]
    return [
        pltpu.VMEM((min(AHEAD, count), chunk, cols), BF16)
        for count, (_, _, cols, chunk) in zip(counts, jobs)
    ] + [pltpu.SemaphoreType.DMA((sum(counts),))]


def product_kernel(sizes, jobs, here, *refs):
    refs = list(refs)

    def take(count):
        taken = refs[:count]
        del refs[:count]
        return taken

    lefts, rights, sources, _ = [take(size) for size in sizes]
    outs, targets = take(len(jobs)), take(len(sources))
    held, (sems, carry_sems) = take(len(jobs)), refs
    stream = Stream(here, rights, jobs, held, sems)
    carries = [
        pltpu.make_async_copy(source, target, carry_sems.at[i])
        for i, (source, target) in enumerate(zip(sources, targets))
    ]
    for carry in carries:
        carry.start()
    stream.multiply(
        lambda first, count: jnp.concatenate([ref[:, first : first + count] for ref in lefts], axis=0), outs
    )
    for carry in carries:
        carry.wait()


def product(name, here, lefts, rights, jobs, types, carried=(), after=()):
    rows = sum(left.shape[0] for left in lefts)
    sizes = (len(lefts), len(rights), len(carried), len(after))
    return pl.pallas_call(
        functools.partial(product_kernel, sizes, jobs),
        out_shape=tuple(pltpu.VMEM((rows, job[2]), dtype) for job, dtype in zip(jobs, types))
        + tuple(pltpu.VMEM(c.shape, c.dtype) for c in carried),
        in_specs=[SMEM] + [VMEM] * len(lefts) + [IN_HBM] * (len(rights) + len(carried)) + [ANYWHERE] * len(after),
        out_specs=(VMEM,) * (len(types) + len(carried)),
        scratch_shapes=stream_scratch(rights, jobs) + [pltpu.SemaphoreType.DMA((max(1, len(carried)),))],
        compiler_params=params(20),
        cost_estimate=QUICK,
        name=name,
    )(here, *in_vmem(*lefts), *[in_hbm(c) for c in (*rights, *carried)], *after)


def cross_add_kernel(own, across, after, out):
    for p in range(own.shape[0]):
        out[p] = (own[p].astype(F32) + across[p ^ 2].astype(F32)).astype(out.dtype)


def add_kernel(*refs):
    *terms, out = refs
    total = terms[0][...].astype(F32)
    for term in terms[1:]:
        total = total + term[...].astype(F32)
    out[...] = total.astype(out.dtype)


def add(*terms, dtype=BF16):
    return pl.pallas_call(
        add_kernel,
        out_shape=pltpu.VMEM(terms[0].shape, dtype),
        in_specs=[VMEM] * len(terms),
        out_specs=VMEM,
        compiler_params=params(8),
        cost_estimate=QUICK,
        name="add",
    )(*in_vmem(*terms))


def by_row(table, steps, slots):
    blocks = [table[i : i + slots] for i in range(0, table.shape[0], slots)]
    return jnp.concatenate([block for block in blocks for _ in range(steps)], axis=0)


def down_kernel(steps, slots, here, own, beside, across, beside_across, pick, down, down_beside, kv, *outs):
    states = jnp.concatenate([ref[...] for ref in (own, beside, across, beside_across)], axis=0)
    picks = by_row(pick[...], steps, slots)
    adapters = down.shape[0]
    rows, rank = states.shape[0], down.shape[2]
    total = jnp.zeros((rows, rank), F32)
    for a in range(2 * adapters):
        part = jnp.dot(states, (down, down_beside)[a // adapters][a % adapters], preferred_element_type=F32)
        total = jnp.where(picks[:, a : a + 1] > 0, part, total)
    half = kv.shape[1] // 2
    new_rows = steps * slots
    for bit, out in enumerate(outs):
        out[:rows, :] = total
        if bit == 0:
            continue
        upper = here[1] == (0, 0, 1, 2)[bit]
        for k in range(half // HEAD_DIM):
            low = kv[:new_rows, k * HEAD_DIM : (k + 1) * HEAD_DIM]
            high = kv[:new_rows, half + k * HEAD_DIM : half + (k + 1) * HEAD_DIM]
            out[rows + k * new_rows : rows + (k + 1) * new_rows, :] = jnp.where(upper, high, low)


def query_kernel(steps, slots, count, here, after, *refs):
    parts, refs = refs[:count], refs[count:]
    scale, pick, up, up_beside, cosine, sine, plain_near, plain_far, out = refs
    all_rows = cosine.shape[0]
    rank_sum = parts[0][:all_rows, :]
    for part in parts[1:]:
        rank_sum = rank_sum + part[:all_rows, :]
    scales = by_row(scale[...], steps, slots)
    picks = by_row(pick[...], steps, slots)
    low_rank = jnp.where(scales > 0, rank_sum * scales, 0.0)
    adapters, rank, width = up.shape
    wide = jnp.concatenate(
        [jnp.where(picks[:, a : a + 1] > 0, low_rank, 0.0) for a in range(2 * adapters)], axis=1
    ).astype(BF16)
    depth = adapters * rank
    ups = [ref.reshape(depth, width) for ref in (up, up_beside)]
    half = plain_near.shape[1]
    rows = steps * slots
    shown = jnp.sum(picks, axis=1, keepdims=True) > 0
    first = (here[0] & 1) * half
    step = min(2 * HEAD_DIM, half)
    for c in range(0, half, step):
        block = pl.ds(pl.multiple_of(first + c, 128), step)
        changes = jnp.dot(wide[:, :depth], ups[0][:, block], preferred_element_type=F32)
        changes = changes + jnp.dot(wide[:, depth:], ups[1][:, block], preferred_element_type=F32)
        for h in range(0, step, HEAD_DIM):
            cols = slice(c + h, c + h + HEAD_DIM)
            plain = jnp.concatenate([plain_near[:, cols], plain_far[:, cols]], axis=0)
            query = plain + changes[:, h : h + HEAD_DIM]
            turned = query * cosine[...] + pltpu.roll(query, HEAD_DIM // 2, 1) * sine[...]
            turned = jnp.where(shown, turned, 0.0).astype(BF16)
            for position in range(4):
                out[position, :, cols] = turned[position * rows : (position + 1) * rows]


def fetch_kernel(places, slots, starts, here, owners, cache, after, *refs):
    sections = len(places)
    *refs, held, key_sems, value_sems, up_sem = refs
    carried = len(refs) // 2 - sections
    ups, outs, targets, done = refs[:carried], refs[carried:][: 2 * sections], refs[carried + 2 * sections : -1], refs[-1]
    ring = held.shape[0]
    count = sections * slots
    order = [(p, i) for p in range(sections) for i in range(slots)]

    def part(up, start, target):
        if start is None:
            return up
        return up.at[:, pl.ds(pl.multiple_of(start(here) * 128, 128), target.shape[1])]

    up_copies = [
        pltpu.make_async_copy(part(up, start, target), target, up_sem.at[0])
        for up, start, target in zip(ups, starts, targets)
    ]

    def key_copy(n):
        position, i = order[n]
        source = cache.at[owners[places[position] * slots + i], 0]
        return pltpu.make_async_copy(source, held.at[n % ring], key_sems.at[n % ring])

    def value_copy(n):
        position, i = order[n]
        source = cache.at[owners[places[position] * slots + i], 1]
        return pltpu.make_async_copy(source, outs[sections + position].at[i], value_sems.at[n])

    for n in range(ring):
        key_copy(n).start()
        value_copy(n).start()
    for copy in up_copies:
        copy.start()
    for n in range(count):
        position, i = order[n]
        key_copy(n).wait()
        outs[position][i] = held[n % ring].T
        if n + ring < count:
            key_copy(n + ring).start()
            value_copy(n + ring).start()
    done[...] = jnp.zeros_like(done)
    for copy in up_copies:
        copy.wait()
    for n in range(count):
        value_copy(n).wait()


def attend_and_hold_kernel(starts, operands, attend_body, here, limits, after, right, *refs):
    inputs, (out, *refs) = refs[:operands], refs[operands:]
    held, (*scratch, sems) = refs[: len(starts)], refs[len(starts) :]
    copies = []
    for i, (start, target) in enumerate(zip(starts, held)):
        first = pl.multiple_of(start(here) * 128, 128)
        source = right.at[:, pl.ds(first, target.shape[1])]
        copies.append(pltpu.make_async_copy(source, target, sems.at[i]))
    for copy in copies:
        copy.start()
    attend_body(here, limits, after, *inputs, out, *scratch)
    for copy in copies:
        copy.wait()


def place_kernel(starts, here, *refs):
    blocks, (out, sems) = refs[: len(starts)], refs[-2:]
    copies = []
    for i, (start, block) in enumerate(zip(starts, blocks)):
        first = pl.multiple_of(start(here) * 128, 128)
        copies.append(pltpu.make_async_copy(block, out.at[:, pl.ds(first, block.shape[1])], sems.at[i]))
    for copy in copies:
        copy.start()
    for copy in copies:
        copy.wait()


def attend_kernel(position, steps, slots, kvl, here, limits, after, own, other, keys, values, *refs):
    fresh = position == 0
    if fresh:
        kv, *received, cosine, sine, out, qf, qs, turned, nk, nv = refs
    else:
        out, qf, qs = refs
    half = own.shape[2] // HEAD_DIM
    heads = 2 * half
    per_kv = heads // kvl
    rows = heads * steps
    tokens = values.shape[1]
    root = 1.0 / math.sqrt(HEAD_DIM)
    qs[...] = jnp.zeros_like(qs)
    lower = here[0] & 1 == 0
    for h in range(half):
        cols = slice(h * HEAD_DIM, (h + 1) * HEAD_DIM)
        mine = own[position, :, cols].astype(F32)
        theirs = other[position ^ 1, :, cols].astype(F32)
        qf[h] = jnp.where(lower, mine, theirs)
        qf[half + h] = jnp.where(lower, theirs, mine)
    for i in range(slots):
        for h in range(heads):
            k = h // per_kv
            qs[i, h * steps : (h + 1) * steps, k * HEAD_DIM : (k + 1) * HEAD_DIM] = qf[
                h, pl.ds(i, steps, stride=slots), :
            ]
    if fresh:
        step_of_row = lax.broadcasted_iota(jnp.int32, (rows, FRESH_ROWS), 0) % steps
        fresh_valid = lax.broadcasted_iota(jnp.int32, (rows, FRESH_ROWS), 1) <= step_of_row
        rows_here = steps * slots
        nk[...] = jnp.zeros_like(nk)
        nv[...] = jnp.zeros_like(nv)
        for k in range(kvl):
            cols = slice(k * HEAD_DIM, (k + 1) * HEAD_DIM)
            if received:
                tp, half_kv = here[1], kvl * HEAD_DIM
                first = cosine.shape[0] + k * rows_here
                one, two, three = [ref[first : first + rows_here, :] for ref in received]
                low, high = kv[:rows_here, cols], kv[:rows_here, half_kv + k * HEAD_DIM : half_kv + (k + 1) * HEAD_DIM]
                key = jnp.where(tp == 0, low, jnp.where(tp == 1, one, jnp.where(tp == 2, three, two)))
                value = jnp.where(tp == 0, two, jnp.where(tp == 1, three, jnp.where(tp == 2, one, high)))
            else:
                key, value = kv[:, cols], kv[:, (kvl + k) * HEAD_DIM : (kvl + k + 1) * HEAD_DIM]
            turned[0, k] = key * cosine[:rows_here, :] + pltpu.roll(key, HEAD_DIM // 2, 1) * sine[:rows_here, :]
            turned[1, k] = value
            for i in range(slots):
                nk[i, :steps, cols] = turned[0, k, pl.ds(i, steps, stride=slots), :]
                nv[i, :steps, cols] = turned[1, k, pl.ds(i, steps, stride=slots), :]
    eye = diagonal(rows)
    token = lax.broadcasted_iota(jnp.int32, (rows, tokens), 1)
    for i in range(slots):
        limit = limits[position * slots + i]
        queries = qs[i].astype(BF16)
        scores = jnp.dot(queries, keys[i], preferred_element_type=F32) * root
        valid = token < limit
        scores = jnp.where(valid, scores, NEGATIVE)
        top = jnp.max(scores, axis=1, keepdims=True)
        if fresh:
            new_scores = lax.dot_general(
                queries, nk[i].astype(BF16), (((1,), (1,)), ((), ())), preferred_element_type=F32
            )
            new_scores = jnp.where(fresh_valid, new_scores * root, NEGATIVE)
            top = jnp.maximum(top, jnp.max(new_scores, axis=1, keepdims=True))
        weights = jnp.where(valid, jnp.exp(scores - top), 0.0)
        total = jnp.sum(weights, axis=1, keepdims=True)
        value = jnp.dot(weights.astype(BF16), values[i], preferred_element_type=F32)
        if fresh:
            new_weights = jnp.where(fresh_valid, jnp.exp(new_scores - top), 0.0)
            total = total + jnp.sum(new_weights, axis=1, keepdims=True)
            value = value + jnp.dot(
                new_weights.astype(BF16), nv[i].astype(BF16), preferred_element_type=F32
            )
        for k in range(kvl):
            block = slice(k * per_kv * steps, (k + 1) * per_kv * steps)
            out[i, block, :] = value[block, k * HEAD_DIM : (k + 1) * HEAD_DIM]
        out[i, rows : rows + 1, :rows] = jnp.sum(jnp.where(eye, top, 0.0), axis=0, keepdims=True)
        out[i, rows + 1 : rows + 2, :rows] = jnp.sum(jnp.where(eye, total, 0.0), axis=0, keepdims=True)


def joined(refs, i, rows, eye):
    tops = [ref[i, rows : rows + 1, :rows] for ref in refs]
    top = functools.reduce(jnp.maximum, tops)
    total, weighted = 0.0, 0.0
    for ref, part_top in zip(refs, tops):
        scale = jnp.exp(part_top - top)
        total = total + ref[i, rows + 1 : rows + 2, :rows] * scale
        column = jnp.sum(jnp.where(eye, scale, 0.0), axis=1, keepdims=True)
        weighted = weighted + ref[i, :rows, :] * column
    return weighted, top, total


def diagonal(rows):
    return lax.broadcasted_iota(jnp.int32, (rows, rows), 0) == lax.broadcasted_iota(
        jnp.int32, (rows, rows), 1
    )


def merge_kernel(a, b, out):
    rows = a.shape[1] - STAT_ROWS
    eye = diagonal(rows)
    for i in range(a.shape[0]):
        weighted, top, total = joined((a, b), i, rows, eye)
        out[i, :rows, :] = weighted
        out[i, rows : rows + 1, :rows] = top
        out[i, rows + 1 : rows + 2, :rows] = total


def finish_kernel(steps, a, b, c, out, wide):
    rows = a.shape[1] - STAT_ROWS
    slots = a.shape[0]
    eye = diagonal(rows)
    for i in range(slots):
        weighted, _, total = joined((a, b, c), i, rows, eye)
        weighted = weighted / jnp.sum(jnp.where(eye, total, 0.0), axis=1, keepdims=True)
        for h in range(rows // steps):
            wide[h, pl.ds(i, steps, stride=slots), :] = weighted[h * steps : (h + 1) * steps, :]
    for h in range(rows // steps):
        out[:, h * HEAD_DIM : (h + 1) * HEAD_DIM] = wide[h].astype(BF16)


def far_kernel(left, *refs):
    half = len(refs) // 2
    for right, out in zip(refs[:half], refs[half:]):
        out[...] = jnp.dot(left[...], right[...], preferred_element_type=F32).astype(out.dtype)


def finish_far_kernel(steps, a, b, c, held_right, attended, held_out, wide):
    finish_kernel(steps, a, b, c, attended, wide)
    held_out[...] = jnp.dot(attended[...], held_right[...], preferred_element_type=F32).astype(BF16)


def attend(position, steps, slots, kvl, here, limits, after, operands, right=None, starts=(), cols=0):
    heads = 2 * operands[0].shape[2] // HEAD_DIM
    rows, columns = heads * steps, operands[3].shape[2]
    scratch = [
        pltpu.VMEM((heads, steps * slots, HEAD_DIM), F32),
        pltpu.VMEM((slots, rows, columns), F32),
    ]
    if position == 0:
        scratch += [
            pltpu.VMEM((2, kvl, steps * slots, HEAD_DIM), F32),
            pltpu.VMEM((slots, FRESH_ROWS, columns), F32),
            pltpu.VMEM((slots, FRESH_ROWS, columns), F32),
        ]
    body = functools.partial(attend_kernel, position, steps, slots, kvl)
    out = pltpu.VMEM((slots, rows + STAT_ROWS, HEAD_DIM), F32)
    if not starts:
        return pl.pallas_call(
            body,
            out_shape=out,
            in_specs=[SMEM] * 2 + [ANYWHERE] + [VMEM] * len(operands),
            out_specs=VMEM,
            scratch_shapes=scratch,
            compiler_params=params(8),
            cost_estimate=QUICK,
            name="attend",
        )(here, limits, after, *in_vmem(*operands))
    block = pltpu.VMEM((right.shape[0], cols), right.dtype)
    return pl.pallas_call(
        functools.partial(attend_and_hold_kernel, starts, len(operands), body),
        out_shape=(out,) + (block,) * len(starts),
        in_specs=[SMEM] * 2 + [ANYWHERE, IN_HBM] + [VMEM] * len(operands),
        out_specs=(VMEM,) * (1 + len(starts)),
        scratch_shapes=scratch + [pltpu.SemaphoreType.DMA((len(starts),))],
        compiler_params=params(8),
        cost_estimate=QUICK,
        name="attend_hold",
    )(here, limits, after, in_hbm(right), *in_vmem(*operands))


def merge(a, b):
    return pl.pallas_call(
        merge_kernel,
        out_shape=pltpu.VMEM(a.shape, F32),
        in_specs=[VMEM] * 2,
        out_specs=VMEM,
        compiler_params=params(8),
        cost_estimate=QUICK,
        name="merge",
    )(*in_vmem(a, b))


def per_device(
    step_token_states,
    input_norm_gain,
    wq,
    wkv,
    wo,
    adapter_down,
    adapter_up,
    prompt_cache_pool,
    prompt_slot,
    prompt_cache_length,
    slot_adapter,
    adapter_ranks,
):
    sections = lax.axis_size("section")
    tp_width = lax.axis_size("tp")
    here = jnp.stack([lax.axis_index("section"), lax.axis_index("tp")]).astype(jnp.int32)
    steps, slots, model_width = step_token_states.shape
    requests = prompt_slot.shape[0]
    section_tokens = prompt_cache_pool.shape[2]
    cols_dev = prompt_cache_pool.shape[3]
    adapters, slice_cols, rank = adapter_down.shape
    local_heads = QUERY_HEADS // tp_width
    half_cols = local_heads // 2 * HEAD_DIM
    kvl = max(1, local_heads // PER_KV)
    width = kvl * HEAD_DIM
    rows = steps * slots
    assert sections == 4

    exponents = jnp.arange(HEAD_DIM // 2, dtype=F32) * (2.0 / HEAD_DIM)
    frequency = ROPE_BASE ** (-exponents)
    frequency = jnp.concatenate([frequency, frequency])[None]
    ints = jax.ShapeDtypeStruct((requests,), jnp.int32)
    normed, piece, owners, limits, pick, scale, cosine, sine = pl.pallas_call(
        functools.partial(start_kernel, section_tokens, adapters),
        out_shape=(pltpu.VMEM((rows, model_width), BF16), pltpu.VMEM((rows, slice_cols), BF16), ints, ints)
        + (pltpu.VMEM((requests, rank), F32),) * 2
        + (pltpu.VMEM((sections * rows, HEAD_DIM), F32),) * 2,
        in_specs=[SMEM] + [IN_HBM] * 4 + [VMEM] + [IN_HBM] * 2,
        out_specs=(VMEM, VMEM, SMEM, SMEM) + (VMEM,) * 4,
        scratch_shapes=[
            pltpu.VMEM((rows, model_width), F32),
            pltpu.VMEM((model_width // 128, 128), F32),
            pltpu.VMEM(step_token_states.shape, BF16),
            pltpu.VMEM((model_width // 128, 128), BF16),
            pltpu.SemaphoreType.DMA((6,)),
            *[
                pltpu.SMEM(array.shape, jnp.int32)
                for array in (prompt_slot, prompt_cache_length, slot_adapter, adapter_ranks)
            ],
        ],
        compiler_params=params(8),
        cost_estimate=QUICK,
        name="start",
    )(
        here,
        *[in_hbm(array) for array in (prompt_slot, prompt_cache_length, slot_adapter, adapter_ranks)],
        frequency,
        in_hbm(step_token_states), in_hbm(input_norm_gain.reshape(model_width // 128, 128)),
    )
    normed_beside = swap(normed, "section", 1)
    piece_across = swap(piece, "section", 2)
    piece_beside = swap(piece, "section", 1)
    late_down, late_up, _ = lax.optimization_barrier((adapter_down, adapter_up, normed_beside))
    down_beside = swap(late_down, "section", 1)
    up_beside = swap(late_up, "section", 1)

    packed = tp_width == 4
    chunk = min(512, model_width // 2)
    jobs = [(0, lambda at: (at[0] & 1) * (half_cols // 128), half_cols, chunk)]
    if packed:
        jobs += [(1, lambda at: 0, wkv.shape[1], 2 * chunk)]
    plain_near, *kv_part, held_down = product(
        "query", here, (normed, normed_beside), (wq, wkv), jobs, [F32] * len(jobs), (adapter_down,)
    )
    kv_part = kv_part[0] if packed else jnp.dot(normed, wkv, preferred_element_type=F32)
    plain_far = swap(plain_near, "section", 2)
    late_across = lax.optimization_barrier((piece_across, plain_near))[0]
    piece_beside_across = swap(late_across, "section", 1)
    payload = pltpu.VMEM((sections * rows + kvl * rows, rank), F32)
    own_part = pltpu.VMEM((sections * rows, rank), F32)
    rank_part, *payloads = pl.pallas_call(
        functools.partial(down_kernel, steps, slots),
        out_shape=(own_part,) + ((payload,) * 3 if packed else ()),
        in_specs=[SMEM] + [VMEM] * 8,
        out_specs=(VMEM,) * (4 if packed else 1),
        compiler_params=params(8),
        cost_estimate=QUICK,
        name="down",
    )(
        here,
        *in_vmem(
            piece, piece_beside, piece_across, piece_beside_across, pick, held_down, down_beside, kv_part
        ),
    )
    if packed:
        received = [swap(payloads[bit], "tp", bit + 1) for bit in (2, 1, 0)][::-1]
        parts = [rank_part, *received[::-1]]
        new = (kv_part, *received)
    else:
        parts = [lax.psum(rank_part, "tp")]
        kv_full = lax.all_gather(kv_part[:rows], "tp", axis=1, tiled=True)
        kv_start = here[1] * local_heads // PER_KV * HEAD_DIM
        new = (
            jnp.concatenate(
                [
                    lax.dynamic_slice_in_dim(kv_full, kv_start, width, 1),
                    lax.dynamic_slice_in_dim(kv_full, KVH * HEAD_DIM + kv_start, width, 1),
                ],
                axis=1,
            ),
        )

    cache = prompt_cache_pool
    if cols_dev < HEAD_DIM:
        share = HEAD_DIM // cols_dev
        groups = [list(range(g, g + share)) for g in range(0, tp_width, share)]
        cache = lax.all_gather(cache, "tp", axis=3, tiled=True, axis_index_groups=groups)
    ring = min(8, slots)

    def fetch(places, after, carried, start=None, shape=None):
        count = len(places)
        out = pl.pallas_call(
            functools.partial(fetch_kernel, places, slots, [start] * len(carried)),
            out_shape=(pltpu.VMEM((slots, width, section_tokens), BF16),) * count
            + (pltpu.VMEM((slots, section_tokens, width), BF16),) * count
            + tuple(pltpu.VMEM(shape or c.shape, c.dtype) for c in carried)
            + (pltpu.VMEM((8, 128), F32),),
            in_specs=[SMEM, SMEM, IN_HBM, ANYWHERE] + [IN_HBM] * len(carried),
            out_specs=(VMEM,) * (2 * count + len(carried) + 1),
            scratch_shapes=[
                pltpu.VMEM((ring, section_tokens, width), BF16),
                pltpu.SemaphoreType.DMA((ring,)),
                pltpu.SemaphoreType.DMA((count * slots,)),
                pltpu.SemaphoreType.DMA((1,)),
            ],
            compiler_params=params(12),
            cost_estimate=QUICK,
            name="fetch",
        )(here, owners, in_hbm(cache), after, *[in_hbm(c) for c in carried])
        return dict(zip(places, zip(out[:count], out[count : 2 * count]))), *out[2 * count :]

    caches, held_up, fetch_done = fetch((3, 2, 1), rank_part, (adapter_up,))

    masked = pl.pallas_call(
        functools.partial(query_kernel, steps, slots, len(parts)),
        out_shape=pltpu.VMEM((sections, rows, half_cols), BF16),
        in_specs=[SMEM, ANYWHERE] + [VMEM] * (len(parts) + 8),
        out_specs=VMEM,
        compiler_params=params(8),
        cost_estimate=QUICK,
        name="queries",
    )(here, fetch_done, *in_vmem(*parts, scale, pick, held_up, up_beside, cosine, sine, plain_near, plain_far))
    masked_across = swap(masked, "section", 2)
    quarter = model_width // tp_width
    depth = wo.shape[0]
    columns = [
        functools.partial(lambda bit, at: (at[1] ^ bit) * (quarter // 128), bit)
        for bit in range(tp_width)
    ]
    if packed:
        more, farthest_wo, fetch_done = fetch((0,), masked, (wo,), columns[-1], (depth, quarter))
    else:
        more, fetch_done = fetch((0,), masked, ())
    caches.update(more)

    query_own = pl.pallas_call(
        cross_add_kernel,
        out_shape=pltpu.VMEM(masked.shape, BF16),
        in_specs=[VMEM] * 2 + [ANYWHERE],
        out_specs=VMEM,
        compiler_params=params(8),
        cost_estimate=QUICK,
        name="sum_queries",
    )(*in_vmem(masked, masked_across), fetch_done)
    query_beside = swap(query_own, "section", 1)

    def attend_to(position, after, *new, **hold):
        operands = (query_own, query_beside, *caches[position], *new)
        return attend(position, steps, slots, kvl, here, limits, after, operands, **hold)

    part_beside_across = attend_to(3, query_beside)
    part_beside = attend_to(1, part_beside_across)
    part_across = attend_to(2, part_beside)
    across = merge(part_across, swap(part_beside_across, "section", 1))
    far = swap(across, "section", 2)
    hold = dict(right=wo, starts=columns[1:-1], cols=quarter) if packed else {}
    part_own = attend_to(0, across, *new, cosine, sine, **hold)
    if packed:
        part_own, *held_wo = part_own
    final = in_vmem(part_own, swap(part_beside, "section", 1), far)
    attended_shape = pltpu.VMEM((rows, local_heads * HEAD_DIM), BF16)
    wide_scratch = pltpu.VMEM((local_heads, rows, HEAD_DIM), F32)
    if packed:
        block = pltpu.VMEM((rows, quarter), BF16)
        attended, farthest = pl.pallas_call(
            functools.partial(finish_far_kernel, steps),
            out_shape=(attended_shape, block),
            in_specs=[VMEM] * 4,
            out_specs=(VMEM,) * 2,
            scratch_shapes=[wide_scratch],
            compiler_params=params(8),
            cost_estimate=QUICK,
            name="finish",
        )(*final, *in_vmem(farthest_wo))
        farthest = swap(farthest, "tp", tp_width - 1)
        held_wo = held_wo[::-1]
        sent = pl.pallas_call(
            far_kernel,
            out_shape=(block,) * len(held_wo),
            in_specs=[VMEM] * (1 + len(held_wo)),
            out_specs=(VMEM,) * len(held_wo),
            compiler_params=params(8),
            cost_estimate=QUICK,
            name="far_output",
        )(*in_vmem(attended, *held_wo))
        received = [swap(block, "tp", bit) for block, bit in zip(sent, range(tp_width - 2, 0, -1))]
        jobs = [(0, columns[0], quarter, depth // CUTS)]
        (total,) = product(
            "own_output", here, (attended,), (wo,), jobs, [F32], after=sent[:1]
        )
        total = add(add(total, farthest, dtype=F32), *received)
        blocks = [total] + [swap(total, "tp", bit) for bit in range(1, tp_width)]

        def place(bits, *earlier):
            return pl.pallas_call(
                functools.partial(place_kernel, [columns[bit] for bit in bits]),
                out_shape=jax.ShapeDtypeStruct((rows, model_width), BF16),
                in_specs=[SMEM] + [VMEM] * len(bits) + [IN_HBM] * len(earlier),
                out_specs=IN_HBM,
                scratch_shapes=[pltpu.SemaphoreType.DMA((len(bits),))],
                input_output_aliases={1 + len(bits): 0} if earlier else {},
                compiler_params=params(8),
                cost_estimate=QUICK,
                name="place",
            )(here, *in_vmem(*[blocks[bit] for bit in bits]), *earlier)

        result = place((2, 1), place((0, 3)))
    else:
        attended = pl.pallas_call(
            functools.partial(finish_kernel, steps),
            out_shape=attended_shape,
            in_specs=[VMEM] * 3,
            out_specs=VMEM,
            scratch_shapes=[wide_scratch],
            compiler_params=params(8),
            cost_estimate=QUICK,
            name="finish",
        )(*final)
        partial_out = jnp.dot(attended, wo, preferred_element_type=F32).astype(BF16)
        result = lax.psum(partial_out, "tp")
    return result.reshape(steps, slots, model_width)


def solution(mesh):
    return jax.shard_map(
        per_device,
        mesh=mesh,
        in_specs=(
            P(None, ("groups", "section"), None),
            P(),
            P(None, "tp"),
            P(None, "tp"),
            P("tp", None),
            P(("groups", "section"), "tp", None),
            P(("groups", "section"), None, "tp"),
            P("groups", None, "section", "tp"),
            P("groups"),
            P("groups"),
            P("groups"),
            P("groups"),
        ),
        out_specs=P(None, ("groups", "section"), None),
        check_vma=False,
    )
```

```python
import functools
import math

import jax
import jax.numpy as jnp
from jax import lax
from jax.experimental import pallas as pl
from jax.experimental.pallas import tpu as pltpu
from jax.sharding import PartitionSpec as P

QUERY_HEADS = 64
KVH = 8
HEAD_DIM = 128
PER_KV = QUERY_HEADS // KVH

EPSILON = 1e-05
ROPE_BASE = 500000.0
ADAPTER_ALPHA = 16.0
NEGATIVE = -1e30
STAT_ROWS = 8
FRESH_ROWS = 16
AHEAD = 6
CUTS = 4
F32 = jnp.float32
BF16 = jnp.bfloat16
VMEM = pl.BlockSpec(memory_space=pltpu.VMEM)
SMEM = pl.BlockSpec(memory_space=pltpu.SMEM)
IN_HBM = pl.BlockSpec(memory_space=pltpu.HBM)
ANYWHERE = pl.BlockSpec(memory_space=pl.ANY)
QUICK = pl.CostEstimate(flops=1, bytes_accessed=1, transcendentals=0)


def in_hbm(value):
    return pltpu.with_memory_space_constraint(value, pltpu.HBM)


def in_vmem(*values):
    return [pltpu.with_memory_space_constraint(value, pltpu.VMEM) for value in values]


def params(mebibytes):
    return pltpu.CompilerParams(vmem_limit_bytes=mebibytes * 1024 * 1024)


def swap(value, axis, bit):
    size = lax.axis_size(axis)
    pairs = [(i, i ^ bit) for i in range(size)]
    return jax.tree.map(lambda a: lax.ppermute(a, axis, pairs), value)


def tables(slots, section_tokens, adapters, here, prompt_slot, prompt_length, slot_adapter, ranks, frequency, *outs):
    owners, limits, pick, scale, cosine, sine = outs
    section = here[0]
    requests = owners.shape[0]
    shape = pick.shape
    row = lax.broadcasted_iota(jnp.int32, shape, 0)
    lane = lax.broadcasted_iota(jnp.int32, shape, 1)

    def place(slot):
        return (lax.div(slot, slots) ^ section) * slots + lax.rem(slot, slots)

    lengths = jnp.zeros(shape, jnp.int32)
    adapter = jnp.zeros(shape, jnp.int32)
    rank = jnp.zeros(shape, jnp.int32)
    for i in range(requests):
        at, length = place(prompt_slot[i]), prompt_length[i]
        owners[at] = i
        limits[at] = jnp.clip(length - section * section_tokens, 0, section_tokens)
        lengths = jnp.where(row == at, length, lengths)
        at, chosen = place(i), slot_adapter[i]
        adapter = jnp.where(row == at, chosen, adapter)
        rank = jnp.where(row == at, ranks[chosen], rank)
    held = jnp.where(lane < adapters, section * adapters + lane, (section ^ 1) * adapters + lane - adapters)
    pick[...] = jnp.where((lane < 2 * adapters) & (adapter == held), 1.0, 0.0)
    rank_f32 = rank.astype(F32)
    scale[...] = jnp.where(lane < rank, ADAPTER_ALPHA / rank_f32, 0.0)
    steps = cosine.shape[0] // requests
    positions = by_row(lengths, steps, slots).astype(F32)
    step = lax.rem(lax.div(lax.broadcasted_iota(jnp.int32, cosine.shape, 0), slots), steps)
    angles = (positions + step.astype(F32)) * frequency[...]
    cosine[...] = jnp.cos(angles)
    low = lax.broadcasted_iota(jnp.int32, cosine.shape, 1) < HEAD_DIM // 2
    sine[...] = jnp.where(low, -jnp.sin(angles), jnp.sin(angles))


def start_kernel(section_tokens, adapters, here, *refs):
    slot_arrays, frequency, refs = refs[:4], refs[4], refs[5:]
    states, gain, normed, piece, *outs, wide, gains, states_in, gain_in, sems = refs[:-4]
    slot_refs = refs[-4:]
    steps, slots, width = states.shape
    copies = [
        pltpu.make_async_copy(gain, gain_in, sems.at[0]),
        pltpu.make_async_copy(states, states_in, sems.at[1]),
    ]
    small = [
        pltpu.make_async_copy(source, target, sems.at[2 + i])
        for i, (source, target) in enumerate(zip(slot_arrays, slot_refs))
    ]
    for copy in small + copies:
        copy.start()
    for copy in small:
        copy.wait()
    tables(slots, section_tokens, adapters, here, *slot_refs, frequency, *outs)
    for copy in copies:
        copy.wait()
    gains[...] = gain_in[...].astype(F32)
    for t in range(steps):
        values = states_in[t].astype(F32)
        inverse = lax.rsqrt(jnp.mean(values * values, axis=-1, keepdims=True) + EPSILON)
        for c in range(width // 128):
            cols = slice(c * 128, (c + 1) * 128)
            wide[t * slots : (t + 1) * slots, cols] = values[:, cols] * inverse * gains[c : c + 1, :]
    normed[...] = wide[...].astype(BF16)
    cols = piece.shape[1]
    piece[...] = wide[:, pl.ds(pl.multiple_of(here[1] * cols, 128), cols)].astype(BF16)


class Stream:
    def __init__(self, here, rights, jobs, held, sems):
        self.items = [
            (j, i) for j, job in enumerate(jobs) for i in range(rights[job[0]].shape[0] // job[3])
        ]
        self.here, self.rights, self.jobs, self.held, self.sems = here, rights, jobs, held, sems
        for n in range(min(AHEAD, len(self.items))):
            self.copy(n).start()

    def copy(self, n):
        j, i = self.items[n]
        which, start, cols, chunk = self.jobs[j]
        first = pl.multiple_of(start(self.here) * 128, 128)
        source = self.rights[which].at[pl.ds(i * chunk, chunk), pl.ds(first, cols)]
        held = self.held[j]
        return pltpu.make_async_copy(source, held.at[i % held.shape[0]], self.sems.at[n])

    def multiply(self, left_rows, outs):
        for n, (j, i) in enumerate(self.items):
            chunk, held = self.jobs[j][3], self.held[j]
            self.copy(n).wait()
            part = jnp.dot(
                left_rows(i * chunk, chunk), held[i % held.shape[0]], preferred_element_type=F32
            )
            total = part if i == 0 else total + part
            if n + AHEAD < len(self.items):
                self.copy(n + AHEAD).start()
            if (i + 1) * chunk == self.rights[self.jobs[j][0]].shape[0]:
                outs[j][...] = total.astype(outs[j].dtype)


def stream_scratch(rights, jobs):
    counts = [rights[which].shape[0] // chunk for which, _, _, chunk in jobs]
    return [
        pltpu.VMEM((min(AHEAD, count), chunk, cols), BF16)
        for count, (_, _, cols, chunk) in zip(counts, jobs)
    ] + [pltpu.SemaphoreType.DMA((sum(counts),))]


def product_kernel(sizes, jobs, here, *refs):
    refs = list(refs)

    def take(count):
        taken = refs[:count]
        del refs[:count]
        return taken

    lefts, rights, sources, _ = [take(size) for size in sizes]
    outs, targets = take(len(jobs)), take(len(sources))
    held, (sems, carry_sems) = take(len(jobs)), refs
    stream = Stream(here, rights, jobs, held, sems)
    carries = [
        pltpu.make_async_copy(source, target, carry_sems.at[i])
        for i, (source, target) in enumerate(zip(sources, targets))
    ]
    for carry in carries:
        carry.start()
    stream.multiply(
        lambda first, count: jnp.concatenate([ref[:, first : first + count] for ref in lefts], axis=0), outs
    )
    for carry in carries:
        carry.wait()


def product(name, here, lefts, rights, jobs, types, carried=(), after=()):
    rows = sum(left.shape[0] for left in lefts)
    sizes = (len(lefts), len(rights), len(carried), len(after))
    return pl.pallas_call(
        functools.partial(product_kernel, sizes, jobs),
        out_shape=tuple(pltpu.VMEM((rows, job[2]), dtype) for job, dtype in zip(jobs, types))
        + tuple(pltpu.VMEM(c.shape, c.dtype) for c in carried),
        in_specs=[SMEM] + [VMEM] * len(lefts) + [IN_HBM] * (len(rights) + len(carried)) + [ANYWHERE] * len(after),
        out_specs=(VMEM,) * (len(types) + len(carried)),
        scratch_shapes=stream_scratch(rights, jobs) + [pltpu.SemaphoreType.DMA((max(1, len(carried)),))],
        compiler_params=params(20),
        cost_estimate=QUICK,
        name=name,
    )(here, *in_vmem(*lefts), *[in_hbm(c) for c in (*rights, *carried)], *after)


def cross_add_kernel(own, across, after, out):
    for p in range(own.shape[0]):
        out[p] = (own[p].astype(F32) + across[p ^ 2].astype(F32)).astype(out.dtype)


def add_kernel(*refs):
    *terms, out = refs
    total = terms[0][...].astype(F32)
    for term in terms[1:]:
        total = total + term[...].astype(F32)
    out[...] = total.astype(out.dtype)


def add(*terms, dtype=BF16):
    return pl.pallas_call(
        add_kernel,
        out_shape=pltpu.VMEM(terms[0].shape, dtype),
        in_specs=[VMEM] * len(terms),
        out_specs=VMEM,
        compiler_params=params(8),
        cost_estimate=QUICK,
        name="add",
    )(*in_vmem(*terms))


def by_row(table, steps, slots):
    blocks = [table[i : i + slots] for i in range(0, table.shape[0], slots)]
    return jnp.concatenate([block for block in blocks for _ in range(steps)], axis=0)


def down_kernel(steps, slots, here, own, beside, across, beside_across, pick, down, down_beside, kv, *outs):
    states = jnp.concatenate([ref[...] for ref in (own, beside, across, beside_across)], axis=0)
    picks = by_row(pick[...], steps, slots)
    adapters = down.shape[0]
    rows, rank = states.shape[0], down.shape[2]
    total = jnp.zeros((rows, rank), F32)
    for a in range(2 * adapters):
        part = jnp.dot(states, (down, down_beside)[a // adapters][a % adapters], preferred_element_type=F32)
        total = jnp.where(picks[:, a : a + 1] > 0, part, total)
    half = kv.shape[1] // 2
    new_rows = steps * slots
    for bit, out in enumerate(outs):
        out[:rows, :] = total
        if bit == 0:
            continue
        upper = here[1] == (0, 0, 1, 2)[bit]
        for k in range(half // HEAD_DIM):
            low = kv[:new_rows, k * HEAD_DIM : (k + 1) * HEAD_DIM]
            high = kv[:new_rows, half + k * HEAD_DIM : half + (k + 1) * HEAD_DIM]
            out[rows + k * new_rows : rows + (k + 1) * new_rows, :] = jnp.where(upper, high, low)


def query_kernel(steps, slots, count, here, after, *refs):
    parts, refs = refs[:count], refs[count:]
    scale, pick, up, up_beside, cosine, sine, plain_near, plain_far, out = refs
    all_rows = cosine.shape[0]
    rank_sum = parts[0][:all_rows, :]
    for part in parts[1:]:
        rank_sum = rank_sum + part[:all_rows, :]
    scales = by_row(scale[...], steps, slots)
    picks = by_row(pick[...], steps, slots)
    low_rank = jnp.where(scales > 0, rank_sum * scales, 0.0)
    adapters, rank, width = up.shape
    wide = jnp.concatenate(
        [jnp.where(picks[:, a : a + 1] > 0, low_rank, 0.0) for a in range(2 * adapters)], axis=1
    ).astype(BF16)
    depth = adapters * rank
    ups = [ref.reshape(depth, width) for ref in (up, up_beside)]
    half = plain_near.shape[1]
    rows = steps * slots
    shown = jnp.sum(picks, axis=1, keepdims=True) > 0
    first = (here[0] & 1) * half
    step = min(2 * HEAD_DIM, half)
    for c in range(0, half, step):
        block = pl.ds(pl.multiple_of(first + c, 128), step)
        changes = jnp.dot(wide[:, :depth], ups[0][:, block], preferred_element_type=F32)
        changes = changes + jnp.dot(wide[:, depth:], ups[1][:, block], preferred_element_type=F32)
        for h in range(0, step, HEAD_DIM):
            cols = slice(c + h, c + h + HEAD_DIM)
            plain = jnp.concatenate([plain_near[:, cols], plain_far[:, cols]], axis=0)
            query = plain + changes[:, h : h + HEAD_DIM]
            turned = query * cosine[...] + pltpu.roll(query, HEAD_DIM // 2, 1) * sine[...]
            turned = jnp.where(shown, turned, 0.0).astype(BF16)
            for position in range(4):
                out[position, :, cols] = turned[position * rows : (position + 1) * rows]


def fetch_kernel(places, slots, starts, here, owners, cache, after, *refs):
    sections = len(places)
    *refs, held, key_sems, value_sems, up_sem = refs
    carried = len(refs) // 2 - sections
    ups, outs, targets, done = refs[:carried], refs[carried:][: 2 * sections], refs[carried + 2 * sections : -1], refs[-1]
    ring = held.shape[0]
    count = sections * slots
    order = [(p, i) for p in range(sections) for i in range(slots)]

    def part(up, start, target):
        if start is None:
            return up
        return up.at[:, pl.ds(pl.multiple_of(start(here) * 128, 128), target.shape[1])]

    up_copies = [
        pltpu.make_async_copy(part(up, start, target), target, up_sem.at[0])
        for up, start, target in zip(ups, starts, targets)
    ]

    def key_copy(n):
        position, i = order[n]
        source = cache.at[owners[places[position] * slots + i], 0]
        return pltpu.make_async_copy(source, held.at[n % ring], key_sems.at[n % ring])

    def value_copy(n):
        position, i = order[n]
        source = cache.at[owners[places[position] * slots + i], 1]
        return pltpu.make_async_copy(source, outs[sections + position].at[i], value_sems.at[n])

    for n in range(ring):
        key_copy(n).start()
        value_copy(n).start()
    for copy in up_copies:
        copy.start()
    for n in range(count):
        position, i = order[n]
        key_copy(n).wait()
        outs[position][i] = held[n % ring].T
        if n + ring < count:
            key_copy(n + ring).start()
            value_copy(n + ring).start()
    done[...] = jnp.zeros_like(done)
    for copy in up_copies:
        copy.wait()
    for n in range(count):
        value_copy(n).wait()


def attend_and_hold_kernel(starts, operands, attend_body, here, limits, after, right, *refs):
    inputs, (out, *refs) = refs[:operands], refs[operands:]
    held, (*scratch, sems) = refs[: len(starts)], refs[len(starts) :]
    copies = []
    for i, (start, target) in enumerate(zip(starts, held)):
        first = pl.multiple_of(start(here) * 128, 128)
        source = right.at[:, pl.ds(first, target.shape[1])]
        copies.append(pltpu.make_async_copy(source, target, sems.at[i]))
    for copy in copies:
        copy.start()
    attend_body(here, limits, after, *inputs, out, *scratch)
    for copy in copies:
        copy.wait()


def place_kernel(starts, here, *refs):
    blocks, (out, sems) = refs[: len(starts)], refs[-2:]
    copies = []
    for i, (start, block) in enumerate(zip(starts, blocks)):
        first = pl.multiple_of(start(here) * 128, 128)
        copies.append(pltpu.make_async_copy(block, out.at[:, pl.ds(first, block.shape[1])], sems.at[i]))
    for copy in copies:
        copy.start()
    for copy in copies:
        copy.wait()


def attend_kernel(position, steps, slots, kvl, here, limits, after, own, other, keys, values, *refs):
    fresh = position == 0
    if fresh:
        kv, *received, cosine, sine, out, qf, qs, turned, nk, nv = refs
    else:
        out, qf, qs = refs
    half = own.shape[2] // HEAD_DIM
    heads = 2 * half
    per_kv = heads // kvl
    rows = heads * steps
    tokens = values.shape[1]
    root = 1.0 / math.sqrt(HEAD_DIM)
    qs[...] = jnp.zeros_like(qs)
    lower = here[0] & 1 == 0
    for h in range(half):
        cols = slice(h * HEAD_DIM, (h + 1) * HEAD_DIM)
        mine = own[position, :, cols].astype(F32)
        theirs = other[position ^ 1, :, cols].astype(F32)
        qf[h] = jnp.where(lower, mine, theirs)
        qf[half + h] = jnp.where(lower, theirs, mine)
    for i in range(slots):
        for h in range(heads):
            k = h // per_kv
            qs[i, h * steps : (h + 1) * steps, k * HEAD_DIM : (k + 1) * HEAD_DIM] = qf[
                h, pl.ds(i, steps, stride=slots), :
            ]
    if fresh:
        step_of_row = lax.broadcasted_iota(jnp.int32, (rows, FRESH_ROWS), 0) % steps
        fresh_valid = lax.broadcasted_iota(jnp.int32, (rows, FRESH_ROWS), 1) <= step_of_row
        rows_here = steps * slots
        nk[...] = jnp.zeros_like(nk)
        nv[...] = jnp.zeros_like(nv)
        for k in range(kvl):
            cols = slice(k * HEAD_DIM, (k + 1) * HEAD_DIM)
            if received:
                tp, half_kv = here[1], kvl * HEAD_DIM
                first = cosine.shape[0] + k * rows_here
                one, two, three = [ref[first : first + rows_here, :] for ref in received]
                low, high = kv[:rows_here, cols], kv[:rows_here, half_kv + k * HEAD_DIM : half_kv + (k + 1) * HEAD_DIM]
                key = jnp.where(tp == 0, low, jnp.where(tp == 1, one, jnp.where(tp == 2, three, two)))
                value = jnp.where(tp == 0, two, jnp.where(tp == 1, three, jnp.where(tp == 2, one, high)))
            else:
                key, value = kv[:, cols], kv[:, (kvl + k) * HEAD_DIM : (kvl + k + 1) * HEAD_DIM]
            turned[0, k] = key * cosine[:rows_here, :] + pltpu.roll(key, HEAD_DIM // 2, 1) * sine[:rows_here, :]
            turned[1, k] = value
            for i in range(slots):
                nk[i, :steps, cols] = turned[0, k, pl.ds(i, steps, stride=slots), :]
                nv[i, :steps, cols] = turned[1, k, pl.ds(i, steps, stride=slots), :]
    eye = diagonal(rows)
    token = lax.broadcasted_iota(jnp.int32, (rows, tokens), 1)
    for i in range(slots):
        limit = limits[position * slots + i]
        queries = qs[i].astype(BF16)
        scores = jnp.dot(queries, keys[i], preferred_element_type=F32) * root
        valid = token < limit
        scores = jnp.where(valid, scores, NEGATIVE)
        top = jnp.max(scores, axis=1, keepdims=True)
        if fresh:
            new_scores = lax.dot_general(
                queries, nk[i].astype(BF16), (((1,), (1,)), ((), ())), preferred_element_type=F32
            )
            new_scores = jnp.where(fresh_valid, new_scores * root, NEGATIVE)
            top = jnp.maximum(top, jnp.max(new_scores, axis=1, keepdims=True))
        weights = jnp.where(valid, jnp.exp(scores - top), 0.0)
        total = jnp.sum(weights, axis=1, keepdims=True)
        value = jnp.dot(weights.astype(BF16), values[i], preferred_element_type=F32)
        if fresh:
            new_weights = jnp.where(fresh_valid, jnp.exp(new_scores - top), 0.0)
            total = total + jnp.sum(new_weights, axis=1, keepdims=True)
            value = value + jnp.dot(
                new_weights.astype(BF16), nv[i].astype(BF16), preferred_element_type=F32
            )
        for k in range(kvl):
            block = slice(k * per_kv * steps, (k + 1) * per_kv * steps)
            out[i, block, :] = value[block, k * HEAD_DIM : (k + 1) * HEAD_DIM]
        out[i, rows : rows + 1, :rows] = jnp.sum(jnp.where(eye, top, 0.0), axis=0, keepdims=True)
        out[i, rows + 1 : rows + 2, :rows] = jnp.sum(jnp.where(eye, total, 0.0), axis=0, keepdims=True)


def joined(refs, i, rows, eye):
    tops = [ref[i, rows : rows + 1, :rows] for ref in refs]
    top = functools.reduce(jnp.maximum, tops)
    total, weighted = 0.0, 0.0
    for ref, part_top in zip(refs, tops):
        scale = jnp.exp(part_top - top)
        total = total + ref[i, rows + 1 : rows + 2, :rows] * scale
        column = jnp.sum(jnp.where(eye, scale, 0.0), axis=1, keepdims=True)
        weighted = weighted + ref[i, :rows, :] * column
    return weighted, top, total


def diagonal(rows):
    return lax.broadcasted_iota(jnp.int32, (rows, rows), 0) == lax.broadcasted_iota(
        jnp.int32, (rows, rows), 1
    )


def merge_kernel(a, b, out):
    rows = a.shape[1] - STAT_ROWS
    eye = diagonal(rows)
    for i in range(a.shape[0]):
        weighted, top, total = joined((a, b), i, rows, eye)
        out[i, :rows, :] = weighted
        out[i, rows : rows + 1, :rows] = top
        out[i, rows + 1 : rows + 2, :rows] = total


def finish_kernel(steps, a, b, c, out, wide):
    rows = a.shape[1] - STAT_ROWS
    slots = a.shape[0]
    eye = diagonal(rows)
    for i in range(slots):
        weighted, _, total = joined((a, b, c), i, rows, eye)
        weighted = weighted / jnp.sum(jnp.where(eye, total, 0.0), axis=1, keepdims=True)
        for h in range(rows // steps):
            wide[h, pl.ds(i, steps, stride=slots), :] = weighted[h * steps : (h + 1) * steps, :]
    for h in range(rows // steps):
        out[:, h * HEAD_DIM : (h + 1) * HEAD_DIM] = wide[h].astype(BF16)


def far_kernel(left, *refs):
    half = len(refs) // 2
    for right, out in zip(refs[:half], refs[half:]):
        out[...] = jnp.dot(left[...], right[...], preferred_element_type=F32).astype(out.dtype)


def finish_far_kernel(steps, a, b, c, held_right, attended, held_out, wide):
    finish_kernel(steps, a, b, c, attended, wide)
    held_out[...] = jnp.dot(attended[...], held_right[...], preferred_element_type=F32).astype(BF16)


def attend(position, steps, slots, kvl, here, limits, after, operands, right=None, starts=(), cols=0):
    heads = 2 * operands[0].shape[2] // HEAD_DIM
    rows, columns = heads * steps, operands[3].shape[2]
    scratch = [
        pltpu.VMEM((heads, steps * slots, HEAD_DIM), F32),
        pltpu.VMEM((slots, rows, columns), F32),
    ]
    if position == 0:
        scratch += [
            pltpu.VMEM((2, kvl, steps * slots, HEAD_DIM), F32),
            pltpu.VMEM((slots, FRESH_ROWS, columns), F32),
            pltpu.VMEM((slots, FRESH_ROWS, columns), F32),
        ]
    body = functools.partial(attend_kernel, position, steps, slots, kvl)
    out = pltpu.VMEM((slots, rows + STAT_ROWS, HEAD_DIM), F32)
    if not starts:
        return pl.pallas_call(
            body,
            out_shape=out,
            in_specs=[SMEM] * 2 + [ANYWHERE] + [VMEM] * len(operands),
            out_specs=VMEM,
            scratch_shapes=scratch,
            compiler_params=params(8),
            cost_estimate=QUICK,
            name="attend",
        )(here, limits, after, *in_vmem(*operands))
    block = pltpu.VMEM((right.shape[0], cols), right.dtype)
    return pl.pallas_call(
        functools.partial(attend_and_hold_kernel, starts, len(operands), body),
        out_shape=(out,) + (block,) * len(starts),
        in_specs=[SMEM] * 2 + [ANYWHERE, IN_HBM] + [VMEM] * len(operands),
        out_specs=(VMEM,) * (1 + len(starts)),
        scratch_shapes=scratch + [pltpu.SemaphoreType.DMA((len(starts),))],
        compiler_params=params(8),
        cost_estimate=QUICK,
        name="attend_hold",
    )(here, limits, after, in_hbm(right), *in_vmem(*operands))


def merge(a, b):
    return pl.pallas_call(
        merge_kernel,
        out_shape=pltpu.VMEM(a.shape, F32),
        in_specs=[VMEM] * 2,
        out_specs=VMEM,
        compiler_params=params(8),
        cost_estimate=QUICK,
        name="merge",
    )(*in_vmem(a, b))


def per_device(
    step_token_states,
    input_norm_gain,
    wq,
    wkv,
    wo,
    adapter_down,
    adapter_up,
    prompt_cache_pool,
    prompt_slot,
    prompt_cache_length,
    slot_adapter,
    adapter_ranks,
):
    sections = lax.axis_size("section")
    tp_width = lax.axis_size("tp")
    here = jnp.stack([lax.axis_index("section"), lax.axis_index("tp")]).astype(jnp.int32)
    steps, slots, model_width = step_token_states.shape
    requests = prompt_slot.shape[0]
    section_tokens = prompt_cache_pool.shape[2]
    cols_dev = prompt_cache_pool.shape[3]
    adapters, slice_cols, rank = adapter_down.shape
    local_heads = QUERY_HEADS // tp_width
    half_cols = local_heads // 2 * HEAD_DIM
    kvl = max(1, local_heads // PER_KV)
    width = kvl * HEAD_DIM
    rows = steps * slots
    assert sections == 4

    exponents = jnp.arange(HEAD_DIM // 2, dtype=F32) * (2.0 / HEAD_DIM)
    frequency = ROPE_BASE ** (-exponents)
    frequency = jnp.concatenate([frequency, frequency])[None]
    ints = jax.ShapeDtypeStruct((requests,), jnp.int32)
    normed, piece, owners, limits, pick, scale, cosine, sine = pl.pallas_call(
        functools.partial(start_kernel, section_tokens, adapters),
        out_shape=(pltpu.VMEM((rows, model_width), BF16), pltpu.VMEM((rows, slice_cols), BF16), ints, ints)
        + (pltpu.VMEM((requests, rank), F32),) * 2
        + (pltpu.VMEM((sections * rows, HEAD_DIM), F32),) * 2,
        in_specs=[SMEM] + [IN_HBM] * 4 + [VMEM] + [IN_HBM] * 2,
        out_specs=(VMEM, VMEM, SMEM, SMEM) + (VMEM,) * 4,
        scratch_shapes=[
            pltpu.VMEM((rows, model_width), F32),
            pltpu.VMEM((model_width // 128, 128), F32),
            pltpu.VMEM(step_token_states.shape, BF16),
            pltpu.VMEM((model_width // 128, 128), BF16),
            pltpu.SemaphoreType.DMA((6,)),
            *[
                pltpu.SMEM(array.shape, jnp.int32)
                for array in (prompt_slot, prompt_cache_length, slot_adapter, adapter_ranks)
            ],
        ],
        compiler_params=params(8),
        cost_estimate=QUICK,
        name="start",
    )(
        here,
        *[in_hbm(array) for array in (prompt_slot, prompt_cache_length, slot_adapter, adapter_ranks)],
        frequency,
        in_hbm(step_token_states), in_hbm(input_norm_gain.reshape(model_width // 128, 128)),
    )
    normed_beside = swap(normed, "section", 1)
    piece_across = swap(piece, "section", 2)
    piece_beside = swap(piece, "section", 1)
    late_down, late_up, _ = lax.optimization_barrier((adapter_down, adapter_up, normed_beside))
    down_beside = swap(late_down, "section", 1)
    up_beside = swap(late_up, "section", 1)

    packed = tp_width == 4
    chunk = min(512, model_width // 2)
    jobs = [(0, lambda at: (at[0] & 1) * (half_cols // 128), half_cols, chunk)]
    if packed:
        jobs += [(1, lambda at: 0, wkv.shape[1], 2 * chunk)]
    plain_near, *kv_part = product(
        "query", here, (normed, normed_beside), (wq, wkv), jobs, [F32] * len(jobs)
    )
    kv_part = kv_part[0] if packed else jnp.dot(normed, wkv, preferred_element_type=F32)
    plain_far = swap(plain_near, "section", 2)
    late_across = lax.optimization_barrier((piece_across, plain_near))[0]
    piece_beside_across = swap(late_across, "section", 1)
    payload = pltpu.VMEM((sections * rows + kvl * rows, rank), F32)
    own_part = pltpu.VMEM((sections * rows, rank), F32)
    rank_part, *payloads = pl.pallas_call(
        functools.partial(down_kernel, steps, slots),
        out_shape=(own_part,) + ((payload,) * 3 if packed else ()),
        in_specs=[SMEM] + [VMEM] * 8,
        out_specs=(VMEM,) * (4 if packed else 1),
        compiler_params=params(8),
        cost_estimate=QUICK,
        name="down",
    )(
        here,
        *in_vmem(
            piece, piece_beside, piece_across, piece_beside_across, pick, adapter_down, down_beside, kv_part
        ),
    )
    if packed:
        received = [swap(payloads[bit], "tp", bit + 1) for bit in (2, 1, 0)][::-1]
        parts = [rank_part, *received[::-1]]
        new = (kv_part, *received)
    else:
        parts = [lax.psum(rank_part, "tp")]
        kv_full = lax.all_gather(kv_part[:rows], "tp", axis=1, tiled=True)
        kv_start = here[1] * local_heads // PER_KV * HEAD_DIM
        new = (
            jnp.concatenate(
                [
                    lax.dynamic_slice_in_dim(kv_full, kv_start, width, 1),
                    lax.dynamic_slice_in_dim(kv_full, KVH * HEAD_DIM + kv_start, width, 1),
                ],
                axis=1,
            ),
        )

    cache = prompt_cache_pool
    if cols_dev < HEAD_DIM:
        share = HEAD_DIM // cols_dev
        groups = [list(range(g, g + share)) for g in range(0, tp_width, share)]
        cache = lax.all_gather(cache, "tp", axis=3, tiled=True, axis_index_groups=groups)
    ring = min(8, slots)

    def fetch(places, after, carried, start=None, shape=None):
        count = len(places)
        out = pl.pallas_call(
            functools.partial(fetch_kernel, places, slots, [start] * len(carried)),
            out_shape=(pltpu.VMEM((slots, width, section_tokens), BF16),) * count
            + (pltpu.VMEM((slots, section_tokens, width), BF16),) * count
            + tuple(pltpu.VMEM(shape or c.shape, c.dtype) for c in carried)
            + (pltpu.VMEM((8, 128), F32),),
            in_specs=[SMEM, SMEM, IN_HBM, ANYWHERE] + [IN_HBM] * len(carried),
            out_specs=(VMEM,) * (2 * count + len(carried) + 1),
            scratch_shapes=[
                pltpu.VMEM((ring, section_tokens, width), BF16),
                pltpu.SemaphoreType.DMA((ring,)),
                pltpu.SemaphoreType.DMA((count * slots,)),
                pltpu.SemaphoreType.DMA((1,)),
            ],
            compiler_params=params(12),
            cost_estimate=QUICK,
            name="fetch",
        )(here, owners, in_hbm(cache), after, *[in_hbm(c) for c in carried])
        return dict(zip(places, zip(out[:count], out[count : 2 * count]))), *out[2 * count :]

    caches, held_up, fetch_done = fetch((3, 2, 1), rank_part, (adapter_up,))

    masked = pl.pallas_call(
        functools.partial(query_kernel, steps, slots, len(parts)),
        out_shape=pltpu.VMEM((sections, rows, half_cols), BF16),
        in_specs=[SMEM, ANYWHERE] + [VMEM] * (len(parts) + 8),
        out_specs=VMEM,
        compiler_params=params(8),
        cost_estimate=QUICK,
        name="queries",
    )(here, fetch_done, *in_vmem(*parts, scale, pick, held_up, up_beside, cosine, sine, plain_near, plain_far))
    masked_across = swap(masked, "section", 2)
    quarter = model_width // tp_width
    depth = wo.shape[0]
    columns = [
        functools.partial(lambda bit, at: (at[1] ^ bit) * (quarter // 128), bit)
        for bit in range(tp_width)
    ]
    if packed:
        more, farthest_wo, fetch_done = fetch((0,), masked, (wo,), columns[-1], (depth, quarter))
    else:
        more, fetch_done = fetch((0,), masked, ())
    caches.update(more)

    query_own = pl.pallas_call(
        cross_add_kernel,
        out_shape=pltpu.VMEM(masked.shape, BF16),
        in_specs=[VMEM] * 2 + [ANYWHERE],
        out_specs=VMEM,
        compiler_params=params(8),
        cost_estimate=QUICK,
        name="sum_queries",
    )(*in_vmem(masked, masked_across), fetch_done)
    query_beside = swap(query_own, "section", 1)

    def attend_to(position, after, *new, **hold):
        operands = (query_own, query_beside, *caches[position], *new)
        return attend(position, steps, slots, kvl, here, limits, after, operands, **hold)

    part_beside_across = attend_to(3, query_beside)
    part_beside = attend_to(1, part_beside_across)
    part_across = attend_to(2, part_beside)
    across = merge(part_across, swap(part_beside_across, "section", 1))
    far = swap(across, "section", 2)
    hold = dict(right=wo, starts=columns[1:-1], cols=quarter) if packed else {}
    part_own = attend_to(0, across, *new, cosine, sine, **hold)
    if packed:
        part_own, *held_wo = part_own
    final = in_vmem(part_own, swap(part_beside, "section", 1), far)
    attended_shape = pltpu.VMEM((rows, local_heads * HEAD_DIM), BF16)
    wide_scratch = pltpu.VMEM((local_heads, rows, HEAD_DIM), F32)
    if packed:
        block = pltpu.VMEM((rows, quarter), BF16)
        attended, farthest = pl.pallas_call(
            functools.partial(finish_far_kernel, steps),
            out_shape=(attended_shape, block),
            in_specs=[VMEM] * 4,
            out_specs=(VMEM,) * 2,
            scratch_shapes=[wide_scratch],
            compiler_params=params(8),
            cost_estimate=QUICK,
            name="finish",
        )(*final, *in_vmem(farthest_wo))
        farthest = swap(farthest, "tp", tp_width - 1)
        held_wo = held_wo[::-1]
        sent = pl.pallas_call(
            far_kernel,
            out_shape=(block,) * len(held_wo),
            in_specs=[VMEM] * (1 + len(held_wo)),
            out_specs=(VMEM,) * len(held_wo),
            compiler_params=params(8),
            cost_estimate=QUICK,
            name="far_output",
        )(*in_vmem(attended, *held_wo))
        received = [swap(block, "tp", bit) for block, bit in zip(sent, range(tp_width - 2, 0, -1))]
        jobs = [(0, columns[0], quarter, depth // CUTS)]
        (total,) = product(
            "own_output", here, (attended,), (wo,), jobs, [F32], after=sent[:1]
        )
        total = add(add(total, farthest, dtype=F32), *received)
        blocks = [total] + [swap(total, "tp", bit) for bit in range(1, tp_width)]

        def place(bits, *earlier):
            return pl.pallas_call(
                functools.partial(place_kernel, [columns[bit] for bit in bits]),
                out_shape=jax.ShapeDtypeStruct((rows, model_width), BF16),
                in_specs=[SMEM] + [VMEM] * len(bits) + [IN_HBM] * len(earlier),
                out_specs=IN_HBM,
                scratch_shapes=[pltpu.SemaphoreType.DMA((len(bits),))],
                input_output_aliases={1 + len(bits): 0} if earlier else {},
                compiler_params=params(8),
                cost_estimate=QUICK,
                name="place",
            )(here, *in_vmem(*[blocks[bit] for bit in bits]), *earlier)

        result = place((2, 1), place((0, 3)))
    else:
        attended = pl.pallas_call(
            functools.partial(finish_kernel, steps),
            out_shape=attended_shape,
            in_specs=[VMEM] * 3,
            out_specs=VMEM,
            scratch_shapes=[wide_scratch],
            compiler_params=params(8),
            cost_estimate=QUICK,
            name="finish",
        )(*final)
        partial_out = jnp.dot(attended, wo, preferred_element_type=F32).astype(BF16)
        result = lax.psum(partial_out, "tp")
    return result.reshape(steps, slots, model_width)


def solution(mesh):
    return jax.shard_map(
        per_device,
        mesh=mesh,
        in_specs=(
            P(None, ("groups", "section"), None),
            P(),
            P(None, "tp"),
            P(None, "tp"),
            P("tp", None),
            P(("groups", "section"), "tp", None),
            P(("groups", "section"), None, "tp"),
            P("groups", None, "section", "tp"),
            P("groups"),
            P("groups"),
            P("groups"),
            P("groups"),
        ),
        out_specs=P(None, ("groups", "section"), None),
        check_vma=False,
    )
```

```python
import functools
import math

import jax
import jax.numpy as jnp
from jax import lax
from jax.experimental import pallas as pl
from jax.experimental.pallas import tpu as pltpu
from jax.sharding import PartitionSpec as P

QUERY_HEADS = 64
KVH = 8
HEAD_DIM = 128
PER_KV = QUERY_HEADS // KVH

EPSILON = 1e-05
ROPE_BASE = 500000.0
ADAPTER_ALPHA = 16.0
NEGATIVE = -1e30
STAT_ROWS = 8
FRESH_ROWS = 16
AHEAD = 6
CUTS = 4
F32 = jnp.float32
BF16 = jnp.bfloat16
VMEM = pl.BlockSpec(memory_space=pltpu.VMEM)
SMEM = pl.BlockSpec(memory_space=pltpu.SMEM)
IN_HBM = pl.BlockSpec(memory_space=pltpu.HBM)
ANYWHERE = pl.BlockSpec(memory_space=pl.ANY)
QUICK = pl.CostEstimate(flops=1, bytes_accessed=1, transcendentals=0)


def in_hbm(value):
    return pltpu.with_memory_space_constraint(value, pltpu.HBM)


def in_vmem(*values):
    return [pltpu.with_memory_space_constraint(value, pltpu.VMEM) for value in values]


def params(mebibytes):
    return pltpu.CompilerParams(vmem_limit_bytes=mebibytes * 1024 * 1024)


def swap(value, axis, bit):
    size = lax.axis_size(axis)
    pairs = [(i, i ^ bit) for i in range(size)]
    return jax.tree.map(lambda a: lax.ppermute(a, axis, pairs), value)


def tables(slots, section_tokens, adapters, here, prompt_slot, prompt_length, slot_adapter, ranks, frequency, *outs):
    owners, limits, pick, scale, cosine, sine = outs
    section = here[0]
    requests = owners.shape[0]
    shape = pick.shape
    row = lax.broadcasted_iota(jnp.int32, shape, 0)
    lane = lax.broadcasted_iota(jnp.int32, shape, 1)

    def place(slot):
        return (lax.div(slot, slots) ^ section) * slots + lax.rem(slot, slots)

    lengths = jnp.zeros(shape, jnp.int32)
    adapter = jnp.zeros(shape, jnp.int32)
    rank = jnp.zeros(shape, jnp.int32)
    for i in range(requests):
        at, length = place(prompt_slot[i]), prompt_length[i]
        owners[at] = i
        limits[at] = jnp.clip(length - section * section_tokens, 0, section_tokens)
        lengths = jnp.where(row == at, length, lengths)
        at, chosen = place(i), slot_adapter[i]
        adapter = jnp.where(row == at, chosen, adapter)
        rank = jnp.where(row == at, ranks[chosen], rank)
    held = jnp.where(lane < adapters, section * adapters + lane, (section ^ 1) * adapters + lane - adapters)
    pick[...] = jnp.where((lane < 2 * adapters) & (adapter == held), 1.0, 0.0)
    rank_f32 = rank.astype(F32)
    scale[...] = jnp.where(lane < rank, ADAPTER_ALPHA / rank_f32, 0.0)
    steps = cosine.shape[0] // requests
    positions = by_row(lengths, steps, slots).astype(F32)
    step = lax.rem(lax.div(lax.broadcasted_iota(jnp.int32, cosine.shape, 0), slots), steps)
    angles = (positions + step.astype(F32)) * frequency[...]
    cosine[...] = jnp.cos(angles)
    low = lax.broadcasted_iota(jnp.int32, cosine.shape, 1) < HEAD_DIM // 2
    sine[...] = jnp.where(low, -jnp.sin(angles), jnp.sin(angles))


def start_kernel(section_tokens, adapters, here, *refs):
    slot_arrays, frequency, refs = refs[:4], refs[4], refs[5:]
    states, gain, normed, piece, *outs, wide, gains, states_in, gain_in, sems = refs[:-4]
    slot_refs = refs[-4:]
    steps, slots, width = states.shape
    copies = [
        pltpu.make_async_copy(gain, gain_in, sems.at[0]),
        pltpu.make_async_copy(states, states_in, sems.at[1]),
    ]
    small = [
        pltpu.make_async_copy(source, target, sems.at[2 + i])
        for i, (source, target) in enumerate(zip(slot_arrays, slot_refs))
    ]
    for copy in small + copies:
        copy.start()
    for copy in small:
        copy.wait()
    tables(slots, section_tokens, adapters, here, *slot_refs, frequency, *outs)
    for copy in copies:
        copy.wait()
    gains[...] = gain_in[...].astype(F32)
    for t in range(steps):
        values = states_in[t].astype(F32)
        inverse = lax.rsqrt(jnp.mean(values * values, axis=-1, keepdims=True) + EPSILON)
        for c in range(width // 128):
            cols = slice(c * 128, (c + 1) * 128)
            wide[t * slots : (t + 1) * slots, cols] = values[:, cols] * inverse * gains[c : c + 1, :]
    normed[...] = wide[...].astype(BF16)
    cols = piece.shape[1]
    piece[...] = wide[:, pl.ds(pl.multiple_of(here[1] * cols, 128), cols)].astype(BF16)


class Stream:
    def __init__(self, here, rights, jobs, held, sems):
        self.items = [
            (j, i) for j, job in enumerate(jobs) for i in range(rights[job[0]].shape[0] // job[3])
        ]
        self.here, self.rights, self.jobs, self.held, self.sems = here, rights, jobs, held, sems
        for n in range(min(AHEAD, len(self.items))):
            self.copy(n).start()

    def copy(self, n):
        j, i = self.items[n]
        which, start, cols, chunk = self.jobs[j]
        first = pl.multiple_of(start(self.here) * 128, 128)
        source = self.rights[which].at[pl.ds(i * chunk, chunk), pl.ds(first, cols)]
        held = self.held[j]
        return pltpu.make_async_copy(source, held.at[i % held.shape[0]], self.sems.at[n])

    def multiply(self, left_rows, outs):
        for n, (j, i) in enumerate(self.items):
            chunk, held = self.jobs[j][3], self.held[j]
            self.copy(n).wait()
            part = jnp.dot(
                left_rows(i * chunk, chunk), held[i % held.shape[0]], preferred_element_type=F32
            )
            total = part if i == 0 else total + part
            if n + AHEAD < len(self.items):
                self.copy(n + AHEAD).start()
            if (i + 1) * chunk == self.rights[self.jobs[j][0]].shape[0]:
                outs[j][...] = total.astype(outs[j].dtype)


def stream_scratch(rights, jobs):
    counts = [rights[which].shape[0] // chunk for which, _, _, chunk in jobs]
    return [
        pltpu.VMEM((min(AHEAD, count), chunk, cols), BF16)
        for count, (_, _, cols, chunk) in zip(counts, jobs)
    ] + [pltpu.SemaphoreType.DMA((sum(counts),))]


def product_kernel(sizes, jobs, here, *refs):
    refs = list(refs)

    def take(count):
        taken = refs[:count]
        del refs[:count]
        return taken

    lefts, rights, sources, _ = [take(size) for size in sizes]
    outs, targets = take(len(jobs)), take(len(sources))
    held, (sems, carry_sems) = take(len(jobs)), refs
    stream = Stream(here, rights, jobs, held, sems)
    carries = [
        pltpu.make_async_copy(source, target, carry_sems.at[i])
        for i, (source, target) in enumerate(zip(sources, targets))
    ]
    for carry in carries:
        carry.start()
    stream.multiply(
        lambda first, count: jnp.concatenate([ref[:, first : first + count] for ref in lefts], axis=0), outs
    )
    for carry in carries:
        carry.wait()


def product(name, here, lefts, rights, jobs, types, carried=(), after=()):
    rows = sum(left.shape[0] for left in lefts)
    sizes = (len(lefts), len(rights), len(carried), len(after))
    return pl.pallas_call(
        functools.partial(product_kernel, sizes, jobs),
        out_shape=tuple(pltpu.VMEM((rows, job[2]), dtype) for job, dtype in zip(jobs, types))
        + tuple(pltpu.VMEM(c.shape, c.dtype) for c in carried),
        in_specs=[SMEM] + [VMEM] * len(lefts) + [IN_HBM] * (len(rights) + len(carried)) + [ANYWHERE] * len(after),
        out_specs=(VMEM,) * (len(types) + len(carried)),
        scratch_shapes=stream_scratch(rights, jobs) + [pltpu.SemaphoreType.DMA((max(1, len(carried)),))],
        compiler_params=params(20),
        cost_estimate=QUICK,
        name=name,
    )(here, *in_vmem(*lefts), *[in_hbm(c) for c in (*rights, *carried)], *after)


def cross_add_kernel(own, across, after, out):
    for p in range(own.shape[0]):
        out[p] = (own[p].astype(F32) + across[p ^ 2].astype(F32)).astype(out.dtype)


def add_kernel(*refs):
    *terms, out = refs
    total = terms[0][...].astype(F32)
    for term in terms[1:]:
        total = total + term[...].astype(F32)
    out[...] = total.astype(out.dtype)


def add(*terms, dtype=BF16):
    return pl.pallas_call(
        add_kernel,
        out_shape=pltpu.VMEM(terms[0].shape, dtype),
        in_specs=[VMEM] * len(terms),
        out_specs=VMEM,
        compiler_params=params(8),
        cost_estimate=QUICK,
        name="add",
    )(*in_vmem(*terms))


def by_row(table, steps, slots):
    blocks = [table[i : i + slots] for i in range(0, table.shape[0], slots)]
    return jnp.concatenate([block for block in blocks for _ in range(steps)], axis=0)


def down_kernel(steps, slots, here, own, beside, across, beside_across, pick, down, down_beside, kv, *outs):
    states = jnp.concatenate([ref[...] for ref in (own, beside, across, beside_across)], axis=0)
    picks = by_row(pick[...], steps, slots)
    adapters = down.shape[0]
    rows, rank = states.shape[0], down.shape[2]
    total = jnp.zeros((rows, rank), F32)
    for a in range(2 * adapters):
        part = jnp.dot(states, (down, down_beside)[a // adapters][a % adapters], preferred_element_type=F32)
        total = jnp.where(picks[:, a : a + 1] > 0, part, total)
    half = kv.shape[1] // 2
    new_rows = steps * slots
    for bit, out in enumerate(outs):
        out[:rows, :] = total
        if bit == 0:
            continue
        upper = here[1] == (0, 0, 1, 2)[bit]
        for k in range(half // HEAD_DIM):
            low = kv[:new_rows, k * HEAD_DIM : (k + 1) * HEAD_DIM]
            high = kv[:new_rows, half + k * HEAD_DIM : half + (k + 1) * HEAD_DIM]
            out[rows + k * new_rows : rows + (k + 1) * new_rows, :] = jnp.where(upper, high, low)


def query_kernel(steps, slots, count, here, after, *refs):
    parts, refs = refs[:count], refs[count:]
    scale, pick, up, up_beside, cosine, sine, plain_near, plain_far, out = refs
    all_rows = cosine.shape[0]
    rank_sum = parts[0][:all_rows, :]
    for part in parts[1:]:
        rank_sum = rank_sum + part[:all_rows, :]
    scales = by_row(scale[...], steps, slots)
    picks = by_row(pick[...], steps, slots)
    low_rank = jnp.where(scales > 0, rank_sum * scales, 0.0)
    adapters, rank, width = up.shape
    wide = jnp.concatenate(
        [jnp.where(picks[:, a : a + 1] > 0, low_rank, 0.0) for a in range(2 * adapters)], axis=1
    ).astype(BF16)
    depth = adapters * rank
    ups = [ref.reshape(depth, width) for ref in (up, up_beside)]
    half = plain_near.shape[1]
    rows = steps * slots
    shown = jnp.sum(picks, axis=1, keepdims=True) > 0
    first = (here[0] & 1) * half
    step = min(2 * HEAD_DIM, half)
    for c in range(0, half, step):
        block = pl.ds(pl.multiple_of(first + c, 128), step)
        changes = jnp.dot(wide[:, :depth], ups[0][:, block], preferred_element_type=F32)
        changes = changes + jnp.dot(wide[:, depth:], ups[1][:, block], preferred_element_type=F32)
        for h in range(0, step, HEAD_DIM):
            cols = slice(c + h, c + h + HEAD_DIM)
            plain = jnp.concatenate([plain_near[:, cols], plain_far[:, cols]], axis=0)
            query = plain + changes[:, h : h + HEAD_DIM]
            turned = query * cosine[...] + pltpu.roll(query, HEAD_DIM // 2, 1) * sine[...]
            turned = jnp.where(shown, turned, 0.0).astype(BF16)
            for position in range(4):
                out[position, :, cols] = turned[position * rows : (position + 1) * rows]


def fetch_kernel(places, slots, starts, here, owners, cache, after, *refs):
    sections = len(places)
    *refs, held, key_sems, value_sems, up_sem = refs
    carried = len(refs) // 2 - sections
    ups, outs, targets, done = refs[:carried], refs[carried:][: 2 * sections], refs[carried + 2 * sections : -1], refs[-1]
    ring = held.shape[0]
    count = sections * slots
    order = [(p, i) for p in range(sections) for i in range(slots)]

    def part(up, start, target):
        if start is None:
            return up
        return up.at[:, pl.ds(pl.multiple_of(start(here) * 128, 128), target.shape[1])]

    up_copies = [
        pltpu.make_async_copy(part(up, start, target), target, up_sem.at[0])
        for up, start, target in zip(ups, starts, targets)
    ]

    def key_copy(n):
        position, i = order[n]
        source = cache.at[owners[places[position] * slots + i], 0]
        return pltpu.make_async_copy(source, held.at[n % ring], key_sems.at[n % ring])

    def value_copy(n):
        position, i = order[n]
        source = cache.at[owners[places[position] * slots + i], 1]
        return pltpu.make_async_copy(source, outs[sections + position].at[i], value_sems.at[n])

    for n in range(ring):
        key_copy(n).start()
        value_copy(n).start()
    for copy in up_copies:
        copy.start()
    for n in range(count):
        position, i = order[n]
        key_copy(n).wait()
        outs[position][i] = held[n % ring].T
        if n + ring < count:
            key_copy(n + ring).start()
            value_copy(n + ring).start()
    done[...] = jnp.zeros_like(done)
    for copy in up_copies:
        copy.wait()
    for n in range(count):
        value_copy(n).wait()


def attend_and_hold_kernel(starts, operands, attend_body, here, limits, after, right, *refs):
    inputs, (out, *refs) = refs[:operands], refs[operands:]
    held, (*scratch, sems) = refs[: len(starts)], refs[len(starts) :]
    copies = []
    for i, (start, target) in enumerate(zip(starts, held)):
        first = pl.multiple_of(start(here) * 128, 128)
        source = right.at[:, pl.ds(first, target.shape[1])]
        copies.append(pltpu.make_async_copy(source, target, sems.at[i]))
    for copy in copies:
        copy.start()
    attend_body(here, limits, after, *inputs, out, *scratch)
    for copy in copies:
        copy.wait()


def place_kernel(starts, here, *refs):
    blocks, (out, sems) = refs[: len(starts)], refs[-2:]
    copies = []
    for i, (start, block) in enumerate(zip(starts, blocks)):
        first = pl.multiple_of(start(here) * 128, 128)
        copies.append(pltpu.make_async_copy(block, out.at[:, pl.ds(first, block.shape[1])], sems.at[i]))
    for copy in copies:
        copy.start()
    for copy in copies:
        copy.wait()


def attend_kernel(position, steps, slots, kvl, here, limits, after, own, other, keys, values, *refs):
    fresh = position == 0
    if fresh:
        kv, *received, cosine, sine, out, qf, qs, turned, nk, nv = refs
    else:
        out, qf, qs = refs
    half = own.shape[2] // HEAD_DIM
    heads = 2 * half
    per_kv = heads // kvl
    rows = heads * steps
    tokens = values.shape[1]
    root = 1.0 / math.sqrt(HEAD_DIM)
    qs[...] = jnp.zeros_like(qs)
    lower = here[0] & 1 == 0
    for h in range(half):
        cols = slice(h * HEAD_DIM, (h + 1) * HEAD_DIM)
        mine = own[position, :, cols].astype(F32)
        theirs = other[position ^ 1, :, cols].astype(F32)
        qf[h] = jnp.where(lower, mine, theirs)
        qf[half + h] = jnp.where(lower, theirs, mine)
    for i in range(slots):
        for h in range(heads):
            k = h // per_kv
            qs[i, h * steps : (h + 1) * steps, k * HEAD_DIM : (k + 1) * HEAD_DIM] = qf[
                h, pl.ds(i, steps, stride=slots), :
            ]
    if fresh:
        step_of_row = lax.broadcasted_iota(jnp.int32, (rows, FRESH_ROWS), 0) % steps
        fresh_valid = lax.broadcasted_iota(jnp.int32, (rows, FRESH_ROWS), 1) <= step_of_row
        rows_here = steps * slots
        nk[...] = jnp.zeros_like(nk)
        nv[...] = jnp.zeros_like(nv)
        for k in range(kvl):
            cols = slice(k * HEAD_DIM, (k + 1) * HEAD_DIM)
            if received:
                tp, half_kv = here[1], kvl * HEAD_DIM
                first = cosine.shape[0] + k * rows_here
                one, two, three = [ref[first : first + rows_here, :] for ref in received]
                low, high = kv[:rows_here, cols], kv[:rows_here, half_kv + k * HEAD_DIM : half_kv + (k + 1) * HEAD_DIM]
                key = jnp.where(tp == 0, low, jnp.where(tp == 1, one, jnp.where(tp == 2, three, two)))
                value = jnp.where(tp == 0, two, jnp.where(tp == 1, three, jnp.where(tp == 2, one, high)))
            else:
                key, value = kv[:, cols], kv[:, (kvl + k) * HEAD_DIM : (kvl + k + 1) * HEAD_DIM]
            turned[0, k] = key * cosine[:rows_here, :] + pltpu.roll(key, HEAD_DIM // 2, 1) * sine[:rows_here, :]
            turned[1, k] = value
            for i in range(slots):
                nk[i, :steps, cols] = turned[0, k, pl.ds(i, steps, stride=slots), :]
                nv[i, :steps, cols] = turned[1, k, pl.ds(i, steps, stride=slots), :]
    eye = diagonal(rows)
    token = lax.broadcasted_iota(jnp.int32, (rows, tokens), 1)
    for i in range(slots):
        limit = limits[position * slots + i]
        queries = qs[i].astype(BF16)
        scores = jnp.dot(queries, keys[i], preferred_element_type=F32) * root
        valid = token < limit
        scores = jnp.where(valid, scores, NEGATIVE)
        top = jnp.max(scores, axis=1, keepdims=True)
        if fresh:
            new_scores = lax.dot_general(
                queries, nk[i].astype(BF16), (((1,), (1,)), ((), ())), preferred_element_type=F32
            )
            new_scores = jnp.where(fresh_valid, new_scores * root, NEGATIVE)
            top = jnp.maximum(top, jnp.max(new_scores, axis=1, keepdims=True))
        weights = jnp.where(valid, jnp.exp(scores - top), 0.0)
        total = jnp.sum(weights, axis=1, keepdims=True)
        value = jnp.dot(weights.astype(BF16), values[i], preferred_element_type=F32)
        if fresh:
            new_weights = jnp.where(fresh_valid, jnp.exp(new_scores - top), 0.0)
            total = total + jnp.sum(new_weights, axis=1, keepdims=True)
            value = value + jnp.dot(
                new_weights.astype(BF16), nv[i].astype(BF16), preferred_element_type=F32
            )
        for k in range(kvl):
            block = slice(k * per_kv * steps, (k + 1) * per_kv * steps)
            out[i, block, :] = value[block, k * HEAD_DIM : (k + 1) * HEAD_DIM]
        out[i, rows : rows + 1, :rows] = jnp.sum(jnp.where(eye, top, 0.0), axis=0, keepdims=True)
        out[i, rows + 1 : rows + 2, :rows] = jnp.sum(jnp.where(eye, total, 0.0), axis=0, keepdims=True)


def joined(refs, i, rows, eye):
    tops = [ref[i, rows : rows + 1, :rows] for ref in refs]
    top = functools.reduce(jnp.maximum, tops)
    total, weighted = 0.0, 0.0
    for ref, part_top in zip(refs, tops):
        scale = jnp.exp(part_top - top)
        total = total + ref[i, rows + 1 : rows + 2, :rows] * scale
        column = jnp.sum(jnp.where(eye, scale, 0.0), axis=1, keepdims=True)
        weighted = weighted + ref[i, :rows, :] * column
    return weighted, top, total


def diagonal(rows):
    return lax.broadcasted_iota(jnp.int32, (rows, rows), 0) == lax.broadcasted_iota(
        jnp.int32, (rows, rows), 1
    )


def merge_kernel(a, b, out):
    rows = a.shape[1] - STAT_ROWS
    eye = diagonal(rows)
    for i in range(a.shape[0]):
        weighted, top, total = joined((a, b), i, rows, eye)
        out[i, :rows, :] = weighted
        out[i, rows : rows + 1, :rows] = top
        out[i, rows + 1 : rows + 2, :rows] = total


def finish_kernel(steps, a, b, c, out, wide):
    rows = a.shape[1] - STAT_ROWS
    slots = a.shape[0]
    eye = diagonal(rows)
    for i in range(slots):
        weighted, _, total = joined((a, b, c), i, rows, eye)
        weighted = weighted / jnp.sum(jnp.where(eye, total, 0.0), axis=1, keepdims=True)
        for h in range(rows // steps):
            wide[h, pl.ds(i, steps, stride=slots), :] = weighted[h * steps : (h + 1) * steps, :]
    for h in range(rows // steps):
        out[:, h * HEAD_DIM : (h + 1) * HEAD_DIM] = wide[h].astype(BF16)


def far_kernel(left, *refs):
    half = len(refs) // 2
    for right, out in zip(refs[:half], refs[half:]):
        out[...] = jnp.dot(left[...], right[...], preferred_element_type=F32).astype(out.dtype)


def finish_far_kernel(steps, a, b, c, held_right, attended, held_out, wide):
    finish_kernel(steps, a, b, c, attended, wide)
    held_out[...] = jnp.dot(attended[...], held_right[...], preferred_element_type=F32).astype(BF16)


def attend(position, steps, slots, kvl, here, limits, after, operands, right=None, starts=(), cols=0):
    heads = 2 * operands[0].shape[2] // HEAD_DIM
    rows, columns = heads * steps, operands[3].shape[2]
    scratch = [
        pltpu.VMEM((heads, steps * slots, HEAD_DIM), F32),
        pltpu.VMEM((slots, rows, columns), F32),
    ]
    if position == 0:
        scratch += [
            pltpu.VMEM((2, kvl, steps * slots, HEAD_DIM), F32),
            pltpu.VMEM((slots, FRESH_ROWS, columns), F32),
            pltpu.VMEM((slots, FRESH_ROWS, columns), F32),
        ]
    body = functools.partial(attend_kernel, position, steps, slots, kvl)
    out = pltpu.VMEM((slots, rows + STAT_ROWS, HEAD_DIM), F32)
    if not starts:
        return pl.pallas_call(
            body,
            out_shape=out,
            in_specs=[SMEM] * 2 + [ANYWHERE] + [VMEM] * len(operands),
            out_specs=VMEM,
            scratch_shapes=scratch,
            compiler_params=params(8),
            cost_estimate=QUICK,
            name="attend",
        )(here, limits, after, *in_vmem(*operands))
    block = pltpu.VMEM((right.shape[0], cols), right.dtype)
    return pl.pallas_call(
        functools.partial(attend_and_hold_kernel, starts, len(operands), body),
        out_shape=(out,) + (block,) * len(starts),
        in_specs=[SMEM] * 2 + [ANYWHERE, IN_HBM] + [VMEM] * len(operands),
        out_specs=(VMEM,) * (1 + len(starts)),
        scratch_shapes=scratch + [pltpu.SemaphoreType.DMA((len(starts),))],
        compiler_params=params(8),
        cost_estimate=QUICK,
        name="attend_hold",
    )(here, limits, after, in_hbm(right), *in_vmem(*operands))


def merge(a, b):
    return pl.pallas_call(
        merge_kernel,
        out_shape=pltpu.VMEM(a.shape, F32),
        in_specs=[VMEM] * 2,
        out_specs=VMEM,
        compiler_params=params(8),
        cost_estimate=QUICK,
        name="merge",
    )(*in_vmem(a, b))


def per_device(
    step_token_states,
    input_norm_gain,
    wq,
    wkv,
    wo,
    adapter_down,
    adapter_up,
    prompt_cache_pool,
    prompt_slot,
    prompt_cache_length,
    slot_adapter,
    adapter_ranks,
):
    sections = lax.axis_size("section")
    tp_width = lax.axis_size("tp")
    here = jnp.stack([lax.axis_index("section"), lax.axis_index("tp")]).astype(jnp.int32)
    steps, slots, model_width = step_token_states.shape
    requests = prompt_slot.shape[0]
    section_tokens = prompt_cache_pool.shape[2]
    cols_dev = prompt_cache_pool.shape[3]
    adapters, slice_cols, rank = adapter_down.shape
    local_heads = QUERY_HEADS // tp_width
    half_cols = local_heads // 2 * HEAD_DIM
    kvl = max(1, local_heads // PER_KV)
    width = kvl * HEAD_DIM
    rows = steps * slots
    assert sections == 4

    exponents = jnp.arange(HEAD_DIM // 2, dtype=F32) * (2.0 / HEAD_DIM)
    frequency = ROPE_BASE ** (-exponents)
    frequency = jnp.concatenate([frequency, frequency])[None]
    ints = jax.ShapeDtypeStruct((requests,), jnp.int32)
    normed, piece, owners, limits, pick, scale, cosine, sine = pl.pallas_call(
        functools.partial(start_kernel, section_tokens, adapters),
        out_shape=(pltpu.VMEM((rows, model_width), BF16), pltpu.VMEM((rows, slice_cols), BF16), ints, ints)
        + (pltpu.VMEM((requests, rank), F32),) * 2
        + (pltpu.VMEM((sections * rows, HEAD_DIM), F32),) * 2,
        in_specs=[SMEM] + [IN_HBM] * 4 + [VMEM] + [IN_HBM] * 2,
        out_specs=(VMEM, VMEM, SMEM, SMEM) + (VMEM,) * 4,
        scratch_shapes=[
            pltpu.VMEM((rows, model_width), F32),
            pltpu.VMEM((model_width // 128, 128), F32),
            pltpu.VMEM(step_token_states.shape, BF16),
            pltpu.VMEM((model_width // 128, 128), BF16),
            pltpu.SemaphoreType.DMA((6,)),
            *[
                pltpu.SMEM(array.shape, jnp.int32)
                for array in (prompt_slot, prompt_cache_length, slot_adapter, adapter_ranks)
            ],
        ],
        compiler_params=params(8),
        cost_estimate=QUICK,
        name="start",
    )(
        here,
        *[in_hbm(array) for array in (prompt_slot, prompt_cache_length, slot_adapter, adapter_ranks)],
        frequency,
        in_hbm(step_token_states), in_hbm(input_norm_gain.reshape(model_width // 128, 128)),
    )
    normed_beside = swap(normed, "section", 1)
    piece_across = swap(piece, "section", 2)
    piece_beside = swap(piece, "section", 1)
    late_down, late_up, _ = lax.optimization_barrier((adapter_down, adapter_up, normed_beside))
    down_beside = swap(late_down, "section", 1)
    up_beside = swap(late_up, "section", 1)

    packed = tp_width == 4
    chunk = min(512, model_width // 2)
    jobs = [(0, lambda at: (at[0] & 1) * (half_cols // 128), half_cols, chunk)]
    if packed:
        jobs += [(1, lambda at: 0, wkv.shape[1], 2 * chunk)]
    plain_near, *kv_part = product(
        "query", here, (normed, normed_beside), (wq, wkv), jobs, [F32] * len(jobs)
    )
    kv_part = kv_part[0] if packed else jnp.dot(normed, wkv, preferred_element_type=F32)
    plain_far = swap(plain_near, "section", 2)
    late_across = lax.optimization_barrier((piece_across, plain_near))[0]
    piece_beside_across = swap(late_across, "section", 1)
    payload = pltpu.VMEM((sections * rows + kvl * rows, rank), F32)
    own_part = pltpu.VMEM((sections * rows, rank), F32)
    rank_part, *payloads = pl.pallas_call(
        functools.partial(down_kernel, steps, slots),
        out_shape=(own_part,) + ((payload,) * 3 if packed else ()),
        in_specs=[SMEM] + [VMEM] * 8,
        out_specs=(VMEM,) * (4 if packed else 1),
        compiler_params=params(8),
        cost_estimate=QUICK,
        name="down",
    )(
        here,
        *in_vmem(
            piece, piece_beside, piece_across, piece_beside_across, pick, adapter_down, down_beside, kv_part
        ),
    )
    if packed:
        received = [swap(payloads[bit], "tp", bit + 1) for bit in (2, 1, 0)][::-1]
        parts = [rank_part, *received[::-1]]
        new = (kv_part, *received)
    else:
        parts = [lax.psum(rank_part, "tp")]
        kv_full = lax.all_gather(kv_part[:rows], "tp", axis=1, tiled=True)
        kv_start = here[1] * local_heads // PER_KV * HEAD_DIM
        new = (
            jnp.concatenate(
                [
                    lax.dynamic_slice_in_dim(kv_full, kv_start, width, 1),
                    lax.dynamic_slice_in_dim(kv_full, KVH * HEAD_DIM + kv_start, width, 1),
                ],
                axis=1,
            ),
        )

    cache = prompt_cache_pool
    if cols_dev < HEAD_DIM:
        share = HEAD_DIM // cols_dev
        groups = [list(range(g, g + share)) for g in range(0, tp_width, share)]
        cache = lax.all_gather(cache, "tp", axis=3, tiled=True, axis_index_groups=groups)
    ring = min(8, slots)

    def fetch(places, after, carried, start=None, shape=None):
        count = len(places)
        out = pl.pallas_call(
            functools.partial(fetch_kernel, places, slots, [start] * len(carried)),
            out_shape=(pltpu.VMEM((slots, width, section_tokens), BF16),) * count
            + (pltpu.VMEM((slots, section_tokens, width), BF16),) * count
            + tuple(pltpu.VMEM(shape or c.shape, c.dtype) for c in carried)
            + (pltpu.VMEM((8, 128), F32),),
            in_specs=[SMEM, SMEM, IN_HBM, ANYWHERE] + [IN_HBM] * len(carried),
            out_specs=(VMEM,) * (2 * count + len(carried) + 1),
            scratch_shapes=[
                pltpu.VMEM((ring, section_tokens, width), BF16),
                pltpu.SemaphoreType.DMA((ring,)),
                pltpu.SemaphoreType.DMA((count * slots,)),
                pltpu.SemaphoreType.DMA((1,)),
            ],
            compiler_params=params(12),
            cost_estimate=QUICK,
            name="fetch",
        )(here, owners, in_hbm(cache), after, *[in_hbm(c) for c in carried])
        return dict(zip(places, zip(out[:count], out[count : 2 * count]))), *out[2 * count :]

    caches, held_up, fetch_done = fetch((3, 2, 1), rank_part, (adapter_up,))

    masked = pl.pallas_call(
        functools.partial(query_kernel, steps, slots, len(parts)),
        out_shape=pltpu.VMEM((sections, rows, half_cols), BF16),
        in_specs=[SMEM, ANYWHERE] + [VMEM] * (len(parts) + 8),
        out_specs=VMEM,
        compiler_params=params(8),
        cost_estimate=QUICK,
        name="queries",
    )(here, fetch_done, *in_vmem(*parts, scale, pick, held_up, up_beside, cosine, sine, plain_near, plain_far))
    masked_across = swap(masked, "section", 2)
    quarter = model_width // tp_width
    depth = wo.shape[0]
    columns = [
        functools.partial(lambda bit, at: (at[1] ^ bit) * (quarter // 128), bit)
        for bit in range(tp_width)
    ]
    if packed:
        more, farthest_wo, fetch_done = fetch((0,), masked, (wo,), columns[2], (depth, quarter))
    else:
        more, fetch_done = fetch((0,), masked, ())
    caches.update(more)

    query_own = pl.pallas_call(
        cross_add_kernel,
        out_shape=pltpu.VMEM(masked.shape, BF16),
        in_specs=[VMEM] * 2 + [ANYWHERE],
        out_specs=VMEM,
        compiler_params=params(8),
        cost_estimate=QUICK,
        name="sum_queries",
    )(*in_vmem(masked, masked_across), fetch_done)
    query_beside = swap(query_own, "section", 1)

    def attend_to(position, after, *new, **hold):
        operands = (query_own, query_beside, *caches[position], *new)
        return attend(position, steps, slots, kvl, here, limits, after, operands, **hold)

    part_beside_across = attend_to(3, query_beside)
    part_beside = attend_to(1, part_beside_across)
    part_across = attend_to(2, part_beside)
    across = merge(part_across, swap(part_beside_across, "section", 1))
    far = swap(across, "section", 2)
    hold = dict(right=wo, starts=columns[1::2], cols=quarter) if packed else {}
    part_own = attend_to(0, across, *new, cosine, sine, **hold)
    if packed:
        part_own, *held_wo = part_own
    final = in_vmem(part_own, swap(part_beside, "section", 1), far)
    attended_shape = pltpu.VMEM((rows, local_heads * HEAD_DIM), BF16)
    wide_scratch = pltpu.VMEM((local_heads, rows, HEAD_DIM), F32)
    if packed:
        block = pltpu.VMEM((rows, quarter), BF16)
        attended, farthest = pl.pallas_call(
            functools.partial(finish_far_kernel, steps),
            out_shape=(attended_shape, block),
            in_specs=[VMEM] * 4,
            out_specs=(VMEM,) * 2,
            scratch_shapes=[wide_scratch],
            compiler_params=params(8),
            cost_estimate=QUICK,
            name="finish",
        )(*final, *in_vmem(farthest_wo))
        farthest = swap(farthest, "tp", 2)
        held_wo = held_wo[::-1]
        sent = pl.pallas_call(
            far_kernel,
            out_shape=(block,) * len(held_wo),
            in_specs=[VMEM] * (1 + len(held_wo)),
            out_specs=(VMEM,) * len(held_wo),
            compiler_params=params(8),
            cost_estimate=QUICK,
            name="far_output",
        )(*in_vmem(attended, *held_wo))
        received = [swap(block, "tp", bit) for block, bit in zip(sent, (3, 1))]
        jobs = [(0, columns[0], quarter, depth // CUTS)]
        (total,) = product(
            "own_output", here, (attended,), (wo,), jobs, [F32], after=sent[:1]
        )
        total = add(add(total, farthest, dtype=F32), *received)
        blocks = [total] + [swap(total, "tp", bit) for bit in range(1, tp_width)]

        def place(bits, *earlier):
            return pl.pallas_call(
                functools.partial(place_kernel, [columns[bit] for bit in bits]),
                out_shape=jax.ShapeDtypeStruct((rows, model_width), BF16),
                in_specs=[SMEM] + [VMEM] * len(bits) + [IN_HBM] * len(earlier),
                out_specs=IN_HBM,
                scratch_shapes=[pltpu.SemaphoreType.DMA((len(bits),))],
                input_output_aliases={1 + len(bits): 0} if earlier else {},
                compiler_params=params(8),
                cost_estimate=QUICK,
                name="place",
            )(here, *in_vmem(*[blocks[bit] for bit in bits]), *earlier)

        result = place((2, 1), place((0, 3)))
    else:
        attended = pl.pallas_call(
            functools.partial(finish_kernel, steps),
            out_shape=attended_shape,
            in_specs=[VMEM] * 3,
            out_specs=VMEM,
            scratch_shapes=[wide_scratch],
            compiler_params=params(8),
            cost_estimate=QUICK,
            name="finish",
        )(*final)
        partial_out = jnp.dot(attended, wo, preferred_element_type=F32).astype(BF16)
        result = lax.psum(partial_out, "tp")
    return result.reshape(steps, slots, model_width)


def solution(mesh):
    return jax.shard_map(
        per_device,
        mesh=mesh,
        in_specs=(
            P(None, ("groups", "section"), None),
            P(),
            P(None, "tp"),
            P(None, "tp"),
            P("tp", None),
            P(("groups", "section"), "tp", None),
            P(("groups", "section"), None, "tp"),
            P("groups", None, "section", "tp"),
            P("groups"),
            P("groups"),
            P("groups"),
            P("groups"),
        ),
        out_specs=P(None, ("groups", "section"), None),
        check_vma=False,
    )
```
